32 devices in a mesh: expert: 16 (over z, x, core), tensor: 2 (over y).
Axes of the slice: x: 2, y: 2, z: 4, core: 2. Of those that a mesh axis runs over, the one named last changes fastest.
Arguments:
- tokens: bfloat16 [4096, 1024], P(('expert', 'tensor')), may hold values from -6 to 6
- gain_attn: float32 [1024], replicated, may hold values from 0.5 to 1.5
- w_query: bfloat16 [1024, 1024], P(None, 'tensor'), may hold values from -0.1875 to 0.1875
- w_key: bfloat16 [1024, 512], P(None, 'tensor'), may hold values from -0.1875 to 0.1875
- w_value: bfloat16 [1024, 512], P(None, 'tensor'), may hold values from -0.1875 to 0.1875
- w_out: bfloat16 [1024, 1024], P('tensor'), may hold values from -1.5 to 1.5
- gain_moe: float32 [1024], replicated, may hold values from 0.5 to 1.5
- router: bfloat16 [1024, 16], replicated, may hold values from -0.09375 to 0.09375
- expert_gate: bfloat16 [16, 1024, 512], P('expert', None, 'tensor'), may hold values from -0.1875 to 0.1875
- expert_up: bfloat16 [16, 1024, 512], P('expert', None, 'tensor'), may hold values from -0.1875 to 0.1875
- expert_down: bfloat16 [16, 512, 1024], P('expert', 'tensor'), may hold values from -0.75 to 0.75
- routes: int32 [4096, 8], P(('expert', 'tensor')), may hold values from 0 to 15, all different within a row
- fill_order: int32 [32, 128], P(('expert', 'tensor')), may hold values from 0 to 127, each once within a row
- cotangent: bfloat16 [4096, 1024], P(('expert', 'tensor')), may hold values from -6 to 6
Outputs:
- output: bfloat16 [4096, 1024], P(('expert', 'tensor'))
- grad_tokens: float32 [4096, 1024], P(('expert', 'tensor'))
- grad_gain_attn: float32 [1024], replicated
- grad_w_query: float32 [1024, 1024], P(None, 'tensor')
- grad_w_key: float32 [1024, 512], P(None, 'tensor')
- grad_w_value: float32 [1024, 512], P(None, 'tensor')
- grad_w_out: float32 [1024, 1024], P('tensor')
- grad_gain_moe: float32 [1024], replicated
- grad_router: float32 [1024, 16], replicated
- grad_expert_gate: float32 [16, 1024, 512], P('expert', None, 'tensor')
- grad_expert_up: float32 [16, 1024, 512], P('expert', None, 'tensor')
- grad_expert_down: float32 [16, 512, 1024], P('expert', 'tensor')
The draws below stay inside these ranges and needn't reach their ends.
Inputs may be any that keep to these rules, and one draw needn't show every extreme that they name: `routes`: each row names 8 different experts; every expert is named by some row. `fill_order`: each row holds every number below 128 once.
All inputs are finite; a program needn't handle non-finite values.
Results may differ from the reference program's by a relative error of at most 0.015.
Values may be sent and summed in bfloat16 or wider, within the bound.
A program may use at most 256 MiB of HBM per device.

```python
import math
import jax
import jax.numpy as jnp
from jax import lax

D = 1024
HEADS = 16
KV_HEADS = 8
HEAD_DIM = 64
FF = 512
TOP = 8
TOK_LOC = 128
EXPERTS = 16
TOK_DEV = 256
TOKENS = 4096
SOURCES = 32
CAP = 80
N_EXPERT = 16
N_TENSOR = 2


def levels(stream_key, shape, cuts, least, largest):
    def one(dim, parts):
        draws = jax.random.uniform(jax.random.fold_in(jax.random.fold_in(stream_key, 6), dim), (parts,), jnp.float32, least / len(cuts), largest / len(cuts))
        return jnp.repeat(jnp.exp(draws), shape[dim] // parts).reshape((-1,) + (1,) * (len(shape) - dim - 1))

    loudness = one(*cuts[0])
    for cut in cuts[1:]:
        loudness = loudness * one(*cut)
    return loudness


def distinct(rng, rows, count, top, lift):
    sequence = jax.random.permutation(jax.random.fold_in(rng, 1), count)
    boost = sequence
    for power in range(3):
        boost = boost * boost // count
    boost = boost * lift // count
    lots = jax.random.randint(jax.random.fold_in(rng, 2), (rows, count), 0, 4096) + boost
    fixed_rows = jax.random.permutation(jax.random.fold_in(rng, 3), rows)[jnp.arange(count) % rows]
    lots = jnp.where(jnp.arange(rows)[:, None] == fixed_rows[None, :], 1 << 14, lots)
    merit = lots * count + jnp.arange(count)
    return lax.top_k(merit.astype(jnp.int32), top)[1].astype(jnp.int32)


def centred(own_key, extent, scale, bound, shards=(), kind=jnp.bfloat16):
    values = scale * jax.random.normal(own_key, extent, jnp.float32)
    if shards:
        values = values * levels(own_key, extent, shards, -0.22, 0.18)
    return jnp.clip(values, -bound, bound).astype(kind)


def setup_inputs(seed: int = 0) -> dict:
    seeds = jax.random.split(jax.random.key(seed), 15)
    return {
        "tokens": centred(seeds[0], (TOKENS, D), 1.0, 6.0, ((0, 32),)),
        "gain_attn": jnp.clip(1.0 + 0.1 * jax.random.normal(seeds[1], (D,), jnp.float32), 0.5, 1.5),
        "w_query": centred(seeds[2], (D, HEADS * HEAD_DIM), D ** -0.5, 0.1875, ((1, 2),)),
        "w_key": centred(seeds[3], (D, KV_HEADS * HEAD_DIM), D ** -0.5, 0.1875, ((1, 2),)),
        "w_value": centred(seeds[4], (D, KV_HEADS * HEAD_DIM), D ** -0.5, 0.1875, ((1, 2),)),
        "w_out": centred(seeds[5], (HEADS * HEAD_DIM, D), (max(4 * D // TOK_DEV, 1)) ** -0.5, 1.5, ((0, 2),)),
        "gain_moe": jnp.clip(1.0 + 0.1 * jax.random.normal(seeds[6], (D,), jnp.float32), 0.5, 1.5),
        "router": centred(seeds[7], (D, EXPERTS), (0.5 * D ** -0.5), 0.09375),
        "expert_gate": centred(seeds[8], (EXPERTS, D, FF), D ** -0.5, 0.1875, ((0, 16), (2, 2))),
        "expert_up": centred(seeds[9], (EXPERTS, D, FF), D ** -0.5, 0.1875, ((0, 16), (2, 2))),
        "expert_down": centred(seeds[10], (EXPERTS, FF, D), (FF // 8) ** -0.5, 0.75, ((0, 16), (1, 2))),
        "routes": distinct(seeds[11], TOKENS, EXPERTS, TOP, 4096),
        "fill_order": jax.vmap(lambda own: jax.random.permutation(own, TOK_LOC))(jax.random.split(seeds[12], SOURCES)).reshape((SOURCES, TOK_LOC)).astype(jnp.int32),
        "cotangent": centred(seeds[13], (TOKENS, D), 1.0, 6.0, ((0, 32),)),
    }


EPSILON = 1e-06
THETA_BASE = 10000.0
MASKED = -1e+30
HIGHEST = lax.Precision.HIGHEST

@jax.custom_vjp
def low(v):
    return lax.optimization_barrier(v.astype(jnp.bfloat16)).astype(jnp.float32)

@jax.custom_vjp
def low_back(v):
    return v

def low_keep(v):
    return (low(v), None)

def low_pass(kept, grad):
    return (grad,)

def back_keep(v):
    return (v, None)

def back_low(kept, grad):
    return (low(grad),)
low.defvjp(low_keep, low_pass)
low_back.defvjp(back_keep, back_low)

def matmul(left, right):
    return jnp.dot(left, right, precision=HIGHEST, preferred_element_type=jnp.float32)

def angles_of(row_count, head_size):
    half = head_size // 2
    freqs = jnp.exp(jnp.arange(half, dtype=jnp.float32) * (-2.0 * math.log(THETA_BASE) / head_size))
    return jnp.arange(row_count, dtype=jnp.float32)[:, None] * freqs[None, :]

def rotate(vectors, angles, sign):
    half = vectors.shape[-1] // 2
    cosine = jnp.cos(angles)[:, None, :]
    sine = sign * jnp.sin(angles)[:, None, :]
    first = vectors[..., :half]
    second = vectors[..., half:]
    return jnp.concatenate([first * cosine - second * sine, second * cosine + first * sine], -1)

def norm_rows(vectors, gain):
    return vectors * lax.rsqrt(lax.optimization_barrier(jnp.mean(vectors * vectors, -1, keepdims=True)) + EPSILON) * gain

def slot_index(route_block, order_block):
    expert_ids = jnp.arange(EXPERTS, dtype=jnp.int32)
    pick_table = (route_block[:, :, None] == expert_ids[None, None, :]).astype(jnp.int32)
    counts = lax.optimization_barrier(jnp.sum(pick_table, 1)).astype(jnp.int32)
    ordered = counts[order_block]
    before = (jnp.cumsum(ordered, 0) - ordered).astype(jnp.int32)
    rank_table = jnp.zeros_like(counts).at[order_block].set(before)
    slot_pos = jnp.take_along_axis(rank_table, route_block, 1)
    return jnp.where(slot_pos < CAP, route_block * CAP + slot_pos, EXPERTS * CAP).astype(jnp.int32)

def attend(queries, key_rows, value_rows):
    q_size = min(512, TOK_DEV)
    blocks = TOK_DEV // q_size
    q_group = HEADS // KV_HEADS
    score_scale = HEAD_DIM ** (-0.5)
    key_pos = jnp.arange(TOK_DEV)

    def one_block(block_args):
        q_block, row_start = block_args
        grouped = q_block.reshape(q_size, KV_HEADS, q_group, HEAD_DIM)
        raw_scores = low_back(jnp.einsum('qkgd,tkd->kgqt', grouped, key_rows, precision=HIGHEST))
        allowed = (row_start + jnp.arange(q_size))[:, None] >= key_pos[None, :]
        scores = jnp.where(allowed, raw_scores * score_scale, MASKED)
        attn_probs = low(jax.nn.softmax(scores, -1))
        mixed_rows = jnp.einsum('kgqt,tkd->qkgd', attn_probs, value_rows, precision=HIGHEST)
        return mixed_rows.reshape(q_size, HEADS * HEAD_DIM)
    stacked = lax.map(jax.checkpoint(one_block), (queries.reshape(blocks, q_size, HEADS, HEAD_DIM), jnp.arange(blocks) * q_size))
    return stacked.reshape(TOK_DEV, HEADS * HEAD_DIM)

def layer(inputs, gain_attn, w_query, w_key, w_value, w_out, gain_moe, router, expert_gate, expert_up, expert_down, route_seq, order_seq):
    normed = low(norm_rows(inputs, gain_attn))
    angles = angles_of(TOK_DEV, HEAD_DIM)
    queries = low(rotate(low_back(matmul(normed, w_query)).reshape(TOK_DEV, HEADS, HEAD_DIM), angles, 1.0))
    key_rows = low(rotate(low_back(matmul(normed, w_key)).reshape(TOK_DEV, KV_HEADS, HEAD_DIM), angles, 1.0))
    value_rows = low(low_back(matmul(normed, w_value))).reshape(TOK_DEV, KV_HEADS, HEAD_DIM)
    attended = low(low_back(attend(queries, key_rows, value_rows)))
    residual = inputs + low_back(matmul(attended, w_out))
    moe_in = low(norm_rows(residual, gain_moe))
    logits = low_back(matmul(moe_in, router))
    gate_probs = jax.nn.softmax(jnp.take_along_axis(logits, route_seq, 1), -1)
    route_blocks = route_seq.reshape(N_TENSOR, TOK_LOC, TOP)
    pair_index = jax.vmap(slot_index)(route_blocks, order_seq)

    def place(block_rows, slot_ids):
        spread = jnp.repeat(block_rows, TOP, 0)
        return jnp.zeros((EXPERTS * CAP + 1, D), jnp.float32).at[slot_ids.reshape(-1)].set(spread)[:-1]
    sent = low_back(jax.vmap(place)(moe_in.reshape(N_TENSOR, TOK_LOC, D), pair_index).reshape(N_TENSOR, EXPERTS, CAP, D))
    gate_pre = low_back(jnp.einsum('tecd,edf->tecf', sent, expert_gate, precision=HIGHEST))
    up_pre = low_back(jnp.einsum('tecd,edf->tecf', sent, expert_up, precision=HIGHEST))
    hidden_act = low(jax.nn.silu(gate_pre) * up_pre)
    returned = low(low_back(jnp.einsum('tecf,efd->tecd', hidden_act, expert_down, precision=HIGHEST)))

    def pick(block_rows, slot_ids):
        slot_table = jnp.concatenate([block_rows.reshape(EXPERTS * CAP, D), jnp.zeros((1, D), jnp.float32)], 0)
        return slot_table[slot_ids]
    picked = jax.vmap(pick)(returned, pair_index).reshape(TOK_DEV, TOP, D)
    return residual + lax.optimization_barrier(jnp.sum(gate_probs[:, :, None] * picked, 1))

def reference(tokens, gain_attn, w_query, w_key, w_value, w_out, gain_moe, router, expert_gate, expert_up, expert_down, routes, fill_order, cotangent):
    params = tuple((weight.astype(jnp.float32) for weight in (gain_attn, w_query, w_key, w_value, w_out, gain_moe, router, expert_gate, expert_up, expert_down)))
    seq_in = tokens.astype(jnp.float32).reshape(N_EXPERT, TOK_DEV, D)
    seq_cot = cotangent.astype(jnp.float32).reshape(N_EXPERT, TOK_DEV, D)
    seq_routes = routes.reshape(N_EXPERT, TOK_DEV, TOP)
    seq_order = fill_order.reshape(N_EXPERT, N_TENSOR, TOK_LOC)

    def advance(totals, pieces):
        inputs, route_seq, order_seq, cot_seq = pieces

        def forward_fn(layer_in, *weights):
            return layer(layer_in, *weights, route_seq, order_seq)
        result, pullback = jax.vjp(forward_fn, inputs, *params)
        gradients = pullback(cot_seq)
        totals = tuple((total_grad + new_grad for total_grad, new_grad in zip(totals, gradients[1:])))
        return (totals, (result, gradients[0]))
    start_totals = tuple((jnp.zeros_like(weight) for weight in params))
    totals, (results, grad_in) = lax.scan(advance, start_totals, (seq_in, seq_routes, seq_order, seq_cot))
    return (results.reshape(TOKENS, D).astype(jnp.bfloat16), grad_in.reshape(TOKENS, D), totals[0], totals[1], totals[2], totals[3], totals[4], totals[5], totals[6], totals[7], totals[8], totals[9])
```

```python
import math

import jax
import jax.numpy as jnp
from jax import lax
from jax.sharding import PartitionSpec as P

HEAD_DIM = 64


EPSILON = 1e-06
THETA_BASE = 10000.0
MASKED = -1e30


def angles_of(row_count, head_size):
    half = head_size // 2
    freqs = jnp.exp(jnp.arange(half, dtype=jnp.float32) * (-2.0 * math.log(THETA_BASE) / head_size))
    return jnp.arange(row_count, dtype=jnp.float32)[:, None] * freqs[None, :]


def rotate(vectors, angles, sign):
    half = vectors.shape[-1] // 2
    cosine = jnp.cos(angles)[:, None, :]
    sine = sign * jnp.sin(angles)[:, None, :]
    first = vectors[..., :half]
    second = vectors[..., half:]
    return jnp.concatenate([first * cosine - second * sine, second * cosine + first * sine], -1)


def contract_last(left, right):
    return lax.dot_general(
        left, right, (((1,), (1,)), ((), ())), preferred_element_type=jnp.float32
    )


def contract_first(left, right):
    return lax.dot_general(
        left, right, (((0,), (0,)), ((), ())), preferred_element_type=jnp.float32
    )


def on_device(
    tokens,
    gain_attn,
    w_query,
    w_key,
    w_value,
    w_out,
    gain_moe,
    router,
    expert_gate,
    expert_up,
    expert_down,
    routes,
    fill_order,
    cotangent,
):
    tok_rows, width = tokens.shape
    tensor_size = lax.axis_size("tensor")
    seq_rows = tok_rows * tensor_size
    head_size = HEAD_DIM
    q_cols = w_query.shape[1]
    kv_cols = w_key.shape[1]
    q_heads = q_cols // head_size
    kv_heads = kv_cols // head_size
    q_group = q_heads // kv_heads
    score_scale = head_size ** (-0.5)
    local_experts = expert_gate.shape[0]
    expert_groups = lax.axis_size("expert")
    experts = local_experts * expert_groups
    top_k = routes.shape[1]
    capacity = (5 * tok_rows * top_k + 4 * experts - 1) // (4 * experts)
    gate_w, up_w, down_w = (expert_gate, expert_up, expert_down)
    inputs = tokens.astype(jnp.float32)
    inv_one = lax.rsqrt(jnp.mean(inputs * inputs, -1, keepdims=True) + EPSILON)
    normed = (inputs * inv_one * gain_attn).astype(jnp.bfloat16)
    normed_all = lax.all_gather(normed, "tensor", axis=0, tiled=True)
    w_joint = jnp.concatenate([w_query, w_key, w_value], 1)
    joint = jnp.dot(normed_all, w_joint, preferred_element_type=jnp.float32)
    angles = angles_of(seq_rows, head_size)
    queries = rotate(joint[:, :q_cols].reshape(seq_rows, q_heads, head_size), angles, 1.0).astype(
        jnp.bfloat16
    )
    key_rows = rotate(
        joint[:, q_cols : q_cols + kv_cols].reshape(seq_rows, kv_heads, head_size), angles, 1.0
    ).astype(jnp.bfloat16)
    value_rows = (
        joint[:, q_cols + kv_cols :].astype(jnp.bfloat16).reshape(seq_rows, kv_heads, head_size)
    )
    q_size = min(512, seq_rows)
    blocks = seq_rows // q_size
    key_pos = jnp.arange(seq_rows)

    def scores_of(q_block, row_start):
        grouped = q_block.reshape(q_size, kv_heads, q_group, head_size)
        raw_scores = (
            jnp.einsum("qkgd,tkd->kgqt", grouped, key_rows, preferred_element_type=jnp.float32)
            * score_scale
        )
        allowed = (row_start + jnp.arange(q_size))[:, None] >= key_pos[None, :]
        return (grouped, jnp.where(allowed, raw_scores, MASKED))

    def forward_block(block_args):
        q_block, row_start = block_args
        grouped, scores = scores_of(q_block, row_start)
        top_score = jnp.max(scores, -1, keepdims=True)
        exp_scores = jnp.exp(scores - top_score)
        row_total = jnp.sum(exp_scores, -1, keepdims=True)
        attn_probs = (exp_scores / row_total).astype(jnp.bfloat16)
        mixed_rows = jnp.einsum(
            "kgqt,tkd->qkgd", attn_probs, value_rows, preferred_element_type=jnp.float32
        )
        return (mixed_rows.astype(jnp.bfloat16).reshape(q_size, q_cols), top_score, row_total)

    q_blocks = queries.reshape(blocks, q_size, q_heads, head_size)
    starts = jnp.arange(blocks) * q_size
    attended, maxima, totals = lax.map(forward_block, (q_blocks, starts))
    attended = attended.reshape(seq_rows, q_cols)
    row_block = attended
    branch = lax.psum_scatter(
        jnp.dot(row_block, w_out, preferred_element_type=jnp.float32),
        "tensor",
        scatter_dimension=0,
        tiled=True,
    )
    residual = inputs + branch
    inv_two = lax.rsqrt(jnp.mean(residual * residual, -1, keepdims=True) + EPSILON)
    scaled = residual * inv_two
    moe_in = (scaled * gain_moe).astype(jnp.bfloat16)
    logits = jnp.dot(moe_in, router, preferred_element_type=jnp.float32)
    expert_ids = jnp.arange(experts, dtype=jnp.int32)
    named = jnp.sum((routes[:, :, None] == expert_ids[None, None, :]).astype(jnp.float32), 1)
    place_of = (fill_order[0][:, None] == jnp.arange(tok_rows)[None, :]).astype(jnp.bfloat16)
    ordered = jnp.dot(place_of, named.astype(jnp.bfloat16), preferred_element_type=jnp.float32)
    earlier = (jnp.arange(tok_rows)[:, None] > jnp.arange(tok_rows)[None, :]).astype(jnp.bfloat16)
    before = jnp.dot(earlier, ordered.astype(jnp.bfloat16), preferred_element_type=jnp.float32)
    rank = contract_first(place_of, before.astype(jnp.bfloat16))
    kept = named * (rank < capacity).astype(jnp.float32)
    top_logit = jnp.max(jnp.where(named > 0, logits, MASKED), -1, keepdims=True)
    exp_logits = jnp.where(named > 0, jnp.exp(jnp.minimum(logits - top_logit, 0.0)), 0.0)
    gates = exp_logits / jnp.sum(exp_logits, -1, keepdims=True)
    weights = gates * kept

    gate_all = lax.all_gather(gate_w[0], "tensor", axis=1, tiled=True)
    up_all = lax.all_gather(up_w[0], "tensor", axis=1, tiled=True)
    down_all = lax.all_gather(down_w[0], "tensor", axis=0, tiled=True)
    grad_out = cotangent.astype(jnp.float32)
    plane_cot = lax.all_gather(cotangent, "expert", axis=0, tiled=True)
    plane_in = lax.all_gather(moe_in, "expert", axis=0, tiled=True)
    plane_weights = lax.all_gather(weights, "expert", axis=0, tiled=True)
    mine = (expert_ids == lax.axis_index("expert")).astype(jnp.float32)
    my_weight = jnp.sum(plane_weights * mine[None, :], -1, keepdims=True)

    gate_pre = jnp.dot(plane_in, gate_all, preferred_element_type=jnp.float32)
    up_pre = jnp.dot(plane_in, up_all, preferred_element_type=jnp.float32)
    back_down = contract_last(plane_cot, down_all)
    gate_sigmoid = jax.nn.sigmoid(gate_pre)
    active = gate_pre * gate_sigmoid
    hidden = active * up_pre
    pair_grad = jnp.sum(hidden * back_down, -1, keepdims=True)
    hidden_w = (hidden * my_weight).astype(jnp.bfloat16)
    grad_hidden = back_down * my_weight
    grad_gate_pre = (
        grad_hidden * up_pre * gate_sigmoid * (1.0 + gate_pre * (1.0 - gate_sigmoid))
    ).astype(jnp.bfloat16)
    grad_up_pre = (grad_hidden * active).astype(jnp.bfloat16)
    out_part = jnp.dot(hidden_w, down_all, preferred_element_type=jnp.float32)
    in_part = contract_last(grad_gate_pre, gate_all) + contract_last(grad_up_pre, up_all)
    out_sum = lax.psum_scatter(
        out_part.astype(jnp.bfloat16), "expert", scatter_dimension=0, tiled=True
    )
    in_sum = lax.psum_scatter(
        in_part.astype(jnp.bfloat16), "expert", scatter_dimension=0, tiled=True
    )
    grad_gates = lax.psum_scatter(
        pair_grad * mine[None, :], "expert", scatter_dimension=0, tiled=True
    ) * kept
    grad_down = lax.psum_scatter(
        contract_first(hidden_w, plane_cot).astype(jnp.bfloat16),
        "tensor", scatter_dimension=0, tiled=True,
    ).astype(jnp.float32)[None]
    grad_gate = lax.psum_scatter(
        contract_first(plane_in, grad_gate_pre).astype(jnp.bfloat16),
        "tensor", scatter_dimension=1, tiled=True,
    ).astype(jnp.float32)[None]
    grad_up = lax.psum_scatter(
        contract_first(plane_in, grad_up_pre).astype(jnp.bfloat16),
        "tensor", scatter_dimension=1, tiled=True,
    ).astype(jnp.float32)[None]
    output_rows = residual + out_sum.astype(jnp.float32)
    grad_logits = (
        gates * (grad_gates - jnp.sum(gates * grad_gates, -1, keepdims=True))
    ).astype(jnp.bfloat16)
    grad_moe_in = in_sum.astype(jnp.float32) + contract_last(grad_logits, router)
    grad_router = contract_first(moe_in, grad_logits)
    grad_gain_moe = jnp.sum(grad_moe_in * scaled, 0)
    grad_norm_two = grad_moe_in * gain_moe
    grad_residual = (
        grad_out
        + inv_two * grad_norm_two
        - residual * inv_two**3 * jnp.mean(grad_norm_two * residual, -1, keepdims=True)
    )
    grad_branch = grad_residual.astype(jnp.bfloat16)
    shard_piece = lax.all_gather(grad_branch, "tensor", axis=0, tiled=True)
    grad_part = contract_last(shard_piece, w_out).astype(jnp.bfloat16)
    grad_mixed = grad_part
    grad_wout = contract_first(attended, shard_piece)
    grad_mixed, grad_w_out = (grad_mixed, grad_wout)
    grad_blocks = grad_mixed.reshape(blocks, q_size, q_heads, head_size)

    def backward_block(carry, block_args):
        grad_keys, grad_values = carry
        q_block, grad_block, row_start, top_score, row_total = block_args
        grouped, scores = scores_of(q_block, row_start)
        attn_probs = jnp.exp(scores - top_score) / row_total
        grad_grouped = grad_block.reshape(q_size, kv_heads, q_group, head_size)
        grad_probs = jnp.einsum(
            "qkgd,tkd->kgqt", grad_grouped, value_rows, preferred_element_type=jnp.float32
        )
        grad_values = grad_values + jnp.einsum(
            "kgqt,qkgd->tkd",
            attn_probs.astype(jnp.bfloat16),
            grad_grouped,
            preferred_element_type=jnp.float32,
        )
        grad_scores = (
            attn_probs
            * (grad_probs - jnp.sum(attn_probs * grad_probs, -1, keepdims=True))
            * score_scale
        ).astype(jnp.bfloat16)
        grad_query = jnp.einsum(
            "kgqt,tkd->qkgd", grad_scores, key_rows, preferred_element_type=jnp.float32
        ).reshape(q_size, q_heads, head_size)
        grad_keys = grad_keys + jnp.einsum(
            "kgqt,qkgd->tkd", grad_scores, grouped, preferred_element_type=jnp.float32
        )
        return ((grad_keys, grad_values), grad_query)

    zero_rows = jnp.zeros((seq_rows, kv_heads, head_size), jnp.float32)
    (grad_keys, grad_values), grad_queries = lax.scan(
        backward_block, (zero_rows, zero_rows), (q_blocks, grad_blocks, starts, maxima, totals)
    )
    grad_queries = grad_queries.reshape(seq_rows, q_heads, head_size)
    grad_q = rotate(grad_queries, angles, -1.0).astype(jnp.bfloat16).reshape(seq_rows, q_cols)
    grad_k = rotate(grad_keys, angles, -1.0).astype(jnp.bfloat16).reshape(seq_rows, kv_cols)
    grad_v = grad_values.astype(jnp.bfloat16).reshape(seq_rows, kv_cols)
    grad_joint = jnp.concatenate([grad_q, grad_k, grad_v], 1)
    grad_w_joint = contract_first(normed_all, grad_joint)
    row_block = grad_joint
    grad_normed = lax.psum_scatter(
        contract_last(row_block, w_joint), "tensor", scatter_dimension=0, tiled=True
    )
    grad_gain_attn = jnp.sum(grad_normed * inputs * inv_one, 0)
    grad_norm_one = grad_normed * gain_attn
    grad_tokens = (
        grad_residual
        + inv_one * grad_norm_one
        - inputs * inv_one**3 * jnp.mean(grad_norm_one * inputs, -1, keepdims=True)
    )
    summed_joint, summed_out = lax.psum((grad_w_joint, grad_w_out), "expert")
    summed_gain_attn, summed_gain_moe, summed_router = lax.psum(
        (grad_gain_attn, grad_gain_moe, grad_router), ("expert", "tensor")
    )
    return (
        output_rows.astype(jnp.bfloat16),
        grad_tokens,
        summed_gain_attn,
        summed_joint[:, :q_cols],
        summed_joint[:, q_cols : q_cols + kv_cols],
        summed_joint[:, q_cols + kv_cols :],
        summed_out,
        summed_gain_moe,
        summed_router,
        grad_gate,
        grad_up,
        grad_down,
    )


def solution(mesh):
    placed = (
        P(("expert", "tensor"), None),
        P(),
        P(None, "tensor"),
        P(None, "tensor"),
        P(None, "tensor"),
        P("tensor", None),
        P(),
        P(),
        P("expert", None, "tensor"),
        P("expert", None, "tensor"),
        P("expert", "tensor", None),
        P(("expert", "tensor"), None),
        P(("expert", "tensor"), None),
        P(("expert", "tensor"), None),
    )
    return jax.shard_map(
        on_device,
        mesh=mesh,
        in_specs=placed,
        out_specs=(
            P(("expert", "tensor"), None),
            P(("expert", "tensor"), None),
            P(),
            P(None, "tensor"),
            P(None, "tensor"),
            P(None, "tensor"),
            P("tensor", None),
            P(),
            P(),
            P("expert", None, "tensor"),
            P("expert", None, "tensor"),
            P("expert", "tensor", None),
        ),
        check_vma=False,
    )
```

```python
import math

import jax
import jax.numpy as jnp
from jax import lax
from jax.experimental import pallas as pl
from jax.experimental.pallas import tpu as pltpu
from jax.sharding import PartitionSpec as P

HEAD_DIM = 64


EPSILON = 1e-06
THETA_BASE = 10000.0
MASKED = -1e30


def angles_of(row_count, head_size):
    half = head_size // 2
    freqs = jnp.exp(jnp.arange(half, dtype=jnp.float32) * (-2.0 * math.log(THETA_BASE) / head_size))
    return jnp.arange(row_count, dtype=jnp.float32)[:, None] * freqs[None, :]


def rotate(vectors, angles, sign):
    half = vectors.shape[-1] // 2
    cosine = jnp.cos(angles)[:, None, :]
    sine = sign * jnp.sin(angles)[:, None, :]
    first = vectors[..., :half]
    second = vectors[..., half:]
    return jnp.concatenate([first * cosine - second * sine, second * cosine + first * sine], -1)


def contract_last(left, right):
    return lax.dot_general(
        left, right, (((1,), (1,)), ((), ())), preferred_element_type=jnp.float32
    )


def contract_first(left, right):
    return lax.dot_general(
        left, right, (((0,), (0,)), ((), ())), preferred_element_type=jnp.float32
    )


F32 = jnp.float32
BF16 = jnp.bfloat16
MESH = pl.DeviceIdType.MESH
BLK = 128
WIDTH = 1024
EXT = 1152
HALF = 512
OWN, PAIR, UP, DOWN, PAIR_UP, PAIR_DOWN, FAR, PAIR_FAR = range(8)
RELATIVE = ((0, 0), (0, 1), (1, 0), (3, 0), (1, 1), (3, 1), (2, 0), (2, 1))
TO_PAIR, TO_UP, TO_DOWN, TO_SIB = range(4)
ALL, TOP_ROWS, LOW_ROWS = ((0, 128), (0, 64), (64, 64))
GATHER = (
    (TO_PAIR, OWN, ALL, 0),
    (TO_UP, OWN, ALL, 0),
    (TO_DOWN, OWN, ALL, 0),
    (TO_UP, PAIR, ALL, 2),
    (TO_DOWN, PAIR, ALL, 2),
    (TO_PAIR, UP, ALL, 1),
    (TO_PAIR, DOWN, ALL, 1),
    (TO_UP, DOWN, TOP_ROWS, 0),
    (TO_DOWN, UP, LOW_ROWS, 0),
    (TO_DOWN, PAIR_UP, LOW_ROWS, 2),
    (TO_UP, PAIR_DOWN, TOP_ROWS, 2),
    (TO_PAIR, FAR, ALL, 1),
) + tuple((TO_SIB, chip, ALL, 0) for chip in range(8))
SIB = 12


class Place:
    def __init__(self):
        e = lax.axis_index("expert")
        t = lax.axis_index("tensor")
        self.e = e
        self.t = t
        self.core = lax.rem(e, 2)
        self.pair = lax.rem(e // 2, 2)
        self.ring = e // 4
        self.dests = (
            (e + 2 - 4 * self.pair, t),
            (lax.rem(e + 4, 16), t),
            (lax.rem(e + 12, 16), t),
            (e + 1 - 2 * self.core, t),
        )
        self.across = (e, 1 - t)

    def chip(self, dr, dp):
        return lax.rem(self.ring + dr, 4) * 2 + (self.pair + dp - 2 * self.pair * dp)

    def barrier(self):
        bar = pltpu.get_barrier_semaphore()
        for dest in self.dests + (self.across,):
            pl.semaphore_signal(bar, inc=1, device_id=dest, device_id_type=MESH)
        pl.semaphore_wait(bar, 5)


def seen_by_receiver(dest, dr, dp):
    if dest == TO_PAIR:
        return dr, 1 - dp
    if dest == TO_UP:
        return (dr + 3) % 4, dp
    if dest == TO_DOWN:
        return (dr + 1) % 4, dp
    return dr, dp


class Gather:
    def __init__(self, place, buf, send_sems, recv_sems):
        self.place, self.buf, self.ss, self.rs = place, buf, send_sems, recv_sems
        lanes = buf.shape[1]
        self.lanes = (pl.ds(0, lanes), pl.ds(0, HALF), pl.ds(HALF, lanes - HALF))

    def piece(self, dr, dp, core, rows, part):
        block = self.place.chip(dr, dp) * 2 + core
        start = pl.multiple_of(block * BLK + rows[0], 64)
        return self.buf.at[pl.ds(start, rows[1]), self.lanes[part]]

    def copy(self, k, receiving):
        dest, chip, rows, part = GATHER[k]
        dr, dp = RELATIVE[chip]
        core = self.place.core
        if receiving:
            dr, dp = seen_by_receiver(dest, dr, dp)
            if dest == TO_SIB:
                core = 1 - core
        ref = self.piece(dr, dp, core, rows, part)
        return pltpu.make_async_remote_copy(
            src_ref=ref,
            dst_ref=ref,
            send_sem=self.ss.at[k],
            recv_sem=self.rs.at[k],
            device_id=self.place.dests[dest],
            device_id_type=MESH,
        )

    def send(self, *keys):
        for k in keys:
            self.copy(k, False).start()

    def recv(self, *keys):
        for k in keys:
            self.copy(k, True).wait_recv()

    def sent(self):
        for k in range(len(GATHER)):
            self.copy(k, False).wait_send()

    def stage0(self):
        self.send(0, 1, 2, SIB + OWN)

    def stage1(self):
        self.recv(0)
        self.send(3, 4, SIB + PAIR)
        self.recv(1)
        self.send(6, 7, SIB + DOWN)
        self.recv(2)
        self.send(5, 8, SIB + UP)

    def stage2(self):
        self.recv(4, 5)
        self.send(9, SIB + PAIR_UP)
        self.recv(3, 6)
        self.send(10, SIB + PAIR_DOWN)
        self.recv(7, 8)
        self.send(11, SIB + FAR)

    def stage3(self):
        self.recv(9, 10, 11)
        self.send(SIB + PAIR_FAR)


SCATTER = (
    (TO_PAIR, PAIR, ALL, 1),
    (TO_PAIR, PAIR_UP, ALL, 1),
    (TO_PAIR, PAIR_DOWN, ALL, 1),
    (TO_PAIR, PAIR_FAR, ALL, 1),
    (TO_DOWN, FAR, TOP_ROWS, 2),
    (TO_UP, FAR, LOW_ROWS, 2),
    (TO_DOWN, PAIR_FAR, TOP_ROWS, 2),
    (TO_UP, PAIR_FAR, LOW_ROWS, 2),
    (TO_DOWN, FAR, TOP_ROWS, 1),
    (TO_UP, FAR, LOW_ROWS, 1),
    (TO_DOWN, DOWN, ALL, 2),
    (TO_UP, UP, ALL, 2),
    (TO_DOWN, PAIR_DOWN, ALL, 2),
    (TO_UP, PAIR_UP, ALL, 2),
    (TO_DOWN, DOWN, ALL, 1),
    (TO_UP, UP, ALL, 1),
    (TO_PAIR, PAIR, ALL, 2),
)


class Scatter:
    def __init__(self, place, sums, theirs, mine_of_sib, first, second, sib_ss, sib_rs, ss, rs):
        self.place, self.sums, self.theirs, self.from_sib = place, sums, theirs, mine_of_sib
        self.first, self.second = first, second
        self.sib_ss, self.sib_rs, self.ss, self.rs = sib_ss, sib_rs, ss, rs
        lanes = sums.shape[2]
        self.lanes = (pl.ds(0, lanes), pl.ds(0, HALF), pl.ds(HALF, lanes - HALF))

    def sib_copy(self, i):
        return pltpu.make_async_remote_copy(
            src_ref=self.theirs.at[i],
            dst_ref=self.from_sib.at[i],
            send_sem=self.sib_ss.at[i],
            recv_sem=self.sib_rs.at[i],
            device_id=self.place.dests[TO_SIB],
            device_id_type=MESH,
        )

    def join(self, i):
        self.sib_copy(i).wait_recv()
        self.sums[i] = (self.sums[i].astype(F32) + self.from_sib[i].astype(F32)).astype(BF16)

    def slot(self, k):
        _, _, rows, part = SCATTER[k]
        if part == 1:
            return self.first.at[FIRST_SLOT[k], pl.ds(0, rows[1])]
        return self.second.at[SECOND_SLOT[k], pl.ds(0, rows[1])]

    def copy(self, k):
        dest, chip, rows, part = SCATTER[k]
        return pltpu.make_async_remote_copy(
            src_ref=self.sums.at[chip, pl.ds(rows[0], rows[1]), self.lanes[part]],
            dst_ref=self.slot(k),
            send_sem=self.ss.at[k],
            recv_sem=self.rs.at[k],
            device_id=self.place.dests[dest],
            device_id_type=MESH,
        )

    def send(self, *keys):
        for k in keys:
            self.copy(k).start()

    def add(self, chip, rows, part, *keys):
        for k in keys:
            self.copy(k).wait_recv()
        here = self.sums.at[chip, pl.ds(rows[0], rows[1]), self.lanes[part]]
        total = here[...].astype(F32)
        for k in keys:
            total = total + self.slot(k)[...].astype(F32)
        here[...] = total.astype(BF16)

    def after(self, chip):
        if chip == PAIR:
            self.send(0)
        elif chip == PAIR_UP:
            self.send(1)
        elif chip == PAIR_DOWN:
            self.send(2)
        elif chip == FAR:
            self.send(4, 5)
        elif chip == PAIR_FAR:
            self.send(3, 6, 7)

    def stage1(self):
        self.add(FAR, ALL, 1, 3)
        self.send(8, 9)
        self.add(PAIR_DOWN, TOP_ROWS, 2, 6)
        self.send(12)
        self.add(PAIR_UP, LOW_ROWS, 2, 7)
        self.send(13)
        self.add(DOWN, TOP_ROWS, 2, 4)
        self.send(10)
        self.add(UP, LOW_ROWS, 2, 5)
        self.send(11)

    def stage2(self):
        self.add(PAIR, ALL, 2, 12, 13)
        self.send(16)
        self.add(DOWN, ALL, 1, 2)
        self.add(DOWN, TOP_ROWS, 1, 8)
        self.send(14)
        self.add(UP, ALL, 1, 1)
        self.add(UP, LOW_ROWS, 1, 9)
        self.send(15)

    def total(self, part):
        keys = (0, 14, 15) if part == 1 else (10, 11, 16)
        for k in keys:
            self.copy(k).wait_recv()
        total = self.sums[OWN, :, self.lanes[part]].astype(F32)
        for k in keys:
            total = total + self.slot(k)[...].astype(F32)
        return total

    def sent(self):
        for i in range(8):
            self.sib_copy(i).wait_send()
        for k in range(len(SCATTER)):
            self.copy(k).wait_send()


FIRST_SLOT = {k: i for i, k in enumerate(k for k in range(17) if SCATTER[k][3] == 1)}
SECOND_SLOT = {k: i for i, k in enumerate(k for k in range(17) if SCATTER[k][3] == 2)}


def dot_nn(a, b):
    return lax.dot_general(a, b, (((1,), (0,)), ((), ())), preferred_element_type=F32)


def dot_nt(a, b):
    return lax.dot_general(a, b, (((1,), (1,)), ((), ())), preferred_element_type=F32)


def pick(i, values):
    out = jnp.int32(values[-1])
    for n in range(len(values) - 2, -1, -1):
        out = jnp.where(i == n, jnp.int32(values[n]), out)
    return out


def expert_step(place, i, x, g, gates_w, ups_w, downs_w, hid, dgate, dup, in_s, in_t, out_s, out_t):
    chip = place.chip(pick(i, [d[0] for d in RELATIVE]), pick(i, [d[1] for d in RELATIVE]))
    rows = pl.ds(pl.multiple_of(chip * 256, 256), 256)
    lane = lax.broadcasted_iota(jnp.int32, (256, 128), 1)
    high, low = lane == place.e, lane == place.e + 16
    weight = jnp.sum(
        jnp.where(high | low, x[rows, WIDTH:EXT].astype(F32), 0.0), -1, keepdims=True
    )
    pair_grad = jnp.zeros((256, 1), F32)
    for h in range(2):
        cols = slice(h * 256, (h + 1) * 256)
        gate_pre = dot_nn(x[rows, :WIDTH], gates_w[h][...])
        up_pre = dot_nn(x[rows, :WIDTH], ups_w[h][...])
        back = dot_nt(g[rows, :], downs_w[h][...])
        sig = jax.nn.sigmoid(gate_pre)
        act = gate_pre * sig
        hidden = act * up_pre
        pair_grad = pair_grad + jnp.sum(hidden * back, -1, keepdims=True)
        grad_hidden = back * weight
        hid[rows, cols] = (hidden * weight).astype(BF16)
        dgate[rows, cols] = (grad_hidden * up_pre * (sig + act * (1.0 - sig))).astype(BF16)
        dup[rows, cols] = (grad_hidden * act).astype(BF16)
    mine = pl.ds(pl.multiple_of(place.core * BLK, BLK), BLK)
    other = pl.ds(pl.multiple_of((1 - place.core) * BLK, BLK), BLK)
    coarse = pair_grad.astype(BF16).astype(F32)
    ext = jnp.where(high, coarse, jnp.where(low, pair_grad - coarse, 0.0))

    def put(ours, theirs, cols, value):
        first, second = value[:BLK], value[BLK:]
        is_first = place.core == 0
        ours[i, :, cols] = jnp.where(is_first, first, second).astype(BF16)
        theirs[i, :, cols] = jnp.where(is_first, second, first).astype(BF16)

    put(in_s, in_t, slice(WIDTH, EXT), ext)
    for n in range(4):
        cols = slice(n * 256, (n + 1) * 256)
        put(
            in_s,
            in_t,
            cols,
            dot_nt(dgate[rows, 0:256], gates_w[0][cols, :])
            + dot_nt(dgate[rows, 256:512], gates_w[1][cols, :])
            + dot_nt(dup[rows, 0:256], ups_w[0][cols, :])
            + dot_nt(dup[rows, 256:512], ups_w[1][cols, :]),
        )
    for n in range(4):
        cols = slice(n * 256, (n + 1) * 256)
        put(
            out_s,
            out_t,
            cols,
            dot_nn(hid[rows, 0:256], downs_w[0][:, cols])
            + dot_nn(hid[rows, 256:512], downs_w[1][:, cols]),
        )


def moe_kernel(
    rows_ref, cot_ref, gate_ref, up_ref, down_ref,
    out_ref, in_ref, ggate_ref, gup_ref, gdown_ref,
    x, g, gate_p, up_p, down_p, hid, dgate, dup,
    in_s, in_t, in_f, out_s, out_t, out_f, in_1, in_2, out_1, out_2,
    gate_o, up_o, down_o, gate_i, up_i, down_i,
    ag_ss, ag_rs, sc_ss, sc_rs, sib_ss, sib_rs, y_ss, y_rs,
):
    place = Place()
    mine = pl.ds(pl.multiple_of(place.e * BLK, BLK), BLK)
    x[mine, :] = rows_ref[...]
    g[mine, :] = cot_ref[...]
    place.barrier()
    gx = Gather(place, x, ag_ss.at[0], ag_rs.at[0])
    gg = Gather(place, g, ag_ss.at[1], ag_rs.at[1])
    si = Scatter(place, in_s, in_t, in_f, in_1, in_2, sib_ss.at[0], sib_rs.at[0], sc_ss.at[0], sc_rs.at[0])
    so = Scatter(place, out_s, out_t, out_f, out_1, out_2, sib_ss.at[1], sib_rs.at[1], sc_ss.at[1], sc_rs.at[1])

    def across(k, src, dst):
        return pltpu.make_async_remote_copy(
            src_ref=src, dst_ref=dst, send_sem=y_ss.at[k], recv_sem=y_rs.at[k],
            device_id=place.across, device_id_type=MESH,
        )

    weight_copies = [across(0, gate_ref, gate_p), across(1, up_ref, up_p), across(2, down_ref, down_p)]
    gx.stage0()
    gg.stage0()
    for copy in weight_copies:
        copy.start()
    gates_w, ups_w, downs_w = (gate_ref, gate_p), (up_ref, up_p), (down_ref, down_p)

    def chip_step(i, carry):
        @pl.when(i == 0)
        def _():
            gx.recv(SIB + OWN)
            gg.recv(SIB + OWN)
            for copy in weight_copies:
                copy.wait_recv()

        @pl.when(i == 1)
        def _():
            gx.stage1()
            gg.stage1()

        @pl.when(i == 4)
        def _():
            gx.stage2()
            gg.stage2()

        @pl.when(i == 5)
        def _():
            gx.stage3()
            gg.stage3()

        for n in range(1, 8):

            @pl.when(i == n)
            def _(n=n):
                gx.recv(SIB + n)
                gg.recv(SIB + n)

        expert_step(place, i, x, g, gates_w, ups_w, downs_w, hid, dgate, dup, in_s, in_t, out_s, out_t)
        si.sib_copy(i).start()
        so.sib_copy(i).start()

        @pl.when(i >= 1)
        def _():
            si.join(i - 1)
            so.join(i - 1)

        for n in range(1, 8):

            @pl.when(i - 1 == n)
            def _(n=n):
                si.after(n)

        return carry

    lax.fori_loop(0, 8, chip_step, 0)

    def grad_step(i, carry):
        @pl.when(i == 0)
        def _():
            si.join(7)
            so.join(7)
            si.after(PAIR_FAR)

        @pl.when(i == 2)
        def _():
            si.stage1()

        @pl.when(i == 4)
        def _():
            si.stage2()
            for n in range(1, 8):
                so.after(n)

        @pl.when(i < 4)
        def _():
            cols = pl.ds(pl.multiple_of(i * 256, 256), 256)
            turned = x[:, cols].T
            both = dot_nn(turned, dgate[...])
            ggate_ref[cols, :] = both[:, :256]
            gate_o[cols, :] = both[:, 256:].astype(BF16)
            both = dot_nn(turned, dup[...])
            gup_ref[cols, :] = both[:, :256]
            up_o[cols, :] = both[:, 256:].astype(BF16)

        @pl.when(i == 4)
        def _():
            across(3, gate_o, gate_i).start()
            across(4, up_o, up_i).start()
            down_o[...] = dot_nn(hid[:, 256:].T, g[...]).astype(BF16)
            across(5, down_o, down_i).start()

        @pl.when(i == 5)
        def _():
            gdown_ref[...] = dot_nn(hid[:, :256].T, g[...])

        return carry

    lax.fori_loop(0, 6, grad_step, 0)
    first = si.total(1)
    in_ref[:, :HALF] = first
    in_ref[:, HALF:] = si.total(2)
    so.stage1()
    so.stage2()
    out_ref[:, :HALF] = so.total(1)
    out_ref[:, HALF:] = so.total(2)
    for k, (o, i, total) in enumerate(
        ((gate_o, gate_i, ggate_ref), (up_o, up_i, gup_ref), (down_o, down_i, gdown_ref))
    ):
        across(3 + k, o, i).wait_recv()
        total[...] = total[...] + i[...].astype(F32)
    gx.sent()
    gg.sent()
    si.sent()
    so.sent()
    for copy in weight_copies:
        copy.wait_send()
    across(3, gate_o, gate_i).wait_send()
    across(4, up_o, up_i).wait_send()
    across(5, down_o, down_i).wait_send()


def moe_call(rows, cot, gate_w, up_w, down_w):
    vm, dma = pltpu.VMEM, pltpu.SemaphoreType.DMA
    spec = pl.BlockSpec(memory_space=pltpu.VMEM)
    return pl.pallas_call(
        moe_kernel,
        out_shape=(
            jax.ShapeDtypeStruct((BLK, WIDTH), F32),
            jax.ShapeDtypeStruct((BLK, EXT), F32),
            jax.ShapeDtypeStruct((WIDTH, 256), F32),
            jax.ShapeDtypeStruct((WIDTH, 256), F32),
            jax.ShapeDtypeStruct((256, WIDTH), F32),
        ),
        in_specs=[spec] * 5,
        out_specs=[spec] * 5,
        scratch_shapes=[
            vm((2048, EXT), BF16), vm((2048, WIDTH), BF16),
            vm((WIDTH, 256), BF16), vm((WIDTH, 256), BF16), vm((256, WIDTH), BF16),
            vm((2048, 512), BF16), vm((2048, 512), BF16), vm((2048, 512), BF16),
            vm((8, BLK, EXT), BF16), vm((8, BLK, EXT), BF16), vm((8, BLK, EXT), BF16),
            vm((8, BLK, WIDTH), BF16), vm((8, BLK, WIDTH), BF16), vm((8, BLK, WIDTH), BF16),
            vm((8, BLK, HALF), BF16), vm((9, BLK, EXT - HALF), BF16),
            vm((8, BLK, HALF), BF16), vm((9, BLK, WIDTH - HALF), BF16),
            vm((WIDTH, 256), BF16), vm((WIDTH, 256), BF16), vm((256, WIDTH), BF16),
            vm((WIDTH, 256), BF16), vm((WIDTH, 256), BF16), vm((256, WIDTH), BF16),
            dma((2, 20)), dma((2, 20)), dma((2, 17)), dma((2, 17)), dma((2, 8)), dma((2, 8)),
            dma((6,)), dma((6,)),
        ],
        compiler_params=pltpu.CompilerParams(
            collective_id=1, has_side_effects=True, vmem_limit_bytes=60 * 2**20
        ),
        cost_estimate=pl.CostEstimate(flops=20 * 10**9, bytes_accessed=10**7, transcendentals=10**6),
        name="experts",
    )(rows, cot, gate_w, up_w, down_w)


def experts_by_collectives(moe_in, weights, cotangent, gate_w, up_w, down_w, expert_ids):
    gate_all = lax.all_gather(gate_w, "tensor", axis=1, tiled=True)
    up_all = lax.all_gather(up_w, "tensor", axis=1, tiled=True)
    down_all = lax.all_gather(down_w, "tensor", axis=0, tiled=True)
    plane_cot = lax.all_gather(cotangent, "expert", axis=0, tiled=True)
    plane_in = lax.all_gather(moe_in, "expert", axis=0, tiled=True)
    plane_weights = lax.all_gather(weights, "expert", axis=0, tiled=True)
    mine = (expert_ids == lax.axis_index("expert")).astype(jnp.float32)
    my_weight = jnp.sum(plane_weights * mine[None, :], -1, keepdims=True)

    gate_pre = jnp.dot(plane_in, gate_all, preferred_element_type=jnp.float32)
    up_pre = jnp.dot(plane_in, up_all, preferred_element_type=jnp.float32)
    back_down = contract_last(plane_cot, down_all)
    gate_sigmoid = jax.nn.sigmoid(gate_pre)
    active = gate_pre * gate_sigmoid
    hidden = active * up_pre
    pair_grad = jnp.sum(hidden * back_down, -1, keepdims=True)
    hidden_w = (hidden * my_weight).astype(jnp.bfloat16)
    grad_hidden = back_down * my_weight
    grad_gate_pre = (
        grad_hidden * up_pre * gate_sigmoid * (1.0 + gate_pre * (1.0 - gate_sigmoid))
    ).astype(jnp.bfloat16)
    grad_up_pre = (grad_hidden * active).astype(jnp.bfloat16)
    out_part = jnp.dot(hidden_w, down_all, preferred_element_type=jnp.float32)
    in_part = contract_last(grad_gate_pre, gate_all) + contract_last(grad_up_pre, up_all)
    out_sum = lax.psum_scatter(
        out_part.astype(jnp.bfloat16), "expert", scatter_dimension=0, tiled=True
    )
    in_sum = lax.psum_scatter(
        in_part.astype(jnp.bfloat16), "expert", scatter_dimension=0, tiled=True
    )
    grad_gates = lax.psum_scatter(
        pair_grad * mine[None, :], "expert", scatter_dimension=0, tiled=True
    )
    grad_down = lax.psum_scatter(
        contract_first(hidden_w, plane_cot).astype(jnp.bfloat16),
        "tensor", scatter_dimension=0, tiled=True,
    ).astype(jnp.float32)[None]
    grad_gate = lax.psum_scatter(
        contract_first(plane_in, grad_gate_pre).astype(jnp.bfloat16),
        "tensor", scatter_dimension=1, tiled=True,
    ).astype(jnp.float32)[None]
    grad_up = lax.psum_scatter(
        contract_first(plane_in, grad_up_pre).astype(jnp.bfloat16),
        "tensor", scatter_dimension=1, tiled=True,
    ).astype(jnp.float32)[None]
    return out_sum, in_sum, grad_gates, grad_gate, grad_up, grad_down


def on_device(
    tokens,
    gain_attn,
    w_query,
    w_key,
    w_value,
    w_out,
    gain_moe,
    router,
    expert_gate,
    expert_up,
    expert_down,
    routes,
    fill_order,
    cotangent,
):
    tok_rows, width = tokens.shape
    tensor_size = lax.axis_size("tensor")
    seq_rows = tok_rows * tensor_size
    head_size = HEAD_DIM
    q_cols = w_query.shape[1]
    kv_cols = w_key.shape[1]
    q_heads = q_cols // head_size
    kv_heads = kv_cols // head_size
    q_group = q_heads // kv_heads
    score_scale = head_size ** (-0.5)
    local_experts = expert_gate.shape[0]
    expert_groups = lax.axis_size("expert")
    experts = local_experts * expert_groups
    top_k = routes.shape[1]
    capacity = (5 * tok_rows * top_k + 4 * experts - 1) // (4 * experts)
    gate_w, up_w, down_w = (expert_gate, expert_up, expert_down)
    inputs = tokens.astype(jnp.float32)
    inv_one = lax.rsqrt(jnp.mean(inputs * inputs, -1, keepdims=True) + EPSILON)
    normed = (inputs * inv_one * gain_attn).astype(jnp.bfloat16)
    normed_all = lax.all_gather(normed, "tensor", axis=0, tiled=True)
    w_joint = jnp.concatenate([w_query, w_key, w_value], 1)
    joint = jnp.dot(normed_all, w_joint, preferred_element_type=jnp.float32)
    angles = angles_of(seq_rows, head_size)
    queries = rotate(joint[:, :q_cols].reshape(seq_rows, q_heads, head_size), angles, 1.0).astype(
        jnp.bfloat16
    )
    key_rows = rotate(
        joint[:, q_cols : q_cols + kv_cols].reshape(seq_rows, kv_heads, head_size), angles, 1.0
    ).astype(jnp.bfloat16)
    value_rows = (
        joint[:, q_cols + kv_cols :].astype(jnp.bfloat16).reshape(seq_rows, kv_heads, head_size)
    )
    q_size = min(512, seq_rows)
    blocks = seq_rows // q_size
    key_pos = jnp.arange(seq_rows)

    def scores_of(q_block, row_start):
        grouped = q_block.reshape(q_size, kv_heads, q_group, head_size)
        raw_scores = (
            jnp.einsum("qkgd,tkd->kgqt", grouped, key_rows, preferred_element_type=jnp.float32)
            * score_scale
        )
        allowed = (row_start + jnp.arange(q_size))[:, None] >= key_pos[None, :]
        return (grouped, jnp.where(allowed, raw_scores, MASKED))

    def forward_block(block_args):
        q_block, row_start = block_args
        grouped, scores = scores_of(q_block, row_start)
        top_score = jnp.max(scores, -1, keepdims=True)
        exp_scores = jnp.exp(scores - top_score)
        row_total = jnp.sum(exp_scores, -1, keepdims=True)
        attn_probs = (exp_scores / row_total).astype(jnp.bfloat16)
        mixed_rows = jnp.einsum(
            "kgqt,tkd->qkgd", attn_probs, value_rows, preferred_element_type=jnp.float32
        )
        return (mixed_rows.astype(jnp.bfloat16).reshape(q_size, q_cols), top_score, row_total)

    q_blocks = queries.reshape(blocks, q_size, q_heads, head_size)
    starts = jnp.arange(blocks) * q_size
    attended, maxima, totals = lax.map(forward_block, (q_blocks, starts))
    attended = attended.reshape(seq_rows, q_cols)
    row_block = attended
    branch = lax.psum_scatter(
        jnp.dot(row_block, w_out, preferred_element_type=jnp.float32),
        "tensor",
        scatter_dimension=0,
        tiled=True,
    )
    residual = inputs + branch
    inv_two = lax.rsqrt(jnp.mean(residual * residual, -1, keepdims=True) + EPSILON)
    scaled = residual * inv_two
    moe_in = (scaled * gain_moe).astype(jnp.bfloat16)
    logits = jnp.dot(moe_in, router, preferred_element_type=jnp.float32)
    expert_ids = jnp.arange(experts, dtype=jnp.int32)
    named = jnp.sum((routes[:, :, None] == expert_ids[None, None, :]).astype(jnp.float32), 1)
    place_of = (fill_order[0][:, None] == jnp.arange(tok_rows)[None, :]).astype(jnp.bfloat16)
    ordered = jnp.dot(place_of, named.astype(jnp.bfloat16), preferred_element_type=jnp.float32)
    earlier = (jnp.arange(tok_rows)[:, None] > jnp.arange(tok_rows)[None, :]).astype(jnp.bfloat16)
    before = jnp.dot(earlier, ordered.astype(jnp.bfloat16), preferred_element_type=jnp.float32)
    rank = contract_first(place_of, before.astype(jnp.bfloat16))
    kept = named * (rank < capacity).astype(jnp.float32)
    top_logit = jnp.max(jnp.where(named > 0, logits, MASKED), -1, keepdims=True)
    exp_logits = jnp.where(named > 0, jnp.exp(jnp.minimum(logits - top_logit, 0.0)), 0.0)
    gates = exp_logits / jnp.sum(exp_logits, -1, keepdims=True)
    weights = gates * kept

    grad_out = cotangent.astype(jnp.float32)
    kernel_fits = (
        expert_groups == 16 and tensor_size == 2 and local_experts == 1
        and tok_rows == BLK and width == WIDTH and gate_w.shape[2] == 256
    )
    if kernel_fits:
        coarse = weights.astype(BF16)
        fine = (weights - coarse.astype(F32)).astype(BF16)
        blank = jnp.zeros((tok_rows, EXT - WIDTH - 2 * experts), BF16)
        rows_ext = jnp.concatenate([moe_in, coarse, fine, blank], 1)
        out_sum, in_ext, grad_gate, grad_up, grad_down = moe_call(
            rows_ext, cotangent, gate_w[0], up_w[0], down_w[0]
        )
        in_sum = in_ext[:, :WIDTH]
        grad_gates = in_ext[:, WIDTH : WIDTH + 16] + in_ext[:, WIDTH + 16 : WIDTH + 32]
        grad_gate, grad_up, grad_down = grad_gate[None], grad_up[None], grad_down[None]
    else:
        out_sum, in_sum, grad_gates, grad_gate, grad_up, grad_down = experts_by_collectives(
            moe_in, weights, cotangent, gate_w[0], up_w[0], down_w[0], expert_ids
        )
    grad_gates = grad_gates * kept
    output_rows = residual + out_sum.astype(jnp.float32)
    grad_logits = (
        gates * (grad_gates - jnp.sum(gates * grad_gates, -1, keepdims=True))
    ).astype(jnp.bfloat16)
    grad_moe_in = in_sum.astype(jnp.float32) + contract_last(grad_logits, router)
    grad_router = contract_first(moe_in, grad_logits)
    grad_gain_moe = jnp.sum(grad_moe_in * scaled, 0)
    grad_norm_two = grad_moe_in * gain_moe
    grad_residual = (
        grad_out
        + inv_two * grad_norm_two
        - residual * inv_two**3 * jnp.mean(grad_norm_two * residual, -1, keepdims=True)
    )
    grad_branch = grad_residual.astype(jnp.bfloat16)
    shard_piece = lax.all_gather(grad_branch, "tensor", axis=0, tiled=True)
    grad_part = contract_last(shard_piece, w_out).astype(jnp.bfloat16)
    grad_mixed = grad_part
    grad_wout = contract_first(attended, shard_piece)
    grad_mixed, grad_w_out = (grad_mixed, grad_wout)
    grad_blocks = grad_mixed.reshape(blocks, q_size, q_heads, head_size)

    def backward_block(carry, block_args):
        grad_keys, grad_values = carry
        q_block, grad_block, row_start, top_score, row_total = block_args
        grouped, scores = scores_of(q_block, row_start)
        attn_probs = jnp.exp(scores - top_score) / row_total
        grad_grouped = grad_block.reshape(q_size, kv_heads, q_group, head_size)
        grad_probs = jnp.einsum(
            "qkgd,tkd->kgqt", grad_grouped, value_rows, preferred_element_type=jnp.float32
        )
        grad_values = grad_values + jnp.einsum(
            "kgqt,qkgd->tkd",
            attn_probs.astype(jnp.bfloat16),
            grad_grouped,
            preferred_element_type=jnp.float32,
        )
        grad_scores = (
            attn_probs
            * (grad_probs - jnp.sum(attn_probs * grad_probs, -1, keepdims=True))
            * score_scale
        ).astype(jnp.bfloat16)
        grad_query = jnp.einsum(
            "kgqt,tkd->qkgd", grad_scores, key_rows, preferred_element_type=jnp.float32
        ).reshape(q_size, q_heads, head_size)
        grad_keys = grad_keys + jnp.einsum(
            "kgqt,qkgd->tkd", grad_scores, grouped, preferred_element_type=jnp.float32
        )
        return ((grad_keys, grad_values), grad_query)

    zero_rows = jnp.zeros((seq_rows, kv_heads, head_size), jnp.float32)
    (grad_keys, grad_values), grad_queries = lax.scan(
        backward_block, (zero_rows, zero_rows), (q_blocks, grad_blocks, starts, maxima, totals)
    )
    grad_queries = grad_queries.reshape(seq_rows, q_heads, head_size)
    grad_q = rotate(grad_queries, angles, -1.0).astype(jnp.bfloat16).reshape(seq_rows, q_cols)
    grad_k = rotate(grad_keys, angles, -1.0).astype(jnp.bfloat16).reshape(seq_rows, kv_cols)
    grad_v = grad_values.astype(jnp.bfloat16).reshape(seq_rows, kv_cols)
    grad_joint = jnp.concatenate([grad_q, grad_k, grad_v], 1)
    grad_w_joint = contract_first(normed_all, grad_joint)
    row_block = grad_joint
    grad_normed = lax.psum_scatter(
        contract_last(row_block, w_joint), "tensor", scatter_dimension=0, tiled=True
    )
    grad_gain_attn = jnp.sum(grad_normed * inputs * inv_one, 0)
    grad_norm_one = grad_normed * gain_attn
    grad_tokens = (
        grad_residual
        + inv_one * grad_norm_one
        - inputs * inv_one**3 * jnp.mean(grad_norm_one * inputs, -1, keepdims=True)
    )
    summed_joint, summed_out = lax.psum((grad_w_joint, grad_w_out), "expert")
    summed_gain_attn, summed_gain_moe, summed_router = lax.psum(
        (grad_gain_attn, grad_gain_moe, grad_router), ("expert", "tensor")
    )
    return (
        output_rows.astype(jnp.bfloat16),
        grad_tokens,
        summed_gain_attn,
        summed_joint[:, :q_cols],
        summed_joint[:, q_cols : q_cols + kv_cols],
        summed_joint[:, q_cols + kv_cols :],
        summed_out,
        summed_gain_moe,
        summed_router,
        grad_gate,
        grad_up,
        grad_down,
    )


def solution(mesh):
    placed = (
        P(("expert", "tensor"), None),
        P(),
        P(None, "tensor"),
        P(None, "tensor"),
        P(None, "tensor"),
        P("tensor", None),
        P(),
        P(),
        P("expert", None, "tensor"),
        P("expert", None, "tensor"),
        P("expert", "tensor", None),
        P(("expert", "tensor"), None),
        P(("expert", "tensor"), None),
        P(("expert", "tensor"), None),
    )
    return jax.shard_map(
        on_device,
        mesh=mesh,
        in_specs=placed,
        out_specs=(
            P(("expert", "tensor"), None),
            P(("expert", "tensor"), None),
            P(),
            P(None, "tensor"),
            P(None, "tensor"),
            P(None, "tensor"),
            P("tensor", None),
            P(),
            P(),
            P("expert", None, "tensor"),
            P("expert", None, "tensor"),
            P("expert", "tensor", None),
        ),
        check_vma=False,
    )
```

```python
import math

import jax
import jax.numpy as jnp
import numpy as np
from jax import lax
from jax.experimental import pallas as pl
from jax.experimental.pallas import tpu as pltpu
from jax.sharding import PartitionSpec as P

HEAD_DIM = 64


EPSILON = 1e-06
THETA_BASE = 10000.0
MASKED = -1e30


def angles_of(row_count, head_size):
    half = head_size // 2
    freqs = jnp.exp(jnp.arange(half, dtype=jnp.float32) * (-2.0 * math.log(THETA_BASE) / head_size))
    return jnp.arange(row_count, dtype=jnp.float32)[:, None] * freqs[None, :]


def rotate(vectors, angles, sign):
    half = vectors.shape[-1] // 2
    cosine = jnp.cos(angles)[:, None, :]
    sine = sign * jnp.sin(angles)[:, None, :]
    first = vectors[..., :half]
    second = vectors[..., half:]
    return jnp.concatenate([first * cosine - second * sine, second * cosine + first * sine], -1)


def contract_last(left, right):
    return lax.dot_general(
        left, right, (((1,), (1,)), ((), ())), preferred_element_type=jnp.float32
    )


def contract_first(left, right):
    return lax.dot_general(
        left, right, (((0,), (0,)), ((), ())), preferred_element_type=jnp.float32
    )


F32 = jnp.float32
BF16 = jnp.bfloat16
MESH = pl.DeviceIdType.MESH
BLK = 128
WIDTH = 1024
EXT = 1152
HALF = 512
OWN, PAIR, UP, DOWN, PAIR_UP, PAIR_DOWN, FAR, PAIR_FAR = range(8)
RELATIVE = ((0, 0), (0, 1), (1, 0), (3, 0), (1, 1), (3, 1), (2, 0), (2, 1))
TO_PAIR, TO_UP, TO_DOWN, TO_SIB = range(4)
ALL, TOP_ROWS, LOW_ROWS = ((0, 2), (0, 1), (1, 1))
GATHER = (
    (TO_PAIR, OWN, ALL, 0),
    (TO_UP, OWN, ALL, 0),
    (TO_DOWN, OWN, ALL, 0),
    (TO_UP, PAIR, ALL, 2),
    (TO_DOWN, PAIR, ALL, 2),
    (TO_PAIR, UP, ALL, 1),
    (TO_PAIR, DOWN, ALL, 1),
    (TO_UP, DOWN, TOP_ROWS, 0),
    (TO_DOWN, UP, LOW_ROWS, 0),
    (TO_DOWN, PAIR_UP, LOW_ROWS, 2),
    (TO_UP, PAIR_DOWN, TOP_ROWS, 2),
    (TO_PAIR, FAR, ALL, 1),
) + tuple((TO_SIB, chip, ALL, 0) for chip in range(8))
SIB = 12


class Place:
    def __init__(self):
        e = lax.axis_index("expert")
        t = lax.axis_index("tensor")
        self.e = e
        self.t = t
        self.core = lax.rem(e, 2)
        self.pair = lax.rem(e // 2, 2)
        self.ring = e // 4
        self.dests = (
            (e + 2 - 4 * self.pair, t),
            (lax.rem(e + 4, 16), t),
            (lax.rem(e + 12, 16), t),
            (e + 1 - 2 * self.core, t),
        )
        self.across = (e, 1 - t)

    def chip(self, dr, dp):
        return lax.rem(self.ring + dr, 4) * 2 + (self.pair + dp - 2 * self.pair * dp)

    def numbered(self, i):
        return self.chip(pick(i, [d[0] for d in RELATIVE]), pick(i, [d[1] for d in RELATIVE]))

    def barrier(self):
        bar = pltpu.get_barrier_semaphore()
        for dest in self.dests + (self.across,):
            pl.semaphore_signal(bar, inc=1, device_id=dest, device_id_type=MESH)
        pl.semaphore_wait(bar, 5)


def pick(i, values):
    out = jnp.int32(values[-1])
    for n in range(len(values) - 2, -1, -1):
        out = jnp.where(i == n, jnp.int32(values[n]), out)
    return out


def seen_by_receiver(dest, dr, dp):
    if dest == TO_PAIR:
        return dr, 1 - dp
    if dest == TO_UP:
        return (dr + 3) % 4, dp
    if dest == TO_DOWN:
        return (dr + 1) % 4, dp
    return dr, dp


class Gather:
    def __init__(self, place, buf, send_sems, recv_sems):
        self.place, self.buf, self.ss, self.rs = place, buf, send_sems, recv_sems
        lanes = buf.shape[1]
        self.size = buf.shape[0] // 16
        self.lanes = (pl.ds(0, lanes), pl.ds(0, HALF), pl.ds(HALF, lanes - HALF))

    def piece(self, dr, dp, core, rows, part):
        block = self.place.chip(dr, dp) * 2 + core
        half = self.size // 2
        start = pl.multiple_of(block * self.size + rows[0] * half, half)
        return self.buf.at[pl.ds(start, rows[1] * half), self.lanes[part]]

    def copy(self, k, receiving):
        dest, chip, rows, part = GATHER[k]
        dr, dp = RELATIVE[chip]
        core = self.place.core
        if receiving:
            dr, dp = seen_by_receiver(dest, dr, dp)
            if dest == TO_SIB:
                core = 1 - core
        ref = self.piece(dr, dp, core, rows, part)
        return pltpu.make_async_remote_copy(
            src_ref=ref,
            dst_ref=ref,
            send_sem=self.ss.at[k],
            recv_sem=self.rs.at[k],
            device_id=self.place.dests[dest],
            device_id_type=MESH,
        )

    def send(self, *keys):
        for k in keys:
            self.copy(k, False).start()

    def recv(self, *keys):
        for k in keys:
            self.copy(k, True).wait_recv()

    def sent(self):
        for k in range(len(GATHER)):
            self.copy(k, False).wait_send()

    def stage0(self):
        self.send(0, 1, 2, SIB + OWN)

    def stage1(self):
        self.recv(0)
        self.send(3, 4, SIB + PAIR)
        self.recv(1)
        self.send(6, 7, SIB + DOWN)
        self.recv(2)
        self.send(5, 8, SIB + UP)

    def stage2(self):
        self.recv(4, 5)
        self.send(9, SIB + PAIR_UP)
        self.recv(3, 6)
        self.send(10, SIB + PAIR_DOWN)
        self.recv(7, 8)
        self.send(11, SIB + FAR)

    def stage3(self):
        self.recv(9, 10, 11)
        self.send(SIB + PAIR_FAR)

    def from_sib(self):
        for n in range(8):
            self.recv(SIB + n)


SCATTER = (
    (TO_PAIR, PAIR, ALL, 1),
    (TO_PAIR, PAIR_UP, ALL, 1),
    (TO_PAIR, PAIR_DOWN, ALL, 1),
    (TO_PAIR, PAIR_FAR, ALL, 1),
    (TO_DOWN, FAR, TOP_ROWS, 2),
    (TO_UP, FAR, LOW_ROWS, 2),
    (TO_DOWN, PAIR_FAR, TOP_ROWS, 2),
    (TO_UP, PAIR_FAR, LOW_ROWS, 2),
    (TO_DOWN, FAR, TOP_ROWS, 1),
    (TO_UP, FAR, LOW_ROWS, 1),
    (TO_DOWN, DOWN, ALL, 2),
    (TO_UP, UP, ALL, 2),
    (TO_DOWN, PAIR_DOWN, ALL, 2),
    (TO_UP, PAIR_UP, ALL, 2),
    (TO_DOWN, DOWN, ALL, 1),
    (TO_UP, UP, ALL, 1),
    (TO_PAIR, PAIR, ALL, 2),
)
FIRST_SLOT = {0: 0, 1: 2, 2: 4, 3: 6, 14: 8, 15: 10, 8: 12, 9: 13}
SECOND_SLOT = {10: 0, 11: 2, 12: 4, 13: 6, 16: 8, 4: 10, 5: 11, 6: 12, 7: 13}


class Scatter:
    def __init__(self, place, sums, theirs, from_sib, first, second, sib_ss, sib_rs, ss, rs):
        self.place, self.sums, self.theirs, self.from_sib = place, sums, theirs, from_sib
        self.first, self.second = first, second
        self.sib_ss, self.sib_rs, self.ss, self.rs = sib_ss, sib_rs, ss, rs
        self.size, lanes = from_sib.shape[1:]
        self.lanes = (pl.ds(0, lanes), pl.ds(0, HALF), pl.ds(HALF, lanes - HALF))

    def sib_copy(self, i):
        return pltpu.make_async_remote_copy(
            src_ref=self.theirs.at[i],
            dst_ref=self.from_sib.at[i],
            send_sem=self.sib_ss.at[i],
            recv_sem=self.sib_rs.at[i],
            device_id=self.place.dests[TO_SIB],
            device_id_type=MESH,
        )

    def join(self, i):
        self.sib_copy(i).wait_recv()
        self.sums[i] = (self.sums[i].astype(F32) + self.from_sib[i].astype(F32)).astype(BF16)

    def rows(self, rows):
        half = self.size // 2
        return pl.ds(rows[0] * half, rows[1] * half)

    def slot(self, k):
        _, _, rows, part = SCATTER[k]
        half = self.size // 2
        buf, at = (self.first, FIRST_SLOT[k]) if part == 1 else (self.second, SECOND_SLOT[k])
        return buf.at[at // 2, pl.ds(at % 2 * half, rows[1] * half)]

    def copy(self, k):
        dest, chip, rows, part = SCATTER[k]
        return pltpu.make_async_remote_copy(
            src_ref=self.sums.at[chip, self.rows(rows), self.lanes[part]],
            dst_ref=self.slot(k),
            send_sem=self.ss.at[k],
            recv_sem=self.rs.at[k],
            device_id=self.place.dests[dest],
            device_id_type=MESH,
        )

    def send(self, *keys):
        for k in keys:
            self.copy(k).start()

    def add(self, chip, rows, part, *keys):
        for k in keys:
            self.copy(k).wait_recv()
        here = self.sums.at[chip, self.rows(rows), self.lanes[part]]
        total = here[...].astype(F32)
        for k in keys:
            total = total + self.slot(k)[...].astype(F32)
        here[...] = total.astype(BF16)

    def after(self, chip):
        if chip == PAIR:
            self.send(0)
        elif chip == PAIR_UP:
            self.send(1)
        elif chip == PAIR_DOWN:
            self.send(2)
        elif chip == FAR:
            self.send(4, 5)
        elif chip == PAIR_FAR:
            self.send(3, 6, 7)

    def stage1(self):
        self.add(FAR, ALL, 1, 3)
        self.send(8, 9)
        self.add(PAIR_DOWN, TOP_ROWS, 2, 6)
        self.send(12)
        self.add(PAIR_UP, LOW_ROWS, 2, 7)
        self.send(13)
        self.add(DOWN, TOP_ROWS, 2, 4)
        self.send(10)
        self.add(UP, LOW_ROWS, 2, 5)
        self.send(11)

    def stage2(self):
        self.add(PAIR, ALL, 2, 12, 13)
        self.send(16)
        self.add(DOWN, ALL, 1, 2)
        self.add(DOWN, TOP_ROWS, 1, 8)
        self.send(14)
        self.add(UP, ALL, 1, 1)
        self.add(UP, LOW_ROWS, 1, 9)
        self.send(15)

    def total(self, part):
        keys = (0, 14, 15) if part == 1 else (10, 11, 16)
        for k in keys:
            self.copy(k).wait_recv()
        total = self.sums[OWN, :, self.lanes[part]].astype(F32)
        for k in keys:
            total = total + self.slot(k)[...].astype(F32)
        return total

    def sent(self):
        for i in range(8):
            self.sib_copy(i).wait_send()
        for k in range(len(SCATTER)):
            self.copy(k).wait_send()


def dot_nn(a, b):
    return lax.dot_general(a, b, (((1,), (0,)), ((), ())), preferred_element_type=F32)


def dot_nt(a, b):
    return lax.dot_general(a, b, (((1,), (1,)), ((), ())), preferred_element_type=F32)


def dot_tn(a, b):
    return lax.dot_general(a, b, (((0,), (0,)), ((), ())), preferred_element_type=F32)


def expert_step(place, i, x, g, gates_w, ups_w, downs_w, hid, dgate, dup, in_s, in_t, out_s, out_t):
    rows = pl.ds(pl.multiple_of(place.numbered(i) * 256, 256), 256)
    lane = lax.broadcasted_iota(jnp.int32, (256, 128), 1)
    high, low = lane == place.e, lane == place.e + 16
    weight = jnp.sum(
        jnp.where(high | low, x[rows, WIDTH:EXT].astype(F32), 0.0), -1, keepdims=True
    )
    pair_grad = jnp.zeros((256, 1), F32)
    for h in range(2):
        cols = slice(h * 256, (h + 1) * 256)
        gate_pre = dot_nn(x[rows, :WIDTH], gates_w[h][...])
        up_pre = dot_nn(x[rows, :WIDTH], ups_w[h][...])
        back = dot_nt(g[rows, :], downs_w[h][...])
        sig = jax.nn.sigmoid(gate_pre)
        act = gate_pre * sig
        hidden = act * up_pre
        pair_grad = pair_grad + jnp.sum(hidden * back, -1, keepdims=True)
        grad_hidden = back * weight
        hid[rows, cols] = (hidden * weight).astype(BF16)
        dgate[rows, cols] = (grad_hidden * up_pre * (sig + act * (1.0 - sig))).astype(BF16)
        dup[rows, cols] = (grad_hidden * act).astype(BF16)
    coarse = pair_grad.astype(BF16).astype(F32)
    ext = jnp.where(high, coarse, jnp.where(low, pair_grad - coarse, 0.0))
    put(place, i, in_s, in_t, slice(WIDTH, EXT), ext)
    for n in range(4):
        cols = slice(n * 256, (n + 1) * 256)
        value = (
            dot_nt(dgate[rows, 0:256], gates_w[0][cols, :])
            + dot_nt(dgate[rows, 256:512], gates_w[1][cols, :])
            + dot_nt(dup[rows, 0:256], ups_w[0][cols, :])
            + dot_nt(dup[rows, 256:512], ups_w[1][cols, :])
        )
        put(place, i, in_s, in_t, cols, value)
    for n in range(4):
        cols = slice(n * 256, (n + 1) * 256)
        value = dot_nn(hid[rows, 0:256], downs_w[0][:, cols]) + dot_nn(
            hid[rows, 256:512], downs_w[1][:, cols]
        )
        put(place, i, out_s, out_t, cols, value)


def put(place, i, ours, theirs, cols, value):
    half = value.shape[0] // 2
    first, second = value[:half], value[half:]
    is_first = place.core == 0
    ours[i, :, cols] = jnp.where(is_first, first, second).astype(BF16)
    theirs[i, :, cols] = jnp.where(is_first, second, first).astype(BF16)


def mean_last(v):
    return jnp.sum(v, -1, keepdims=True) * (1.0 / v.shape[-1])


def swapped(v):
    lane = lax.broadcasted_iota(jnp.int32, v.shape, 1)
    return jnp.where(lax.rem(lane, 64) < 32, pltpu.roll(v, 96, 1), pltpu.roll(v, 32, 1))


def doubled(v, half):
    lane = lax.broadcasted_iota(jnp.int32, v.shape, 1)
    one = jnp.where((lane < 64) == (half == 0), v, 0.0)
    return one + pltpu.roll(one, 64, 1)


def stacked(v):
    lane = lax.broadcasted_iota(jnp.int32, v.shape, 1)
    return jnp.concatenate([jnp.where(lane < 64, v, 0.0), jnp.where(lane < 64, 0.0, v)], 0)


def unstacked(v):
    rows = v.shape[0] // 2
    lane = lax.broadcasted_iota(jnp.int32, (rows, 128), 1)
    return jnp.where(lane < 64, v[:rows], v[rows:])


def layer_kernel(
    capacity,
    tokens_ref, cot_ref, gain_one_ref, gain_two_ref, wq_ref, wk_ref, wv_ref, wo_ref, router_ref,
    routes_ref, fill_ref, cos_ref, sin_ref, gate_ref, up_ref, down_ref,
    output_ref, grad_tokens_ref, joint_ref, wo_grad_ref,
    ggate_ref, gup_ref, gdown_ref, gate_i, up_i, down_i,
    x, g, gate_p, up_p, down_p, hid, dgate, dup,
    in_s, in_t, in_f, out_s, out_t, out_f, in_1, in_2, out_1, out_2, gate_o, up_o, down_o,
    normed, keys, values, queries, probs, attended, branch_o, branch_i, residual, gates_s, kept_s,
    branch_grad, joint_grad, norm_i, ext_o, ext_i, ext_t, wo_part,
    j_f, j_1, j_2, w_f, w_1, w_2,
    ag_ss, ag_rs, sc_ss, sc_rs, sib_ss, sib_rs, y_ss, y_rs,
):
    place = Place()
    mine = pl.ds(pl.multiple_of(place.e * BLK, BLK), BLK)
    own = pl.ds(pl.multiple_of(place.t * BLK, BLK), BLK)
    peers = pl.ds(pl.multiple_of((1 - place.t) * BLK, BLK), BLK)
    gx = Gather(place, x, ag_ss.at[0], ag_rs.at[0])
    gg = Gather(place, g, ag_ss.at[1], ag_rs.at[1])
    gj = Gather(place, joint_ref, ag_ss.at[2], ag_rs.at[2])
    gw = Gather(place, wo_grad_ref, ag_ss.at[3], ag_rs.at[3])

    def scatter(n, *refs):
        return Scatter(place, *refs, sib_ss.at[n], sib_rs.at[n], sc_ss.at[n], sc_rs.at[n])

    si = scatter(0, in_s, in_t, in_f, in_1, in_2)
    so = scatter(1, out_s, out_t, out_f, out_1, out_2)
    narrow = lambda ref, start, size, lanes: ref.at[:, pl.ds(start, size), pl.ds(0, lanes)]
    sj = scatter(2, narrow(in_s, 0, 64, EXT), narrow(in_t, 0, 64, EXT), j_f, j_1, j_2)
    sw = scatter(3, narrow(in_s, 64, 32, WIDTH), narrow(in_t, 64, 32, WIDTH), w_f, w_1, w_2)

    def across(k):
        src, dst = {
            0: (normed.at[own], normed.at[own]),
            1: (gate_ref, gate_p),
            2: (up_ref, up_p),
            3: (down_ref, down_p),
            4: (branch_o, branch_i),
            5: (gate_o, gate_i),
            6: (up_o, up_i),
            7: (down_o, down_i),
            8: (branch_grad.at[own], branch_grad.at[own]),
            9: (ext_o, ext_i),
            10: (branch_o, norm_i),
        }[k]
        return pltpu.make_async_remote_copy(
            src_ref=src, dst_ref=dst, send_sem=y_ss.at[k], recv_sem=y_rs.at[k],
            device_id=place.across, device_id_type=MESH,
        )

    def arrived(k):
        ref = {0: normed, 8: branch_grad}.get(k)
        if ref is None:
            across(k).wait_recv()
        else:
            pltpu.make_async_remote_copy(
                src_ref=ref.at[peers], dst_ref=ref.at[peers], send_sem=y_ss.at[k],
                recv_sem=y_rs.at[k], device_id=place.across, device_id_type=MESH,
            ).wait_recv()

    g[mine, :] = cot_ref[...]
    inputs = tokens_ref[...].astype(F32)
    inv_one = lax.rsqrt(mean_last(inputs * inputs) + EPSILON)
    normed[own, :] = (inputs * inv_one * gain_one_ref[...]).astype(BF16)
    place.barrier()
    across(0).start()
    gg.stage0()
    for k in (1, 2, 3):
        across(k).start()

    lane = lax.broadcasted_iota(jnp.int32, (BLK, BLK), 1)
    row = lax.broadcasted_iota(jnp.int32, (BLK, BLK), 0)
    named = jnp.zeros((BLK, BLK), F32)
    routes = routes_ref[...]
    for j in range(routes.shape[1]):
        named = named + (routes[:, j : j + 1] == lane).astype(F32)
    place_of = (fill_ref[...] == row).astype(F32).astype(BF16)
    ordered = dot_tn(place_of, named.astype(BF16))
    earlier = (row > lane).astype(F32).astype(BF16)
    before = dot_nn(earlier, ordered.astype(BF16))
    rank = dot_nn(place_of, before.astype(BF16))
    kept = jnp.where(rank < capacity, named, 0.0)
    kept_s[...] = kept

    def project(rows):
        cos, sin = cos_ref[rows, :], sin_ref[rows, :]
        for n in range(2):
            part = dot_nn(normed[rows, :], wq_ref[:, n * 256 : (n + 1) * 256])
            for m in range(2):
                one = part[:, m * 128 : (m + 1) * 128]
                queries[rows, n * 256 + m * 128 : n * 256 + (m + 1) * 128] = (
                    one * cos + swapped(one) * sin
                ).astype(BF16)
        part = dot_nn(normed[rows, :], wk_ref[...])
        for m in range(2):
            one = part[:, m * 128 : (m + 1) * 128]
            keys[rows, m * 128 : (m + 1) * 128] = (one * cos + swapped(one) * sin).astype(BF16)
        values[rows, :] = dot_nn(normed[rows, :], wv_ref[...]).astype(BF16)

    project(own)
    arrived(0)
    project(peers)
    gg.stage1()

    scale = HEAD_DIM ** (-0.5)

    def heads_of(m, half):
        cols = pl.ds(pl.multiple_of(m * 128, 128), 128)
        key = doubled(keys[:, cols].astype(F32), half).astype(BF16)
        value = doubled(values[:, cols].astype(F32), half).astype(BF16)
        j = m * 2 + half
        wide = pl.ds(pl.multiple_of(j * 128, 128), 128)
        query = stacked(queries[:, wide].astype(F32)).astype(BF16)
        return j, wide, key, value, query

    def attend(m, carry):
        place_q = lax.rem(lax.broadcasted_iota(jnp.int32, (512, 256), 0), 256)
        place_k = lax.broadcasted_iota(jnp.int32, (512, 256), 1)
        for half in range(2):
            j, wide, key, value, query = heads_of(m, half)
            scores = jnp.where(place_q >= place_k, dot_nt(query, key) * scale, MASKED)
            raised = jnp.exp(scores - jnp.max(scores, -1, keepdims=True))
            share = raised / jnp.sum(raised, -1, keepdims=True)
            probs[j] = share
            attended[:, wide] = unstacked(dot_nn(share.astype(BF16), value)).astype(BF16)
        return carry

    lax.fori_loop(0, 2, attend, 0)
    gg.stage2()
    branch_o[...] = dot_nn(attended[peers, :], wo_ref[...]).astype(BF16)
    across(4).start()
    own_branch = dot_nn(attended[own, :], wo_ref[...])
    gg.stage3()
    across(4).wait_recv()
    resid = tokens_ref[...].astype(F32) + own_branch + branch_i[...].astype(F32)
    residual[...] = resid
    inv_two = lax.rsqrt(mean_last(resid * resid) + EPSILON)
    moe_in = (resid * inv_two * gain_two_ref[...]).astype(BF16)
    logits = dot_nn(moe_in, router_ref[...])
    is_named = named > 0.0
    top = jnp.max(jnp.where(is_named, logits, MASKED), -1, keepdims=True)
    raised = jnp.where(is_named, jnp.exp(jnp.minimum(logits - top, 0.0)), 0.0)
    gates = raised / jnp.sum(raised, -1, keepdims=True)
    gates_s[...] = gates
    weights = gates * kept
    coarse = weights.astype(BF16).astype(F32)
    x[mine, :WIDTH] = moe_in
    x[mine, WIDTH:] = (coarse + pltpu.roll(weights - coarse, 16, 1)).astype(BF16)

    gx.stage0()
    gates_w, ups_w, downs_w = (gate_ref, gate_p), (up_ref, up_p), (down_ref, down_p)

    def chip_step(i, carry):
        @pl.when(i == 0)
        def _():
            gg.from_sib()
            gx.recv(SIB + OWN)
            for k in (1, 2, 3):
                across(k).wait_recv()

        @pl.when(i == 1)
        def _():
            gx.stage1()

        @pl.when(i == 4)
        def _():
            gx.stage2()

        @pl.when(i == 5)
        def _():
            gx.stage3()

        for n in range(1, 8):

            @pl.when(i == n)
            def _(n=n):
                gx.recv(SIB + n)

        expert_step(place, i, x, g, gates_w, ups_w, downs_w, hid, dgate, dup, in_s, in_t, out_s, out_t)
        si.sib_copy(i).start()
        so.sib_copy(i).start()

        @pl.when(i >= 1)
        def _():
            si.join(i - 1)
            so.join(i - 1)

        for n in range(1, 8):

            @pl.when(i - 1 == n)
            def _(n=n):
                si.after(n)

        return carry

    lax.fori_loop(0, 8, chip_step, 0)

    def grad_step(i, carry):
        @pl.when(i == 0)
        def _():
            si.join(7)
            si.after(PAIR_FAR)
            so.join(7)

        @pl.when(i == 2)
        def _():
            si.stage1()

        @pl.when(i == 4)
        def _():
            si.stage2()
            for n in range(1, 8):
                so.after(n)

        @pl.when(i < 4)
        def _():
            cols = pl.ds(pl.multiple_of(i * 256, 256), 256)
            turned = x[:, cols].T
            both = dot_nn(turned, dgate[...])
            ggate_ref[cols, :] = both[:, :256]
            gate_o[cols, :] = both[:, 256:].astype(BF16)
            both = dot_nn(turned, dup[...])
            gup_ref[cols, :] = both[:, :256]
            up_o[cols, :] = both[:, 256:].astype(BF16)

        @pl.when(i == 4)
        def _():
            down_o[...] = dot_nn(hid[:, 256:].T, g[...]).astype(BF16)

        @pl.when(i == 5)
        def _():
            gdown_ref[...] = dot_nn(hid[:, :256].T, g[...])

        return carry

    lax.fori_loop(0, 6, grad_step, 0)

    from_experts = jnp.concatenate([si.total(1), si.total(2)], 1)
    pairs = from_experts[:, WIDTH:]
    gates = gates_s[...]
    grad_gates = (pairs + pltpu.roll(pairs, 112, 1)) * kept_s[...]
    grad_logits = (gates * (grad_gates - jnp.sum(gates * grad_gates, -1, keepdims=True))).astype(BF16)
    grad_moe_in = from_experts[:, :WIDTH] + dot_nt(grad_logits, router_ref[...])
    resid = residual[...]
    inv_two = lax.rsqrt(mean_last(resid * resid) + EPSILON)
    grad_n = grad_moe_in * gain_two_ref[...]
    grad_residual = (
        cot_ref[...].astype(F32)
        + inv_two * grad_n
        - resid * (inv_two * inv_two * inv_two * mean_last(grad_n * resid))
    )
    branch_grad[own, :] = grad_residual.astype(BF16)
    across(8).start()
    for k in (5, 6, 7):
        across(k).start()
    grad_tokens_ref[...] = grad_residual
    small = dot_tn(grad_logits, x[mine, :WIDTH])
    ext_o[0:16, :] = small[0:16, :]
    ext_o[16:17, :] = jnp.sum(grad_moe_in * resid * inv_two, 0, keepdims=True)

    def grad_attended(rows):
        joint_grad[rows, :512] = dot_nt(branch_grad[rows, :], wo_ref[...]).astype(BF16)

    grad_attended(own)
    arrived(8)
    grad_attended(peers)
    wo_part[...] = dot_tn(attended[...], branch_grad[...]).astype(BF16)

    si.sent()

    def share_out(n, carry):
        start = pl.multiple_of(place.numbered(n) * 64, 64)
        put(place, n, sw.sums, sw.theirs, slice(0, WIDTH), wo_part[pl.ds(start, 64), :])
        sw.sib_copy(n).start()
        return carry

    lax.fori_loop(0, 8, share_out, 0)
    so.stage1()

    def attend_back(m, carry):
        cols = pl.ds(pl.multiple_of(m * 128, 128), 128)
        cos, sin = cos_ref[...], sin_ref[...]
        from_values, from_keys = [], []
        for half in range(2):
            j, wide, key, value, query = heads_of(m, half)
            grad_mixed = stacked(joint_grad[:, wide].astype(F32)).astype(BF16)
            share = probs[j]
            grad_probs = dot_nt(grad_mixed, value)
            grad_scores = (
                share * (grad_probs - jnp.sum(share * grad_probs, -1, keepdims=True)) * scale
            ).astype(BF16)
            grad_query = unstacked(dot_nn(grad_scores, key))
            joint_grad[:, wide] = (grad_query * cos - swapped(grad_query) * sin).astype(BF16)
            one = dot_tn(share.astype(BF16), grad_mixed)
            from_values.append(one + pltpu.roll(one, 64, 1))
            one = dot_tn(grad_scores, query)
            from_keys.append(one + pltpu.roll(one, 64, 1))
        low_lanes = lax.broadcasted_iota(jnp.int32, (256, 128), 1) < 64
        grad_key = jnp.where(low_lanes, from_keys[0], from_keys[1])
        at_key = pl.ds(pl.multiple_of(512 + m * 128, 128), 128)
        at_value = pl.ds(pl.multiple_of(768 + m * 128, 128), 128)
        joint_grad[:, at_key] = (grad_key * cos - swapped(grad_key) * sin).astype(BF16)
        joint_grad[:, at_value] = jnp.where(low_lanes, from_values[0], from_values[1]).astype(BF16)
        return carry

    lax.fori_loop(0, 2, attend_back, 0)

    def joined(n, carry):
        sw.join(n)
        return carry

    lax.fori_loop(0, 8, joined, 0)
    for n in range(1, 8):
        sw.after(n)
    so.stage2()

    def grad_normed(rows):
        grads = joint_grad[rows, :]
        parts = []
        for n in range(4):
            at = slice(n * 256, (n + 1) * 256)
            parts.append(
                dot_nt(grads[:, :512], wq_ref[at, :])
                + dot_nt(grads[:, 512:768], wk_ref[at, :])
                + dot_nt(grads[:, 768:], wv_ref[at, :])
            )
        return jnp.concatenate(parts, 1)

    part = grad_normed(peers)
    across(4).wait_send()
    branch_o[...] = part.astype(BF16)
    across(10).start()
    gain_sum = jnp.sum(part * normed[peers, :].astype(F32), 0, keepdims=True)
    own_part = grad_normed(own)
    gain_sum = gain_sum + jnp.sum(own_part * normed[own, :].astype(F32), 0, keepdims=True)
    ext_o[17:18, :] = gain_sum / gain_one_ref[...]
    ext_o[18:24, :] = jnp.zeros((6, WIDTH), F32)
    across(9).start()
    sw.stage1()

    def share_joint(n, carry):
        cols = pl.ds(pl.multiple_of(place.numbered(n) * 128, 128), 128)
        put(place, n, sj.sums, sj.theirs, slice(0, WIDTH), dot_nn(normed[:, cols].T, joint_grad[...]))
        return carry

    lax.fori_loop(0, 8, share_joint, 0)
    across(9).wait_recv()
    ext = ext_o[...] + ext_i[...]
    ext_t[...] = jnp.concatenate([ext, jnp.zeros((104, WIDTH), F32)], 0).T

    def share_ext(n, carry):
        rows = pl.ds(pl.multiple_of(place.numbered(n) * 128, 128), 128)
        put(place, n, sj.sums, sj.theirs, slice(WIDTH, EXT), ext_t[rows, :])
        sj.sib_copy(n).start()
        return carry

    lax.fori_loop(0, 8, share_ext, 0)
    sw.stage2()

    def joined_joint(n, carry):
        sj.join(n)
        for k in range(1, 8):

            @pl.when(n == k)
            def _(k=k):
                sj.after(k)

        return carry

    lax.fori_loop(0, 8, joined_joint, 0)
    block = pl.ds(pl.multiple_of(place.e * 32, 32), 32)
    wo_grad_ref[block, :HALF] = sw.total(1).astype(BF16)
    wo_grad_ref[block, HALF:] = sw.total(2).astype(BF16)
    gw.stage0()
    sj.stage1()

    across(10).wait_recv()
    grad_n = (own_part + norm_i[...].astype(F32)) * gain_one_ref[...]
    inputs = tokens_ref[...].astype(F32)
    inv_one = lax.rsqrt(mean_last(inputs * inputs) + EPSILON)
    grad_tokens_ref[...] = (
        grad_tokens_ref[...]
        + inv_one * grad_n
        - inputs * (inv_one * inv_one * inv_one * mean_last(grad_n * inputs))
    )
    sj.stage2()
    gw.stage1()
    output_ref[:, :HALF] = (residual[:, :HALF] + so.total(1)).astype(BF16)
    output_ref[:, HALF:] = (residual[:, HALF:] + so.total(2)).astype(BF16)
    block = pl.ds(pl.multiple_of(place.e * 64, 64), 64)
    joint_ref[block, :HALF] = sj.total(1).astype(BF16)
    joint_ref[block, HALF:] = sj.total(2).astype(BF16)
    gj.stage0()
    gw.stage2()
    gj.stage1()
    gw.stage3()
    gj.stage2()
    gj.stage3()
    gj.from_sib()
    gw.from_sib()
    for k in (5, 6, 7):
        across(k).wait_recv()
    for k in (0, 1, 2, 3, 5, 6, 7, 8, 9, 10):
        across(k).wait_send()
    for tree in (gx, gg, gj, gw, so, sj, sw):
        tree.sent()


def layer_call(capacity, *operands):
    vm, dma = pltpu.VMEM, pltpu.SemaphoreType.DMA
    spec = pl.BlockSpec(memory_space=pltpu.VMEM)
    sds = jax.ShapeDtypeStruct

    def body(*refs):
        return layer_kernel(capacity, *refs)

    outs = (
        sds((BLK, WIDTH), BF16),
        sds((BLK, WIDTH), F32),
        sds((WIDTH, EXT), BF16),
        sds((HALF, WIDTH), BF16),
        sds((WIDTH, 256), F32),
        sds((WIDTH, 256), F32),
        sds((256, WIDTH), F32),
        sds((WIDTH, 256), BF16),
        sds((WIDTH, 256), BF16),
        sds((256, WIDTH), BF16),
    )
    return pl.pallas_call(
        body,
        out_shape=outs,
        in_specs=[spec] * len(operands),
        out_specs=[spec] * len(outs),
        scratch_shapes=[
            vm((2048, EXT), BF16), vm((2048, WIDTH), BF16),
            vm((WIDTH, 256), BF16), vm((WIDTH, 256), BF16), vm((256, WIDTH), BF16),
            vm((2048, 512), BF16), vm((2048, 512), BF16), vm((2048, 512), BF16),
            vm((8, BLK, EXT), BF16), vm((8, BLK, EXT), BF16), vm((8, BLK, EXT), BF16),
            vm((8, BLK, WIDTH), BF16), vm((8, BLK, WIDTH), BF16), vm((8, BLK, WIDTH), BF16),
            vm((7, BLK, HALF), BF16), vm((7, BLK, EXT - HALF), BF16),
            vm((7, BLK, HALF), BF16), vm((7, BLK, WIDTH - HALF), BF16),
            vm((WIDTH, 256), BF16), vm((WIDTH, 256), BF16), vm((256, WIDTH), BF16),
            vm((256, WIDTH), BF16), vm((256, 256), BF16), vm((256, 256), BF16), vm((256, 512), BF16),
            vm((4, 512, 256), F32), vm((256, 512), BF16),
            vm((BLK, WIDTH), BF16), vm((BLK, WIDTH), BF16), vm((BLK, WIDTH), F32),
            vm((BLK, BLK), F32), vm((BLK, BLK), F32),
            vm((256, WIDTH), BF16), vm((256, WIDTH), BF16),
            vm((BLK, WIDTH), BF16),
            vm((24, WIDTH), F32), vm((24, WIDTH), F32), vm((WIDTH, BLK), F32), vm((512, WIDTH), BF16),
            vm((8, 64, EXT), BF16), vm((7, 64, HALF), BF16), vm((7, 64, EXT - HALF), BF16),
            vm((8, 32, WIDTH), BF16), vm((7, 32, HALF), BF16), vm((7, 32, HALF), BF16),
            dma((4, 20)), dma((4, 20)), dma((4, 17)), dma((4, 17)), dma((4, 8)), dma((4, 8)),
            dma((11,)), dma((11,)),
        ],
        compiler_params=pltpu.CompilerParams(
            collective_id=1, has_side_effects=True, vmem_limit_bytes=63 * 2**20
        ),
        cost_estimate=pl.CostEstimate(flops=24 * 10**9, bytes_accessed=10**7, transcendentals=10**6),
        name="layer",
    )(*operands)


def tables(rows):
    half = HEAD_DIM // 2
    freqs = np.exp(np.arange(half, dtype=np.float32) * np.float32(-2.0 * math.log(THETA_BASE) / HEAD_DIM))
    angles = np.arange(rows, dtype=np.float32)[:, None] * freqs[None, :]
    cos, sin = np.cos(angles), np.sin(angles)
    return (
        np.concatenate([cos] * 4, 1).astype(np.float32),
        np.concatenate([-sin, sin] * 2, 1).astype(np.float32),
    )


def on_device(
    tokens,
    gain_attn,
    w_query,
    w_key,
    w_value,
    w_out,
    gain_moe,
    router,
    expert_gate,
    expert_up,
    expert_down,
    routes,
    fill_order,
    cotangent,
):
    tok_rows, width = tokens.shape
    tensor_size = lax.axis_size("tensor")
    seq_rows = tok_rows * tensor_size
    head_size = HEAD_DIM
    q_cols = w_query.shape[1]
    kv_cols = w_key.shape[1]
    q_heads = q_cols // head_size
    kv_heads = kv_cols // head_size
    q_group = q_heads // kv_heads
    score_scale = head_size ** (-0.5)
    local_experts = expert_gate.shape[0]
    expert_groups = lax.axis_size("expert")
    experts = local_experts * expert_groups
    top_k = routes.shape[1]
    capacity = (5 * tok_rows * top_k + 4 * experts - 1) // (4 * experts)
    gate_w, up_w, down_w = (expert_gate, expert_up, expert_down)
    inputs = tokens.astype(jnp.float32)
    inv_one = lax.rsqrt(jnp.mean(inputs * inputs, -1, keepdims=True) + EPSILON)
    normed = (inputs * inv_one * gain_attn).astype(jnp.bfloat16)
    normed_all = lax.all_gather(normed, "tensor", axis=0, tiled=True)
    w_joint = jnp.concatenate([w_query, w_key, w_value], 1)
    joint = jnp.dot(normed_all, w_joint, preferred_element_type=jnp.float32)
    angles = angles_of(seq_rows, head_size)
    queries = rotate(joint[:, :q_cols].reshape(seq_rows, q_heads, head_size), angles, 1.0).astype(
        jnp.bfloat16
    )
    key_rows = rotate(
        joint[:, q_cols : q_cols + kv_cols].reshape(seq_rows, kv_heads, head_size), angles, 1.0
    ).astype(jnp.bfloat16)
    value_rows = (
        joint[:, q_cols + kv_cols :].astype(jnp.bfloat16).reshape(seq_rows, kv_heads, head_size)
    )
    q_size = min(512, seq_rows)
    blocks = seq_rows // q_size
    key_pos = jnp.arange(seq_rows)

    def scores_of(q_block, row_start):
        grouped = q_block.reshape(q_size, kv_heads, q_group, head_size)
        raw_scores = (
            jnp.einsum("qkgd,tkd->kgqt", grouped, key_rows, preferred_element_type=jnp.float32)
            * score_scale
        )
        allowed = (row_start + jnp.arange(q_size))[:, None] >= key_pos[None, :]
        return (grouped, jnp.where(allowed, raw_scores, MASKED))

    def forward_block(block_args):
        q_block, row_start = block_args
        grouped, scores = scores_of(q_block, row_start)
        top_score = jnp.max(scores, -1, keepdims=True)
        exp_scores = jnp.exp(scores - top_score)
        row_total = jnp.sum(exp_scores, -1, keepdims=True)
        attn_probs = (exp_scores / row_total).astype(jnp.bfloat16)
        mixed_rows = jnp.einsum(
            "kgqt,tkd->qkgd", attn_probs, value_rows, preferred_element_type=jnp.float32
        )
        return (mixed_rows.astype(jnp.bfloat16).reshape(q_size, q_cols), top_score, row_total)

    q_blocks = queries.reshape(blocks, q_size, q_heads, head_size)
    starts = jnp.arange(blocks) * q_size
    attended, maxima, totals = lax.map(forward_block, (q_blocks, starts))
    attended = attended.reshape(seq_rows, q_cols)
    row_block = attended
    branch = lax.psum_scatter(
        jnp.dot(row_block, w_out, preferred_element_type=jnp.float32),
        "tensor",
        scatter_dimension=0,
        tiled=True,
    )
    residual = inputs + branch
    inv_two = lax.rsqrt(jnp.mean(residual * residual, -1, keepdims=True) + EPSILON)
    scaled = residual * inv_two
    moe_in = (scaled * gain_moe).astype(jnp.bfloat16)
    logits = jnp.dot(moe_in, router, preferred_element_type=jnp.float32)
    expert_ids = jnp.arange(experts, dtype=jnp.int32)
    named = jnp.sum((routes[:, :, None] == expert_ids[None, None, :]).astype(jnp.float32), 1)
    place_of = (fill_order[0][:, None] == jnp.arange(tok_rows)[None, :]).astype(jnp.bfloat16)
    ordered = jnp.dot(place_of, named.astype(jnp.bfloat16), preferred_element_type=jnp.float32)
    earlier = (jnp.arange(tok_rows)[:, None] > jnp.arange(tok_rows)[None, :]).astype(jnp.bfloat16)
    before = jnp.dot(earlier, ordered.astype(jnp.bfloat16), preferred_element_type=jnp.float32)
    rank = contract_first(place_of, before.astype(jnp.bfloat16))
    kept = named * (rank < capacity).astype(jnp.float32)
    top_logit = jnp.max(jnp.where(named > 0, logits, MASKED), -1, keepdims=True)
    exp_logits = jnp.where(named > 0, jnp.exp(jnp.minimum(logits - top_logit, 0.0)), 0.0)
    gates = exp_logits / jnp.sum(exp_logits, -1, keepdims=True)
    weights = gates * kept

    gate_all = lax.all_gather(gate_w[0], "tensor", axis=1, tiled=True)
    up_all = lax.all_gather(up_w[0], "tensor", axis=1, tiled=True)
    down_all = lax.all_gather(down_w[0], "tensor", axis=0, tiled=True)
    grad_out = cotangent.astype(jnp.float32)
    plane_cot = lax.all_gather(cotangent, "expert", axis=0, tiled=True)
    plane_in = lax.all_gather(moe_in, "expert", axis=0, tiled=True)
    plane_weights = lax.all_gather(weights, "expert", axis=0, tiled=True)
    mine = (expert_ids == lax.axis_index("expert")).astype(jnp.float32)
    my_weight = jnp.sum(plane_weights * mine[None, :], -1, keepdims=True)

    gate_pre = jnp.dot(plane_in, gate_all, preferred_element_type=jnp.float32)
    up_pre = jnp.dot(plane_in, up_all, preferred_element_type=jnp.float32)
    back_down = contract_last(plane_cot, down_all)
    gate_sigmoid = jax.nn.sigmoid(gate_pre)
    active = gate_pre * gate_sigmoid
    hidden = active * up_pre
    pair_grad = jnp.sum(hidden * back_down, -1, keepdims=True)
    hidden_w = (hidden * my_weight).astype(jnp.bfloat16)
    grad_hidden = back_down * my_weight
    grad_gate_pre = (
        grad_hidden * up_pre * gate_sigmoid * (1.0 + gate_pre * (1.0 - gate_sigmoid))
    ).astype(jnp.bfloat16)
    grad_up_pre = (grad_hidden * active).astype(jnp.bfloat16)
    out_part = jnp.dot(hidden_w, down_all, preferred_element_type=jnp.float32)
    in_part = contract_last(grad_gate_pre, gate_all) + contract_last(grad_up_pre, up_all)
    out_sum = lax.psum_scatter(
        out_part.astype(jnp.bfloat16), "expert", scatter_dimension=0, tiled=True
    )
    in_sum = lax.psum_scatter(
        in_part.astype(jnp.bfloat16), "expert", scatter_dimension=0, tiled=True
    )
    grad_gates = lax.psum_scatter(
        pair_grad * mine[None, :], "expert", scatter_dimension=0, tiled=True
    ) * kept
    grad_down = lax.psum_scatter(
        contract_first(hidden_w, plane_cot).astype(jnp.bfloat16),
        "tensor", scatter_dimension=0, tiled=True,
    ).astype(jnp.float32)[None]
    grad_gate = lax.psum_scatter(
        contract_first(plane_in, grad_gate_pre).astype(jnp.bfloat16),
        "tensor", scatter_dimension=1, tiled=True,
    ).astype(jnp.float32)[None]
    grad_up = lax.psum_scatter(
        contract_first(plane_in, grad_up_pre).astype(jnp.bfloat16),
        "tensor", scatter_dimension=1, tiled=True,
    ).astype(jnp.float32)[None]
    output_rows = residual + out_sum.astype(jnp.float32)
    grad_logits = (
        gates * (grad_gates - jnp.sum(gates * grad_gates, -1, keepdims=True))
    ).astype(jnp.bfloat16)
    grad_moe_in = in_sum.astype(jnp.float32) + contract_last(grad_logits, router)
    grad_router = contract_first(moe_in, grad_logits)
    grad_gain_moe = jnp.sum(grad_moe_in * scaled, 0)
    grad_norm_two = grad_moe_in * gain_moe
    grad_residual = (
        grad_out
        + inv_two * grad_norm_two
        - residual * inv_two**3 * jnp.mean(grad_norm_two * residual, -1, keepdims=True)
    )
    grad_branch = grad_residual.astype(jnp.bfloat16)
    shard_piece = lax.all_gather(grad_branch, "tensor", axis=0, tiled=True)
    grad_part = contract_last(shard_piece, w_out).astype(jnp.bfloat16)
    grad_mixed = grad_part
    grad_wout = contract_first(attended, shard_piece)
    grad_mixed, grad_w_out = (grad_mixed, grad_wout)
    grad_blocks = grad_mixed.reshape(blocks, q_size, q_heads, head_size)

    def backward_block(carry, block_args):
        grad_keys, grad_values = carry
        q_block, grad_block, row_start, top_score, row_total = block_args
        grouped, scores = scores_of(q_block, row_start)
        attn_probs = jnp.exp(scores - top_score) / row_total
        grad_grouped = grad_block.reshape(q_size, kv_heads, q_group, head_size)
        grad_probs = jnp.einsum(
            "qkgd,tkd->kgqt", grad_grouped, value_rows, preferred_element_type=jnp.float32
        )
        grad_values = grad_values + jnp.einsum(
            "kgqt,qkgd->tkd",
            attn_probs.astype(jnp.bfloat16),
            grad_grouped,
            preferred_element_type=jnp.float32,
        )
        grad_scores = (
            attn_probs
            * (grad_probs - jnp.sum(attn_probs * grad_probs, -1, keepdims=True))
            * score_scale
        ).astype(jnp.bfloat16)
        grad_query = jnp.einsum(
            "kgqt,tkd->qkgd", grad_scores, key_rows, preferred_element_type=jnp.float32
        ).reshape(q_size, q_heads, head_size)
        grad_keys = grad_keys + jnp.einsum(
            "kgqt,qkgd->tkd", grad_scores, grouped, preferred_element_type=jnp.float32
        )
        return ((grad_keys, grad_values), grad_query)

    zero_rows = jnp.zeros((seq_rows, kv_heads, head_size), jnp.float32)
    (grad_keys, grad_values), grad_queries = lax.scan(
        backward_block, (zero_rows, zero_rows), (q_blocks, grad_blocks, starts, maxima, totals)
    )
    grad_queries = grad_queries.reshape(seq_rows, q_heads, head_size)
    grad_q = rotate(grad_queries, angles, -1.0).astype(jnp.bfloat16).reshape(seq_rows, q_cols)
    grad_k = rotate(grad_keys, angles, -1.0).astype(jnp.bfloat16).reshape(seq_rows, kv_cols)
    grad_v = grad_values.astype(jnp.bfloat16).reshape(seq_rows, kv_cols)
    grad_joint = jnp.concatenate([grad_q, grad_k, grad_v], 1)
    grad_w_joint = contract_first(normed_all, grad_joint)
    row_block = grad_joint
    grad_normed = lax.psum_scatter(
        contract_last(row_block, w_joint), "tensor", scatter_dimension=0, tiled=True
    )
    grad_gain_attn = jnp.sum(grad_normed * inputs * inv_one, 0)
    grad_norm_one = grad_normed * gain_attn
    grad_tokens = (
        grad_residual
        + inv_one * grad_norm_one
        - inputs * inv_one**3 * jnp.mean(grad_norm_one * inputs, -1, keepdims=True)
    )
    summed_joint, summed_out = lax.psum((grad_w_joint, grad_w_out), "expert")
    summed_gain_attn, summed_gain_moe, summed_router = lax.psum(
        (grad_gain_attn, grad_gain_moe, grad_router), ("expert", "tensor")
    )
    return (
        output_rows.astype(jnp.bfloat16),
        grad_tokens,
        summed_gain_attn,
        summed_joint[:, :q_cols],
        summed_joint[:, q_cols : q_cols + kv_cols],
        summed_joint[:, q_cols + kv_cols :],
        summed_out,
        summed_gain_moe,
        summed_router,
        grad_gate,
        grad_up,
        grad_down,
    )


def by_kernel(
    tokens,
    gain_attn,
    w_query,
    w_key,
    w_value,
    w_out,
    gain_moe,
    router,
    expert_gate,
    expert_up,
    expert_down,
    routes,
    fill_order,
    cotangent,
):
    tok_rows = tokens.shape[0]
    experts = router.shape[1]
    capacity = (5 * tok_rows * routes.shape[1] + 4 * experts - 1) // (4 * experts)
    cos, sin = tables(tok_rows * 2)
    wide_router = jnp.pad(router, ((0, 0), (0, BLK - experts)))
    out, grad_tokens, joint, wo_grad, ggate, gup, gdown, gate_i, up_i, down_i = layer_call(
        capacity,
        tokens, cotangent, gain_attn[None], gain_moe[None], w_query, w_key, w_value, w_out,
        wide_router, routes, fill_order, jnp.asarray(cos), jnp.asarray(sin),
        expert_gate[0], expert_up[0], expert_down[0],
    )
    small = joint[:, WIDTH:].astype(F32)
    return (
        out,
        grad_tokens,
        small[:, experts + 1],
        joint[:, :512].astype(F32),
        joint[:, 512:768].astype(F32),
        joint[:, 768:WIDTH].astype(F32),
        wo_grad.astype(F32),
        small[:, experts],
        small[:, :experts],
        (ggate + gate_i.astype(F32))[None],
        (gup + up_i.astype(F32))[None],
        (gdown + down_i.astype(F32))[None],
    )


def kernel_fits(mesh_shape, shapes):
    return mesh_shape == (16, 2) and shapes == (
        (128, 1024), (1024,), (1024, 512), (1024, 256), (1024, 256), (512, 1024), (1024,), (1024, 16),
        (1, 1024, 256), (1, 1024, 256), (1, 256, 1024), (128, 8), (1, 128), (128, 1024),
    )


def on_any(*operands):
    sizes = (lax.axis_size("expert"), lax.axis_size("tensor"))
    if kernel_fits(sizes, tuple(a.shape for a in operands)):
        return by_kernel(*operands)
    return on_device(*operands)


def solution(mesh):
    placed = (
        P(("expert", "tensor"), None),
        P(),
        P(None, "tensor"),
        P(None, "tensor"),
        P(None, "tensor"),
        P("tensor", None),
        P(),
        P(),
        P("expert", None, "tensor"),
        P("expert", None, "tensor"),
        P("expert", "tensor", None),
        P(("expert", "tensor"), None),
        P(("expert", "tensor"), None),
        P(("expert", "tensor"), None),
    )
    return jax.shard_map(
        on_any,
        mesh=mesh,
        in_specs=placed,
        out_specs=(
            P(("expert", "tensor"), None),
            P(("expert", "tensor"), None),
            P(),
            P(None, "tensor"),
            P(None, "tensor"),
            P(None, "tensor"),
            P("tensor", None),
            P(),
            P(),
            P("expert", None, "tensor"),
            P("expert", None, "tensor"),
            P("expert", "tensor", None),
        ),
        check_vma=False,
    )
```

```python
import math

import jax
import jax.numpy as jnp
import numpy as np
from jax import lax
from jax.experimental import pallas as pl
from jax.experimental.pallas import tpu as pltpu
from jax.sharding import PartitionSpec as P

HEAD_DIM = 64


EPSILON = 1e-06
THETA_BASE = 10000.0
MASKED = -1e30


def angles_of(row_count, head_size):
    half = head_size // 2
    freqs = jnp.exp(jnp.arange(half, dtype=jnp.float32) * (-2.0 * math.log(THETA_BASE) / head_size))
    return jnp.arange(row_count, dtype=jnp.float32)[:, None] * freqs[None, :]


def rotate(vectors, angles, sign):
    half = vectors.shape[-1] // 2
    cosine = jnp.cos(angles)[:, None, :]
    sine = sign * jnp.sin(angles)[:, None, :]
    first = vectors[..., :half]
    second = vectors[..., half:]
    return jnp.concatenate([first * cosine - second * sine, second * cosine + first * sine], -1)


def contract_last(left, right):
    return lax.dot_general(
        left, right, (((1,), (1,)), ((), ())), preferred_element_type=jnp.float32
    )


def contract_first(left, right):
    return lax.dot_general(
        left, right, (((0,), (0,)), ((), ())), preferred_element_type=jnp.float32
    )


F32 = jnp.float32
BF16 = jnp.bfloat16
MESH = pl.DeviceIdType.MESH
BLK = 128
WIDTH = 1024
EXT = 1152
HALF = 512
NEAREST = (0, 1, 2, 3, 1, 0, 2, 3, 2, 3, 1, 0, 3, 2, 1, 0)
EXPERT_ORDER = ((2, 1), (2, 0), (1, 0), (3, 1), (3, 0), (1, 1), (0, 1), (0, 0))
PAIR_FIRST = ((2, 1), (3, 1), (1, 1), (0, 1), (2, 0), (3, 0), (1, 0), (0, 0))


def pick(i, values):
    out = jnp.int32(values[-1])
    for n in range(len(values) - 2, -1, -1):
        out = jnp.where(i == n, jnp.int32(values[n]), out)
    return out


class Place:
    def __init__(self):
        e = lax.axis_index("expert")
        t = lax.axis_index("tensor")
        self.e = e
        self.t = t
        self.core = lax.rem(e, 2)
        self.pair = lax.rem(e // 2, 2)
        self.ring = e // 4
        self.other = (e + 2 - 4 * self.pair, t)
        self.sib = (e + 1 - 2 * self.core, t)
        self.across = (e, 1 - t)

    def at(self, ring):
        return (ring * 4 + lax.rem(self.e, 4), self.t)

    def chip(self, ring, other):
        return ring * 2 + (self.pair + other - 2 * self.pair * other)

    def step(self, i, order):
        ring = self.near(pick(i, [k for k, _ in order]))
        return ring, pick(i, [other for _, other in order])

    def near(self, k):
        return pick(self.ring * 4 + k, NEAREST)

    def barrier(self):
        bar = pltpu.get_barrier_semaphore()
        for dest in [self.at(lax.rem(self.ring + m, 4)) for m in (1, 2, 3)] + [
            self.other, self.sib, self.across,
        ]:
            pl.semaphore_signal(bar, inc=1, device_id=dest, device_id_type=MESH)
        pl.semaphore_wait(bar, 6)


def if_(condition, action):
    if condition is True:
        action()
    else:
        pl.when(condition)(action)


class Gather:
    def __init__(self, place, buf, send_sems, recv_sems):
        self.place, self.buf, self.ss, self.rs = place, buf, send_sems, recv_sems
        self.size = buf.shape[0] // 16

    def where(self, n):
        r = self.place.ring
        if n == 0:
            return r, True
        j = (n - 1) // 2
        return (r - 1 - j, r > j) if n % 2 else (r + 1 + j, 3 - r > j)

    def copy(self, ring, other, core, sem, dest):
        block = self.place.chip(ring, other) * 2 + core
        ref = self.buf.at[pl.ds(pl.multiple_of(block * self.size, self.size), self.size)]
        return pltpu.make_async_remote_copy(
            src_ref=ref, dst_ref=ref, send_sem=self.ss.at[sem], recv_sem=self.rs.at[sem],
            device_id=dest, device_id_type=MESH,
        )

    def up(self, k):
        r = self.place.ring
        return self.copy(r - k, 0, self.place.core, k, self.place.at(r + 1))

    def down(self, k):
        r = self.place.ring
        return self.copy(r + k, 0, self.place.core, 3 + k, self.place.at(r - 1))

    def over(self, n, arriving=0):
        return self.copy(self.where(n)[0], arriving, self.place.core, 6 + n, self.place.other)

    def to_sib(self, n, other, arriving=False):
        core = 1 - self.place.core if arriving else self.place.core
        return self.copy(self.where(n)[0], other, core, 13 + 7 * other + n, self.place.sib)

    def start(self):
        r = self.place.ring
        if_(r < 3, lambda: self.up(0).start())
        if_(r > 0, lambda: self.down(0).start())
        self.over(0).start()
        self.to_sib(0, 0).start()

    def arrive(self, j):
        r = self.place.ring

        def from_below():
            self.copy(r - 1 - j, 0, self.place.core, j, self.place.other).wait_recv()
            if j < 2:
                if_(r < 3, lambda: self.up(j + 1).start())
            self.over(1 + 2 * j).start()
            self.to_sib(1 + 2 * j, 0).start()

        def from_above():
            self.copy(r + 1 + j, 0, self.place.core, 3 + j, self.place.other).wait_recv()
            if j < 2:
                if_(r > 0, lambda: self.down(j + 1).start())
            self.over(2 + 2 * j).start()
            self.to_sib(2 + 2 * j, 0).start()

        if_(r > j, from_below)
        if_(3 - r > j, from_above)

    def arrive_over(self, *numbers):
        for n in numbers:

            def taken(n=n):
                self.over(n, 1).wait_recv()
                self.to_sib(n, 1).start()

            if_(self.where(n)[1], taken)

    def from_sib(self, other, *numbers):
        for n in numbers:
            if_(self.where(n)[1], lambda n=n: self.to_sib(n, other, True).wait_recv())

    def sent(self):
        r = self.place.ring
        for k in range(3):
            if_((r < 3) & (r >= k), lambda k=k: self.up(k).wait_send())
            if_((r > 0) & (3 - r >= k), lambda k=k: self.down(k).wait_send())
        for n in range(7):

            def all_of(n=n):
                self.over(n).wait_send()
                self.to_sib(n, 0).wait_send()
                self.to_sib(n, 1).wait_send()

            if_(self.where(n)[1], all_of)


class Scatter:
    def __init__(self, place, sums, theirs, from_sib, over, along, sib_ss, sib_rs, ss, rs):
        self.place, self.sums, self.theirs, self.from_sib = place, sums, theirs, from_sib
        self.over, self.along = over, along
        self.sib_ss, self.sib_rs, self.ss, self.rs = sib_ss, sib_rs, ss, rs

    def sib_copy(self, i):
        return pltpu.make_async_remote_copy(
            src_ref=self.theirs.at[i], dst_ref=self.from_sib.at[i],
            send_sem=self.sib_ss.at[i], recv_sem=self.sib_rs.at[i],
            device_id=self.place.sib, device_id_type=MESH,
        )

    def join(self, i):
        self.sib_copy(i).wait_recv()
        self.sums[i] = (self.sums[i].astype(F32) + self.from_sib[i].astype(F32)).astype(BF16)

    def over_copy(self, ring):
        return pltpu.make_async_remote_copy(
            src_ref=self.sums.at[4 + ring], dst_ref=self.over.at[ring],
            send_sem=self.ss.at[ring], recv_sem=self.rs.at[ring],
            device_id=self.place.other, device_id_type=MESH,
        )

    def along_copy(self, ring):
        m = lax.rem(self.place.ring - ring + 4, 4)
        return pltpu.make_async_remote_copy(
            src_ref=self.sums.at[ring], dst_ref=self.along.at[m - 1],
            send_sem=self.ss.at[3 + m], recv_sem=self.rs.at[3 + m],
            device_id=self.place.at(ring), device_id_type=MESH,
        )

    def relay(self, *ks):
        for k in ks:
            ring = self.place.near(k)
            self.over_copy(ring).wait_recv()
            self.sums[ring] = (
                self.sums[ring].astype(F32) + self.over[ring].astype(F32)
            ).astype(BF16)
            self.along_copy(ring).start()

    def total(self):
        ring = self.place.ring
        self.over_copy(ring).wait_recv()
        for m in (1, 2, 3):
            pltpu.make_async_remote_copy(
                src_ref=self.sums.at[ring], dst_ref=self.along.at[m - 1],
                send_sem=self.ss.at[3 + m], recv_sem=self.rs.at[3 + m],
                device_id=self.place.other, device_id_type=MESH,
            ).wait_recv()
        return (
            (self.sums[ring].astype(F32) + self.over[ring].astype(F32))
            + (self.along[0].astype(F32) + self.along[1].astype(F32))
            + self.along[2].astype(F32)
        )

    def sib_sent(self):
        for i in range(8):
            self.sib_copy(i).wait_send()

    def sent(self):
        for ring in range(4):
            self.over_copy(ring).wait_send()
        for k in (1, 2, 3):
            self.along_copy(self.place.near(k)).wait_send()


def dot_nn(a, b):
    return lax.dot_general(a, b, (((1,), (0,)), ((), ())), preferred_element_type=F32)


def dot_nt(a, b):
    return lax.dot_general(a, b, (((1,), (1,)), ((), ())), preferred_element_type=F32)


def dot_tn(a, b):
    return lax.dot_general(a, b, (((0,), (0,)), ((), ())), preferred_element_type=F32)


def expert_step(place, ring, other, x, g, gates_w, ups_w, downs_w, hid, dgate, dup, in_s, in_t, out_s, out_t):
    i = other * 4 + ring
    rows = pl.ds(pl.multiple_of(place.chip(ring, other) * 256, 256), 256)
    lane = lax.broadcasted_iota(jnp.int32, (256, 128), 1)
    high, low = lane == place.e, lane == place.e + 16
    weight = jnp.sum(
        jnp.where(high | low, x[rows, WIDTH:EXT].astype(F32), 0.0), -1, keepdims=True
    )
    pair_grad = jnp.zeros((256, 1), F32)
    for h in range(2):
        cols = slice(h * 256, (h + 1) * 256)
        gate_pre = dot_nn(x[rows, :WIDTH], gates_w[h][...])
        up_pre = dot_nn(x[rows, :WIDTH], ups_w[h][...])
        back = dot_nt(g[rows, :], downs_w[h][...])
        sig = jax.nn.sigmoid(gate_pre)
        act = gate_pre * sig
        hidden = act * up_pre
        pair_grad = pair_grad + jnp.sum(hidden * back, -1, keepdims=True)
        grad_hidden = back * weight
        hid[rows, cols] = (hidden * weight).astype(BF16)
        dgate[rows, cols] = (grad_hidden * up_pre * (sig + act * (1.0 - sig))).astype(BF16)
        dup[rows, cols] = (grad_hidden * act).astype(BF16)
    coarse = pair_grad.astype(BF16).astype(F32)
    ext = jnp.where(high, coarse, jnp.where(low, pair_grad - coarse, 0.0))
    put(place, i, in_s, in_t, slice(WIDTH, EXT), ext)
    for n in range(4):
        cols = slice(n * 256, (n + 1) * 256)
        value = (
            dot_nt(dgate[rows, 0:256], gates_w[0][cols, :])
            + dot_nt(dgate[rows, 256:512], gates_w[1][cols, :])
            + dot_nt(dup[rows, 0:256], ups_w[0][cols, :])
            + dot_nt(dup[rows, 256:512], ups_w[1][cols, :])
        )
        put(place, i, in_s, in_t, cols, value)
    for n in range(4):
        cols = slice(n * 256, (n + 1) * 256)
        value = dot_nn(hid[rows, 0:256], downs_w[0][:, cols]) + dot_nn(
            hid[rows, 256:512], downs_w[1][:, cols]
        )
        put(place, i, out_s, out_t, cols, value)


def put(place, i, ours, theirs, cols, value):
    half = value.shape[0] // 2
    first, second = value[:half], value[half:]
    is_first = place.core == 0
    ours[i, :, cols] = jnp.where(is_first, first, second).astype(BF16)
    theirs[i, :, cols] = jnp.where(is_first, second, first).astype(BF16)


def mean_last(v):
    return jnp.sum(v, -1, keepdims=True) * (1.0 / v.shape[-1])


def swapped(v):
    lane = lax.broadcasted_iota(jnp.int32, v.shape, 1)
    return jnp.where(lax.rem(lane, 64) < 32, pltpu.roll(v, 96, 1), pltpu.roll(v, 32, 1))


def doubled(v, half):
    lane = lax.broadcasted_iota(jnp.int32, v.shape, 1)
    one = jnp.where((lane < 64) == (half == 0), v, 0.0)
    return one + pltpu.roll(one, 64, 1)


def stacked(v):
    lane = lax.broadcasted_iota(jnp.int32, v.shape, 1)
    return jnp.concatenate([jnp.where(lane < 64, v, 0.0), jnp.where(lane < 64, 0.0, v)], 0)


def unstacked(v):
    rows = v.shape[0] // 2
    lane = lax.broadcasted_iota(jnp.int32, (rows, 128), 1)
    return jnp.where(lane < 64, v[:rows], v[rows:])


def layer_kernel(
    capacity,
    tokens_ref, cot_ref, gain_one_ref, gain_two_ref, wq_ref, wk_ref, wv_ref, wo_ref, router_ref,
    routes_ref, fill_ref, cos_ref, sin_ref, gate_ref, up_ref, down_ref,
    output_ref, grad_tokens_ref, joint_ref, wo_grad_ref,
    ggate_ref, gup_ref, gdown_ref, gate_i, up_i, down_i,
    x, g, gate_p, up_p, down_p, hid, dgate, dup,
    in_s, in_t, in_f, out_s, out_t, out_f, in_1, in_2, out_1, out_2, gate_o, up_o, down_o,
    normed, keys, values, queries, probs, attended, branch_o, branch_i, residual, gates_s, kept_s,
    branch_grad, joint_grad, norm_i, ext_o, ext_i, ext_t, wo_part,
    j_f, j_1, j_2, w_f, w_1, w_2,
    ag_ss, ag_rs, sc_ss, sc_rs, sib_ss, sib_rs, y_ss, y_rs,
):
    place = Place()
    mine = pl.ds(pl.multiple_of(place.e * BLK, BLK), BLK)
    own = pl.ds(pl.multiple_of(place.t * BLK, BLK), BLK)
    peers = pl.ds(pl.multiple_of((1 - place.t) * BLK, BLK), BLK)
    gx = Gather(place, x, ag_ss.at[0], ag_rs.at[0])
    gg = Gather(place, g, ag_ss.at[1], ag_rs.at[1])
    gj = Gather(place, joint_ref, ag_ss.at[2], ag_rs.at[2])
    gw = Gather(place, wo_grad_ref, ag_ss.at[3], ag_rs.at[3])

    def scatter(n, *refs):
        return Scatter(place, *refs, sib_ss.at[n], sib_rs.at[n], sc_ss.at[n], sc_rs.at[n])

    si = scatter(0, in_s, in_t, in_f, in_1, in_2)
    so = scatter(1, out_s, out_t, out_f, out_1, out_2)
    narrow = lambda ref, start, size, lanes: ref.at[:, pl.ds(start, size), pl.ds(0, lanes)]
    sj = scatter(2, narrow(in_s, 0, 64, EXT), narrow(in_t, 0, 64, EXT), j_f, j_1, j_2)
    sw = scatter(3, narrow(in_s, 64, 32, WIDTH), narrow(in_t, 64, 32, WIDTH), w_f, w_1, w_2)

    def across(k):
        src, dst = {
            0: (normed.at[own], normed.at[own]),
            1: (gate_ref, gate_p),
            2: (up_ref, up_p),
            3: (down_ref, down_p),
            4: (branch_o, branch_i),
            5: (gate_o, gate_i),
            6: (up_o, up_i),
            7: (down_o, down_i),
            8: (branch_grad.at[own], branch_grad.at[own]),
            9: (ext_o, ext_i),
            10: (branch_o, norm_i),
        }[k]
        return pltpu.make_async_remote_copy(
            src_ref=src, dst_ref=dst, send_sem=y_ss.at[k], recv_sem=y_rs.at[k],
            device_id=place.across, device_id_type=MESH,
        )

    def arrived(k):
        ref = {0: normed, 8: branch_grad}.get(k)
        if ref is None:
            across(k).wait_recv()
        else:
            pltpu.make_async_remote_copy(
                src_ref=ref.at[peers], dst_ref=ref.at[peers], send_sem=y_ss.at[k],
                recv_sem=y_rs.at[k], device_id=place.across, device_id_type=MESH,
            ).wait_recv()

    g[mine, :] = cot_ref[...]
    inputs = tokens_ref[...].astype(F32)
    inv_one = lax.rsqrt(mean_last(inputs * inputs) + EPSILON)
    normed[own, :] = (inputs * inv_one * gain_one_ref[...]).astype(BF16)
    place.barrier()
    across(0).start()
    gg.start()

    lane = lax.broadcasted_iota(jnp.int32, (BLK, BLK), 1)
    row = lax.broadcasted_iota(jnp.int32, (BLK, BLK), 0)
    named = jnp.zeros((BLK, BLK), F32)
    routes = routes_ref[...]
    for j in range(routes.shape[1]):
        named = named + (routes[:, j : j + 1] == lane).astype(F32)
    place_of = (fill_ref[...] == row).astype(F32).astype(BF16)
    ordered = dot_tn(place_of, named.astype(BF16))
    earlier = (row > lane).astype(F32).astype(BF16)
    before = dot_nn(earlier, ordered.astype(BF16))
    rank = dot_nn(place_of, before.astype(BF16))
    kept = jnp.where(rank < capacity, named, 0.0)
    kept_s[...] = kept

    def project(rows):
        cos, sin = cos_ref[rows, :], sin_ref[rows, :]
        for n in range(2):
            part = dot_nn(normed[rows, :], wq_ref[:, n * 256 : (n + 1) * 256])
            for m in range(2):
                one = part[:, m * 128 : (m + 1) * 128]
                queries[rows, n * 256 + m * 128 : n * 256 + (m + 1) * 128] = (
                    one * cos + swapped(one) * sin
                ).astype(BF16)
        part = dot_nn(normed[rows, :], wk_ref[...])
        for m in range(2):
            one = part[:, m * 128 : (m + 1) * 128]
            keys[rows, m * 128 : (m + 1) * 128] = (one * cos + swapped(one) * sin).astype(BF16)
        values[rows, :] = dot_nn(normed[rows, :], wv_ref[...]).astype(BF16)

    project(own)
    arrived(0)
    across(1).start()
    project(peers)
    gg.arrive(0)
    gg.arrive_over(0)

    scale = HEAD_DIM ** (-0.5)

    def heads_of(m, half):
        cols = pl.ds(pl.multiple_of(m * 128, 128), 128)
        key = doubled(keys[:, cols].astype(F32), half).astype(BF16)
        value = doubled(values[:, cols].astype(F32), half).astype(BF16)
        j = m * 2 + half
        wide = pl.ds(pl.multiple_of(j * 128, 128), 128)
        query = stacked(queries[:, wide].astype(F32)).astype(BF16)
        return j, wide, key, value, query

    def attend(m, carry):
        place_q = lax.rem(lax.broadcasted_iota(jnp.int32, (512, 256), 0), 256)
        place_k = lax.broadcasted_iota(jnp.int32, (512, 256), 1)
        for half in range(2):
            j, wide, key, value, query = heads_of(m, half)
            scores = jnp.where(place_q >= place_k, dot_nt(query, key) * scale, MASKED)
            raised = jnp.exp(scores - jnp.max(scores, -1, keepdims=True))
            share = raised / jnp.sum(raised, -1, keepdims=True)
            probs[j] = share
            attended[:, wide] = unstacked(dot_nn(share.astype(BF16), value)).astype(BF16)
        return carry

    lax.fori_loop(0, 2, attend, 0)
    gg.arrive(1)
    gg.arrive_over(1, 2)
    branch_o[...] = dot_nn(attended[peers, :], wo_ref[...]).astype(BF16)
    across(4).start()
    own_branch = dot_nn(attended[own, :], wo_ref[...])
    gg.arrive(2)
    gg.arrive_over(3, 4)
    across(4).wait_recv()
    across(2).start()
    across(3).start()
    resid = tokens_ref[...].astype(F32) + own_branch + branch_i[...].astype(F32)
    residual[...] = resid
    inv_two = lax.rsqrt(mean_last(resid * resid) + EPSILON)
    moe_in = (resid * inv_two * gain_two_ref[...]).astype(BF16)
    logits = dot_nn(moe_in, router_ref[...])
    is_named = named > 0.0
    top = jnp.max(jnp.where(is_named, logits, MASKED), -1, keepdims=True)
    raised = jnp.where(is_named, jnp.exp(jnp.minimum(logits - top, 0.0)), 0.0)
    gates = raised / jnp.sum(raised, -1, keepdims=True)
    gates_s[...] = gates
    weights = gates * kept
    coarse = weights.astype(BF16).astype(F32)
    x[mine, :WIDTH] = moe_in
    x[mine, WIDTH:] = (coarse + pltpu.roll(weights - coarse, 16, 1)).astype(BF16)

    gx.start()
    gg.arrive_over(5, 6)
    gates_w, ups_w, downs_w = (gate_ref, gate_p), (up_ref, up_p), (down_ref, down_p)
    gx.arrive(0)
    gx.arrive_over(0)
    gx.arrive(1)
    gx.arrive_over(1, 2)
    gx.arrive(2)
    gx.arrive_over(3, 4)
    gg.from_sib(0, *range(7))
    gg.from_sib(1, *range(7))
    gx.from_sib(0, *range(7))
    gx.from_sib(1, *range(5))
    for k in (1, 2, 3):
        across(k).wait_recv()

    def joined(i):
        ring, other = place.step(i, EXPERT_ORDER)
        si.join(other * 4 + ring)
        so.join(other * 4 + ring)

        @pl.when(other == 1)
        def _():
            si.over_copy(ring).start()

    def chip_step(i, carry):
        @pl.when(i == 3)
        def _():
            gx.arrive_over(5, 6)
            gx.from_sib(1, 5, 6)

        ring, other = place.step(i, EXPERT_ORDER)
        expert_step(
            place, ring, other, x, g, gates_w, ups_w, downs_w, hid, dgate, dup, in_s, in_t, out_s, out_t
        )
        si.sib_copy(other * 4 + ring).start()
        so.sib_copy(other * 4 + ring).start()

        @pl.when(i >= 1)
        def _():
            joined(i - 1)

        return carry

    lax.fori_loop(0, 8, chip_step, 0)

    def grad_step(i, carry):
        @pl.when(i == 0)
        def _():
            joined(jnp.int32(7))

        @pl.when(i == 1)
        def _():
            si.relay(2)

        @pl.when(i == 3)
        def _():
            si.relay(3)

        @pl.when(i == 5)
        def _():
            si.relay(1)

        @pl.when((i >= 2))
        def _():
            cols = pl.ds(pl.multiple_of((i - 2) * 256, 256), 256)
            turned = x[:, cols].T
            both = dot_nn(turned, dgate[...])
            ggate_ref[cols, :] = both[:, :256]
            gate_o[cols, :] = both[:, 256:].astype(BF16)
            both = dot_nn(turned, dup[...])
            gup_ref[cols, :] = both[:, :256]
            up_o[cols, :] = both[:, 256:].astype(BF16)

        @pl.when(i == 0)
        def _():
            down_o[...] = dot_nn(hid[:, 256:].T, g[...]).astype(BF16)

        @pl.when(i == 1)
        def _():
            across(7).start()
            gdown_ref[...] = dot_nn(hid[:, :256].T, g[...])

        return carry

    lax.fori_loop(0, 6, grad_step, 0)
    across(5).start()
    for k in (2, 3, 1, 0):
        so.over_copy(place.near(k)).start()

    from_experts = si.total()
    pairs = from_experts[:, WIDTH:]
    gates = gates_s[...]
    grad_gates = (pairs + pltpu.roll(pairs, 112, 1)) * kept_s[...]
    grad_logits = (gates * (grad_gates - jnp.sum(gates * grad_gates, -1, keepdims=True))).astype(BF16)
    grad_moe_in = from_experts[:, :WIDTH] + dot_nt(grad_logits, router_ref[...])
    resid = residual[...]
    inv_two = lax.rsqrt(mean_last(resid * resid) + EPSILON)
    grad_n = grad_moe_in * gain_two_ref[...]
    grad_residual = (
        cot_ref[...].astype(F32)
        + inv_two * grad_n
        - resid * (inv_two * inv_two * inv_two * mean_last(grad_n * resid))
    )
    branch_grad[own, :] = grad_residual.astype(BF16)
    across(8).start()
    grad_tokens_ref[...] = grad_residual
    small = dot_tn(grad_logits, x[mine, :WIDTH])
    ext_o[0:16, :] = small[0:16, :]
    ext_o[16:17, :] = jnp.sum(grad_moe_in * resid * inv_two, 0, keepdims=True)

    def grad_attended(rows):
        joint_grad[rows, :512] = dot_nt(branch_grad[rows, :], wo_ref[...]).astype(BF16)

    grad_attended(own)
    arrived(8)
    across(6).start()
    grad_attended(peers)
    wo_part[...] = dot_tn(attended[...], branch_grad[...]).astype(BF16)

    si.sib_sent()
    si.sent()

    def share_out(n, carry):
        ring, other = place.step(n, PAIR_FIRST)
        start = pl.multiple_of(place.chip(ring, other) * 64, 64)
        i = other * 4 + ring
        put(place, i, sw.sums, sw.theirs, slice(0, WIDTH), wo_part[pl.ds(start, 64), :])
        sw.sib_copy(i).start()
        return carry

    lax.fori_loop(0, 8, share_out, 0)
    so.relay(2)

    def attend_back(m, carry):
        cols = pl.ds(pl.multiple_of(m * 128, 128), 128)
        cos, sin = cos_ref[...], sin_ref[...]
        from_values, from_keys = [], []
        for half in range(2):
            j, wide, key, value, query = heads_of(m, half)
            grad_mixed = stacked(joint_grad[:, wide].astype(F32)).astype(BF16)
            share = probs[j]
            grad_probs = dot_nt(grad_mixed, value)
            grad_scores = (
                share * (grad_probs - jnp.sum(share * grad_probs, -1, keepdims=True)) * scale
            ).astype(BF16)
            grad_query = unstacked(dot_nn(grad_scores, key))
            joint_grad[:, wide] = (grad_query * cos - swapped(grad_query) * sin).astype(BF16)
            one = dot_tn(share.astype(BF16), grad_mixed)
            from_values.append(one + pltpu.roll(one, 64, 1))
            one = dot_tn(grad_scores, query)
            from_keys.append(one + pltpu.roll(one, 64, 1))
        low_lanes = lax.broadcasted_iota(jnp.int32, (256, 128), 1) < 64
        grad_key = jnp.where(low_lanes, from_keys[0], from_keys[1])
        at_key = pl.ds(pl.multiple_of(512 + m * 128, 128), 128)
        at_value = pl.ds(pl.multiple_of(768 + m * 128, 128), 128)
        joint_grad[:, at_key] = (grad_key * cos - swapped(grad_key) * sin).astype(BF16)
        joint_grad[:, at_value] = jnp.where(low_lanes, from_values[0], from_values[1]).astype(BF16)
        return carry

    lax.fori_loop(0, 2, attend_back, 0)

    def all_joined(tree):
        def one(n, carry):
            ring, other = place.step(n, PAIR_FIRST)
            tree.join(other * 4 + ring)

            @pl.when(other == 1)
            def _():
                tree.over_copy(ring).start()

            return carry

        lax.fori_loop(0, 8, one, 0)

    all_joined(sw)
    so.relay(3)

    def grad_normed(rows):
        grads = joint_grad[rows, :]
        parts = []
        for n in range(4):
            at = slice(n * 256, (n + 1) * 256)
            parts.append(
                dot_nt(grads[:, :512], wq_ref[at, :])
                + dot_nt(grads[:, 512:768], wk_ref[at, :])
                + dot_nt(grads[:, 768:], wv_ref[at, :])
            )
        return jnp.concatenate(parts, 1)

    part = grad_normed(peers)
    across(4).wait_send()
    branch_o[...] = part.astype(BF16)
    across(10).start()
    gain_sum = jnp.sum(part * normed[peers, :].astype(F32), 0, keepdims=True)
    own_part = grad_normed(own)
    gain_sum = gain_sum + jnp.sum(own_part * normed[own, :].astype(F32), 0, keepdims=True)
    ext_o[17:18, :] = gain_sum / gain_one_ref[...]
    ext_o[18:24, :] = jnp.zeros((6, WIDTH), F32)
    across(9).start()
    so.relay(1)

    def share_joint(n, carry):
        ring, other = place.step(n, PAIR_FIRST)
        cols = pl.ds(pl.multiple_of(place.chip(ring, other) * 128, 128), 128)
        value = dot_nn(normed[:, cols].T, joint_grad[...])
        put(place, other * 4 + ring, sj.sums, sj.theirs, slice(0, WIDTH), value)
        return carry

    lax.fori_loop(0, 8, share_joint, 0)
    across(9).wait_recv()
    ext = ext_o[...] + ext_i[...]
    ext_t[...] = jnp.concatenate([ext, jnp.zeros((104, WIDTH), F32)], 0).T

    def share_ext(n, carry):
        ring, other = place.step(n, PAIR_FIRST)
        rows = pl.ds(pl.multiple_of(place.chip(ring, other) * 128, 128), 128)
        i = other * 4 + ring
        put(place, i, sj.sums, sj.theirs, slice(WIDTH, EXT), ext_t[rows, :])
        sj.sib_copy(i).start()
        return carry

    lax.fori_loop(0, 8, share_ext, 0)
    sw.relay(2, 3, 1)
    all_joined(sj)
    block = pl.ds(pl.multiple_of(place.e * 32, 32), 32)
    wo_grad_ref[block, :] = sw.total().astype(BF16)
    gw.start()

    across(10).wait_recv()
    grad_n = (own_part + norm_i[...].astype(F32)) * gain_one_ref[...]
    inputs = tokens_ref[...].astype(F32)
    inv_one = lax.rsqrt(mean_last(inputs * inputs) + EPSILON)
    grad_tokens_ref[...] = (
        grad_tokens_ref[...]
        + inv_one * grad_n
        - inputs * (inv_one * inv_one * inv_one * mean_last(grad_n * inputs))
    )
    sj.relay(2, 3)
    gw.arrive(0)
    gw.arrive_over(0)
    sj.relay(1)
    output_ref[...] = (residual[...] + so.total()).astype(BF16)
    gw.arrive(1)
    gw.arrive_over(1, 2)
    block = pl.ds(pl.multiple_of(place.e * 64, 64), 64)
    joint_ref[block, :] = sj.total().astype(BF16)
    gj.start()
    gw.arrive(2)
    gw.arrive_over(3, 4)
    gj.arrive(0)
    gj.arrive_over(0)
    gw.arrive_over(5, 6)
    gj.arrive(1)
    gj.arrive_over(1, 2)
    gj.arrive(2)
    gj.arrive_over(3, 4)
    gj.arrive_over(5, 6)
    for tree in (gj, gw):
        tree.from_sib(0, *range(7))
        tree.from_sib(1, *range(7))
    for k in (5, 6, 7):
        across(k).wait_recv()
    for k in (0, 1, 2, 3, 5, 6, 7, 8, 9, 10):
        across(k).wait_send()
    for tree in (so, sj, sw):
        tree.sib_sent()
    for tree in (gx, gg, gj, gw, so, sj, sw):
        tree.sent()


def layer_call(capacity, *operands):
    vm, dma = pltpu.VMEM, pltpu.SemaphoreType.DMA
    spec = pl.BlockSpec(memory_space=pltpu.VMEM)
    sds = jax.ShapeDtypeStruct

    def body(*refs):
        return layer_kernel(capacity, *refs)

    outs = (
        sds((BLK, WIDTH), BF16),
        sds((BLK, WIDTH), F32),
        sds((WIDTH, EXT), BF16),
        sds((HALF, WIDTH), BF16),
        sds((WIDTH, 256), F32),
        sds((WIDTH, 256), F32),
        sds((256, WIDTH), F32),
        sds((WIDTH, 256), BF16),
        sds((WIDTH, 256), BF16),
        sds((256, WIDTH), BF16),
    )
    return pl.pallas_call(
        body,
        out_shape=outs,
        in_specs=[spec] * len(operands),
        out_specs=[spec] * len(outs),
        scratch_shapes=[
            vm((2048, EXT), BF16), vm((2048, WIDTH), BF16),
            vm((WIDTH, 256), BF16), vm((WIDTH, 256), BF16), vm((256, WIDTH), BF16),
            vm((2048, 512), BF16), vm((2048, 512), BF16), vm((2048, 512), BF16),
            vm((8, BLK, EXT), BF16), vm((8, BLK, EXT), BF16), vm((8, BLK, EXT), BF16),
            vm((8, BLK, WIDTH), BF16), vm((8, BLK, WIDTH), BF16), vm((8, BLK, WIDTH), BF16),
            vm((4, BLK, EXT), BF16), vm((3, BLK, EXT), BF16),
            vm((4, BLK, WIDTH), BF16), vm((3, BLK, WIDTH), BF16),
            vm((WIDTH, 256), BF16), vm((WIDTH, 256), BF16), vm((256, WIDTH), BF16),
            vm((256, WIDTH), BF16), vm((256, 256), BF16), vm((256, 256), BF16), vm((256, 512), BF16),
            vm((4, 512, 256), F32), vm((256, 512), BF16),
            vm((BLK, WIDTH), BF16), vm((BLK, WIDTH), BF16), vm((BLK, WIDTH), F32),
            vm((BLK, BLK), F32), vm((BLK, BLK), F32),
            vm((256, WIDTH), BF16), vm((256, WIDTH), BF16),
            vm((BLK, WIDTH), BF16),
            vm((24, WIDTH), F32), vm((24, WIDTH), F32), vm((WIDTH, BLK), F32), vm((512, WIDTH), BF16),
            vm((8, 64, EXT), BF16), vm((4, 64, EXT), BF16), vm((3, 64, EXT), BF16),
            vm((8, 32, WIDTH), BF16), vm((4, 32, WIDTH), BF16), vm((3, 32, WIDTH), BF16),
            dma((4, 27)), dma((4, 27)), dma((4, 7)), dma((4, 7)), dma((4, 8)), dma((4, 8)),
            dma((11,)), dma((11,)),
        ],
        compiler_params=pltpu.CompilerParams(
            collective_id=1, has_side_effects=True, vmem_limit_bytes=63 * 2**20
        ),
        cost_estimate=pl.CostEstimate(flops=24 * 10**9, bytes_accessed=10**7, transcendentals=10**6),
        name="layer",
    )(*operands)


def tables(rows):
    half = HEAD_DIM // 2
    freqs = np.exp(np.arange(half, dtype=np.float32) * np.float32(-2.0 * math.log(THETA_BASE) / HEAD_DIM))
    angles = np.arange(rows, dtype=np.float32)[:, None] * freqs[None, :]
    cos, sin = np.cos(angles), np.sin(angles)
    return (
        np.concatenate([cos] * 4, 1).astype(np.float32),
        np.concatenate([-sin, sin] * 2, 1).astype(np.float32),
    )


def on_device(
    tokens,
    gain_attn,
    w_query,
    w_key,
    w_value,
    w_out,
    gain_moe,
    router,
    expert_gate,
    expert_up,
    expert_down,
    routes,
    fill_order,
    cotangent,
):
    tok_rows, width = tokens.shape
    tensor_size = lax.axis_size("tensor")
    seq_rows = tok_rows * tensor_size
    head_size = HEAD_DIM
    q_cols = w_query.shape[1]
    kv_cols = w_key.shape[1]
    q_heads = q_cols // head_size
    kv_heads = kv_cols // head_size
    q_group = q_heads // kv_heads
    score_scale = head_size ** (-0.5)
    local_experts = expert_gate.shape[0]
    expert_groups = lax.axis_size("expert")
    experts = local_experts * expert_groups
    top_k = routes.shape[1]
    capacity = (5 * tok_rows * top_k + 4 * experts - 1) // (4 * experts)
    gate_w, up_w, down_w = (expert_gate, expert_up, expert_down)
    inputs = tokens.astype(jnp.float32)
    inv_one = lax.rsqrt(jnp.mean(inputs * inputs, -1, keepdims=True) + EPSILON)
    normed = (inputs * inv_one * gain_attn).astype(jnp.bfloat16)
    normed_all = lax.all_gather(normed, "tensor", axis=0, tiled=True)
    w_joint = jnp.concatenate([w_query, w_key, w_value], 1)
    joint = jnp.dot(normed_all, w_joint, preferred_element_type=jnp.float32)
    angles = angles_of(seq_rows, head_size)
    queries = rotate(joint[:, :q_cols].reshape(seq_rows, q_heads, head_size), angles, 1.0).astype(
        jnp.bfloat16
    )
    key_rows = rotate(
        joint[:, q_cols : q_cols + kv_cols].reshape(seq_rows, kv_heads, head_size), angles, 1.0
    ).astype(jnp.bfloat16)
    value_rows = (
        joint[:, q_cols + kv_cols :].astype(jnp.bfloat16).reshape(seq_rows, kv_heads, head_size)
    )
    q_size = min(512, seq_rows)
    blocks = seq_rows // q_size
    key_pos = jnp.arange(seq_rows)

    def scores_of(q_block, row_start):
        grouped = q_block.reshape(q_size, kv_heads, q_group, head_size)
        raw_scores = (
            jnp.einsum("qkgd,tkd->kgqt", grouped, key_rows, preferred_element_type=jnp.float32)
            * score_scale
        )
        allowed = (row_start + jnp.arange(q_size))[:, None] >= key_pos[None, :]
        return (grouped, jnp.where(allowed, raw_scores, MASKED))

    def forward_block(block_args):
        q_block, row_start = block_args
        grouped, scores = scores_of(q_block, row_start)
        top_score = jnp.max(scores, -1, keepdims=True)
        exp_scores = jnp.exp(scores - top_score)
        row_total = jnp.sum(exp_scores, -1, keepdims=True)
        attn_probs = (exp_scores / row_total).astype(jnp.bfloat16)
        mixed_rows = jnp.einsum(
            "kgqt,tkd->qkgd", attn_probs, value_rows, preferred_element_type=jnp.float32
        )
        return (mixed_rows.astype(jnp.bfloat16).reshape(q_size, q_cols), top_score, row_total)

    q_blocks = queries.reshape(blocks, q_size, q_heads, head_size)
    starts = jnp.arange(blocks) * q_size
    attended, maxima, totals = lax.map(forward_block, (q_blocks, starts))
    attended = attended.reshape(seq_rows, q_cols)
    row_block = attended
    branch = lax.psum_scatter(
        jnp.dot(row_block, w_out, preferred_element_type=jnp.float32),
        "tensor",
        scatter_dimension=0,
        tiled=True,
    )
    residual = inputs + branch
    inv_two = lax.rsqrt(jnp.mean(residual * residual, -1, keepdims=True) + EPSILON)
    scaled = residual * inv_two
    moe_in = (scaled * gain_moe).astype(jnp.bfloat16)
    logits = jnp.dot(moe_in, router, preferred_element_type=jnp.float32)
    expert_ids = jnp.arange(experts, dtype=jnp.int32)
    named = jnp.sum((routes[:, :, None] == expert_ids[None, None, :]).astype(jnp.float32), 1)
    place_of = (fill_order[0][:, None] == jnp.arange(tok_rows)[None, :]).astype(jnp.bfloat16)
    ordered = jnp.dot(place_of, named.astype(jnp.bfloat16), preferred_element_type=jnp.float32)
    earlier = (jnp.arange(tok_rows)[:, None] > jnp.arange(tok_rows)[None, :]).astype(jnp.bfloat16)
    before = jnp.dot(earlier, ordered.astype(jnp.bfloat16), preferred_element_type=jnp.float32)
    rank = contract_first(place_of, before.astype(jnp.bfloat16))
    kept = named * (rank < capacity).astype(jnp.float32)
    top_logit = jnp.max(jnp.where(named > 0, logits, MASKED), -1, keepdims=True)
    exp_logits = jnp.where(named > 0, jnp.exp(jnp.minimum(logits - top_logit, 0.0)), 0.0)
    gates = exp_logits / jnp.sum(exp_logits, -1, keepdims=True)
    weights = gates * kept

    gate_all = lax.all_gather(gate_w[0], "tensor", axis=1, tiled=True)
    up_all = lax.all_gather(up_w[0], "tensor", axis=1, tiled=True)
    down_all = lax.all_gather(down_w[0], "tensor", axis=0, tiled=True)
    grad_out = cotangent.astype(jnp.float32)
    plane_cot = lax.all_gather(cotangent, "expert", axis=0, tiled=True)
    plane_in = lax.all_gather(moe_in, "expert", axis=0, tiled=True)
    plane_weights = lax.all_gather(weights, "expert", axis=0, tiled=True)
    mine = (expert_ids == lax.axis_index("expert")).astype(jnp.float32)
    my_weight = jnp.sum(plane_weights * mine[None, :], -1, keepdims=True)

    gate_pre = jnp.dot(plane_in, gate_all, preferred_element_type=jnp.float32)
    up_pre = jnp.dot(plane_in, up_all, preferred_element_type=jnp.float32)
    back_down = contract_last(plane_cot, down_all)
    gate_sigmoid = jax.nn.sigmoid(gate_pre)
    active = gate_pre * gate_sigmoid
    hidden = active * up_pre
    pair_grad = jnp.sum(hidden * back_down, -1, keepdims=True)
    hidden_w = (hidden * my_weight).astype(jnp.bfloat16)
    grad_hidden = back_down * my_weight
    grad_gate_pre = (
        grad_hidden * up_pre * gate_sigmoid * (1.0 + gate_pre * (1.0 - gate_sigmoid))
    ).astype(jnp.bfloat16)
    grad_up_pre = (grad_hidden * active).astype(jnp.bfloat16)
    out_part = jnp.dot(hidden_w, down_all, preferred_element_type=jnp.float32)
    in_part = contract_last(grad_gate_pre, gate_all) + contract_last(grad_up_pre, up_all)
    out_sum = lax.psum_scatter(
        out_part.astype(jnp.bfloat16), "expert", scatter_dimension=0, tiled=True
    )
    in_sum = lax.psum_scatter(
        in_part.astype(jnp.bfloat16), "expert", scatter_dimension=0, tiled=True
    )
    grad_gates = lax.psum_scatter(
        pair_grad * mine[None, :], "expert", scatter_dimension=0, tiled=True
    ) * kept
    grad_down = lax.psum_scatter(
        contract_first(hidden_w, plane_cot).astype(jnp.bfloat16),
        "tensor", scatter_dimension=0, tiled=True,
    ).astype(jnp.float32)[None]
    grad_gate = lax.psum_scatter(
        contract_first(plane_in, grad_gate_pre).astype(jnp.bfloat16),
        "tensor", scatter_dimension=1, tiled=True,
    ).astype(jnp.float32)[None]
    grad_up = lax.psum_scatter(
        contract_first(plane_in, grad_up_pre).astype(jnp.bfloat16),
        "tensor", scatter_dimension=1, tiled=True,
    ).astype(jnp.float32)[None]
    output_rows = residual + out_sum.astype(jnp.float32)
    grad_logits = (
        gates * (grad_gates - jnp.sum(gates * grad_gates, -1, keepdims=True))
    ).astype(jnp.bfloat16)
    grad_moe_in = in_sum.astype(jnp.float32) + contract_last(grad_logits, router)
    grad_router = contract_first(moe_in, grad_logits)
    grad_gain_moe = jnp.sum(grad_moe_in * scaled, 0)
    grad_norm_two = grad_moe_in * gain_moe
    grad_residual = (
        grad_out
        + inv_two * grad_norm_two
        - residual * inv_two**3 * jnp.mean(grad_norm_two * residual, -1, keepdims=True)
    )
    grad_branch = grad_residual.astype(jnp.bfloat16)
    shard_piece = lax.all_gather(grad_branch, "tensor", axis=0, tiled=True)
    grad_part = contract_last(shard_piece, w_out).astype(jnp.bfloat16)
    grad_mixed = grad_part
    grad_wout = contract_first(attended, shard_piece)
    grad_mixed, grad_w_out = (grad_mixed, grad_wout)
    grad_blocks = grad_mixed.reshape(blocks, q_size, q_heads, head_size)

    def backward_block(carry, block_args):
        grad_keys, grad_values = carry
        q_block, grad_block, row_start, top_score, row_total = block_args
        grouped, scores = scores_of(q_block, row_start)
        attn_probs = jnp.exp(scores - top_score) / row_total
        grad_grouped = grad_block.reshape(q_size, kv_heads, q_group, head_size)
        grad_probs = jnp.einsum(
            "qkgd,tkd->kgqt", grad_grouped, value_rows, preferred_element_type=jnp.float32
        )
        grad_values = grad_values + jnp.einsum(
            "kgqt,qkgd->tkd",
            attn_probs.astype(jnp.bfloat16),
            grad_grouped,
            preferred_element_type=jnp.float32,
        )
        grad_scores = (
            attn_probs
            * (grad_probs - jnp.sum(attn_probs * grad_probs, -1, keepdims=True))
            * score_scale
        ).astype(jnp.bfloat16)
        grad_query = jnp.einsum(
            "kgqt,tkd->qkgd", grad_scores, key_rows, preferred_element_type=jnp.float32
        ).reshape(q_size, q_heads, head_size)
        grad_keys = grad_keys + jnp.einsum(
            "kgqt,qkgd->tkd", grad_scores, grouped, preferred_element_type=jnp.float32
        )
        return ((grad_keys, grad_values), grad_query)

    zero_rows = jnp.zeros((seq_rows, kv_heads, head_size), jnp.float32)
    (grad_keys, grad_values), grad_queries = lax.scan(
        backward_block, (zero_rows, zero_rows), (q_blocks, grad_blocks, starts, maxima, totals)
    )
    grad_queries = grad_queries.reshape(seq_rows, q_heads, head_size)
    grad_q = rotate(grad_queries, angles, -1.0).astype(jnp.bfloat16).reshape(seq_rows, q_cols)
    grad_k = rotate(grad_keys, angles, -1.0).astype(jnp.bfloat16).reshape(seq_rows, kv_cols)
    grad_v = grad_values.astype(jnp.bfloat16).reshape(seq_rows, kv_cols)
    grad_joint = jnp.concatenate([grad_q, grad_k, grad_v], 1)
    grad_w_joint = contract_first(normed_all, grad_joint)
    row_block = grad_joint
    grad_normed = lax.psum_scatter(
        contract_last(row_block, w_joint), "tensor", scatter_dimension=0, tiled=True
    )
    grad_gain_attn = jnp.sum(grad_normed * inputs * inv_one, 0)
    grad_norm_one = grad_normed * gain_attn
    grad_tokens = (
        grad_residual
        + inv_one * grad_norm_one
        - inputs * inv_one**3 * jnp.mean(grad_norm_one * inputs, -1, keepdims=True)
    )
    summed_joint, summed_out = lax.psum((grad_w_joint, grad_w_out), "expert")
    summed_gain_attn, summed_gain_moe, summed_router = lax.psum(
        (grad_gain_attn, grad_gain_moe, grad_router), ("expert", "tensor")
    )
    return (
        output_rows.astype(jnp.bfloat16),
        grad_tokens,
        summed_gain_attn,
        summed_joint[:, :q_cols],
        summed_joint[:, q_cols : q_cols + kv_cols],
        summed_joint[:, q_cols + kv_cols :],
        summed_out,
        summed_gain_moe,
        summed_router,
        grad_gate,
        grad_up,
        grad_down,
    )


def by_kernel(
    tokens,
    gain_attn,
    w_query,
    w_key,
    w_value,
    w_out,
    gain_moe,
    router,
    expert_gate,
    expert_up,
    expert_down,
    routes,
    fill_order,
    cotangent,
):
    tok_rows = tokens.shape[0]
    experts = router.shape[1]
    capacity = (5 * tok_rows * routes.shape[1] + 4 * experts - 1) // (4 * experts)
    cos, sin = tables(tok_rows * 2)
    wide_router = jnp.pad(router, ((0, 0), (0, BLK - experts)))
    out, grad_tokens, joint, wo_grad, ggate, gup, gdown, gate_i, up_i, down_i = layer_call(
        capacity,
        tokens, cotangent, gain_attn[None], gain_moe[None], w_query, w_key, w_value, w_out,
        wide_router, routes, fill_order, jnp.asarray(cos), jnp.asarray(sin),
        expert_gate[0], expert_up[0], expert_down[0],
    )
    small = joint[:, WIDTH:].astype(F32)
    return (
        out,
        grad_tokens,
        small[:, experts + 1],
        joint[:, :512].astype(F32),
        joint[:, 512:768].astype(F32),
        joint[:, 768:WIDTH].astype(F32),
        wo_grad.astype(F32),
        small[:, experts],
        small[:, :experts],
        (ggate + gate_i.astype(F32))[None],
        (gup + up_i.astype(F32))[None],
        (gdown + down_i.astype(F32))[None],
    )


def kernel_fits(mesh_shape, shapes):
    return mesh_shape == (16, 2) and shapes == (
        (128, 1024), (1024,), (1024, 512), (1024, 256), (1024, 256), (512, 1024), (1024,), (1024, 16),
        (1, 1024, 256), (1, 1024, 256), (1, 256, 1024), (128, 8), (1, 128), (128, 1024),
    )


def on_any(*operands):
    sizes = (lax.axis_size("expert"), lax.axis_size("tensor"))
    if kernel_fits(sizes, tuple(a.shape for a in operands)):
        return by_kernel(*operands)
    return on_device(*operands)


def solution(mesh):
    placed = (
        P(("expert", "tensor"), None),
        P(),
        P(None, "tensor"),
        P(None, "tensor"),
        P(None, "tensor"),
        P("tensor", None),
        P(),
        P(),
        P("expert", None, "tensor"),
        P("expert", None, "tensor"),
        P("expert", "tensor", None),
        P(("expert", "tensor"), None),
        P(("expert", "tensor"), None),
        P(("expert", "tensor"), None),
    )
    return jax.shard_map(
        on_any,
        mesh=mesh,
        in_specs=placed,
        out_specs=(
            P(("expert", "tensor"), None),
            P(("expert", "tensor"), None),
            P(),
            P(None, "tensor"),
            P(None, "tensor"),
            P(None, "tensor"),
            P("tensor", None),
            P(),
            P(),
            P("expert", None, "tensor"),
            P("expert", None, "tensor"),
            P("expert", "tensor", None),
        ),
        check_vma=False,
    )
```

```python
import math

import jax
import jax.numpy as jnp
import numpy as np
from jax import lax
from jax.experimental import pallas as pl
from jax.experimental.pallas import tpu as pltpu
from jax.sharding import PartitionSpec as P

HEAD_DIM = 64


EPSILON = 1e-06
THETA_BASE = 10000.0
MASKED = -1e30


def angles_of(row_count, head_size):
    half = head_size // 2
    freqs = jnp.exp(jnp.arange(half, dtype=jnp.float32) * (-2.0 * math.log(THETA_BASE) / head_size))
    return jnp.arange(row_count, dtype=jnp.float32)[:, None] * freqs[None, :]


def rotate(vectors, angles, sign):
    half = vectors.shape[-1] // 2
    cosine = jnp.cos(angles)[:, None, :]
    sine = sign * jnp.sin(angles)[:, None, :]
    first = vectors[..., :half]
    second = vectors[..., half:]
    return jnp.concatenate([first * cosine - second * sine, second * cosine + first * sine], -1)


def contract_last(left, right):
    return lax.dot_general(
        left, right, (((1,), (1,)), ((), ())), preferred_element_type=jnp.float32
    )


def contract_first(left, right):
    return lax.dot_general(
        left, right, (((0,), (0,)), ((), ())), preferred_element_type=jnp.float32
    )


F32 = jnp.float32
BF16 = jnp.bfloat16
MESH = pl.DeviceIdType.MESH
BLK = 128
WIDTH = 1024
EXT = 1152
HALF = 512
NEAREST = (0, 1, 2, 3, 1, 0, 2, 3, 2, 3, 1, 0, 3, 2, 1, 0)
EXPERT_ORDER = ((1, 1), (1, 0), (2, 1), (2, 0), (3, 1), (3, 0), (0, 1), (0, 0))
PAIR_FIRST = ((3, 1), (2, 1), (1, 1), (0, 1), (3, 0), (2, 0), (1, 0), (0, 0))


def pick(i, values):
    out = jnp.int32(values[-1])
    for n in range(len(values) - 2, -1, -1):
        out = jnp.where(i == n, jnp.int32(values[n]), out)
    return out


class Place:
    def __init__(self):
        e = lax.axis_index("expert")
        t = lax.axis_index("tensor")
        self.e = e
        self.t = t
        self.core = lax.rem(e, 2)
        self.pair = lax.rem(e // 2, 2)
        self.ring = e // 4
        self.other = (e + 2 - 4 * self.pair, t)
        self.sib = (e + 1 - 2 * self.core, t)
        self.across = (e, 1 - t)

    def at(self, ring):
        return (ring * 4 + lax.rem(self.e, 4), self.t)

    def chip(self, ring, other):
        return ring * 2 + (self.pair + other - 2 * self.pair * other)

    def step(self, i, order):
        ring = self.near(pick(i, [k for k, _ in order]))
        return ring, pick(i, [other for _, other in order])

    def near(self, k):
        return pick(self.ring * 4 + k, NEAREST)

    def barrier(self):
        bar = pltpu.get_barrier_semaphore()
        for dest in [self.at(lax.rem(self.ring + m, 4)) for m in (1, 2, 3)] + [
            self.other, self.sib, self.across,
        ]:
            pl.semaphore_signal(bar, inc=1, device_id=dest, device_id_type=MESH)
        pl.semaphore_wait(bar, 6)


def if_(condition, action):
    if condition is True:
        action()
    else:
        pl.when(condition)(action)


class Gather:
    def __init__(self, place, buf, send_sems, recv_sems):
        self.place, self.buf, self.ss, self.rs = place, buf, send_sems, recv_sems
        self.size = buf.shape[0] // 16

    def where(self, n):
        r = self.place.ring
        if n == 0:
            return r, True
        j = (n - 1) // 2
        return (r - 1 - j, r > j) if n % 2 else (r + 1 + j, 3 - r > j)

    def copy(self, ring, other, core, sem, dest):
        block = self.place.chip(ring, other) * 2 + core
        ref = self.buf.at[pl.ds(pl.multiple_of(block * self.size, self.size), self.size)]
        return pltpu.make_async_remote_copy(
            src_ref=ref, dst_ref=ref, send_sem=self.ss.at[sem], recv_sem=self.rs.at[sem],
            device_id=dest, device_id_type=MESH,
        )

    def up(self, k):
        r = self.place.ring
        return self.copy(r - k, 0, self.place.core, k, self.place.at(r + 1))

    def down(self, k):
        r = self.place.ring
        return self.copy(r + k, 0, self.place.core, 3 + k, self.place.at(r - 1))

    def over(self, n, arriving=0):
        return self.copy(self.where(n)[0], arriving, self.place.core, 6 + n, self.place.other)

    def to_sib(self, n, other, arriving=False):
        core = 1 - self.place.core if arriving else self.place.core
        return self.copy(self.where(n)[0], other, core, 13 + 7 * other + n, self.place.sib)

    def start(self):
        r = self.place.ring
        if_(r < 3, lambda: self.up(0).start())
        if_(r > 0, lambda: self.down(0).start())
        self.over(0).start()
        self.to_sib(0, 0).start()

    def arrive(self, j):
        r = self.place.ring

        def from_below():
            self.copy(r - 1 - j, 0, self.place.core, j, self.place.other).wait_recv()
            if j < 2:
                if_(r < 3, lambda: self.up(j + 1).start())
            self.over(1 + 2 * j).start()
            self.to_sib(1 + 2 * j, 0).start()

        def from_above():
            self.copy(r + 1 + j, 0, self.place.core, 3 + j, self.place.other).wait_recv()
            if j < 2:
                if_(r > 0, lambda: self.down(j + 1).start())
            self.over(2 + 2 * j).start()
            self.to_sib(2 + 2 * j, 0).start()

        if_(r > j, from_below)
        if_(3 - r > j, from_above)

    def arrive_over(self, *numbers):
        for n in numbers:

            def taken(n=n):
                self.over(n, 1).wait_recv()
                self.to_sib(n, 1).start()

            if_(self.where(n)[1], taken)

    def from_sib(self, other, *numbers):
        for n in numbers:
            if_(self.where(n)[1], lambda n=n: self.to_sib(n, other, True).wait_recv())

    def sent(self):
        r = self.place.ring
        for k in range(3):
            if_((r < 3) & (r >= k), lambda k=k: self.up(k).wait_send())
            if_((r > 0) & (3 - r >= k), lambda k=k: self.down(k).wait_send())
        for n in range(7):

            def all_of(n=n):
                self.over(n).wait_send()
                self.to_sib(n, 0).wait_send()
                self.to_sib(n, 1).wait_send()

            if_(self.where(n)[1], all_of)


class Scatter:
    def __init__(self, place, sums, theirs, from_sib, over, along, sib_ss, sib_rs, ss, rs):
        self.place, self.sums, self.theirs, self.from_sib = place, sums, theirs, from_sib
        self.over, self.along = over, along
        self.sib_ss, self.sib_rs, self.ss, self.rs = sib_ss, sib_rs, ss, rs
        self.left = (0, 1, 2, 3)

    def sib_copy(self, i):
        return pltpu.make_async_remote_copy(
            src_ref=self.theirs.at[i], dst_ref=self.from_sib.at[i],
            send_sem=self.sib_ss.at[i], recv_sem=self.sib_rs.at[i],
            device_id=self.place.sib, device_id_type=MESH,
        )

    def join(self, i):
        self.sib_copy(i).wait_recv()
        total = self.sums[i].astype(F32) + self.from_sib[i].astype(F32)
        self.sums[i] = total.astype(self.from_sib.dtype)

    def join_all(self):
        for n, (k, other) in enumerate(PAIR_FIRST):
            ring = self.place.near(k)
            self.join(other * 4 + ring)
            if other:
                if n >= 2:
                    self.over_copy(self.place.near(PAIR_FIRST[n - 2][0])).wait_send()
                self.over_copy(ring).start()
        self.left = (1, 0)

    def over_copy(self, ring):
        return pltpu.make_async_remote_copy(
            src_ref=self.sums.at[4 + ring], dst_ref=self.over.at[ring],
            send_sem=self.ss.at[ring], recv_sem=self.rs.at[ring],
            device_id=self.place.other, device_id_type=MESH,
        )

    def along_copy(self, ring):
        m = lax.rem(self.place.ring - ring + 4, 4)
        return pltpu.make_async_remote_copy(
            src_ref=self.sums.at[ring], dst_ref=self.along.at[m - 1],
            send_sem=self.ss.at[3 + m], recv_sem=self.rs.at[3 + m],
            device_id=self.place.at(ring), device_id_type=MESH,
        )

    def relay(self, *ks):
        for k in ks:
            ring = self.place.near(k)
            self.over_copy(ring).wait_recv()
            total = self.sums[ring].astype(F32) + self.over[ring].astype(F32)
            self.sums[ring] = total.astype(self.over.dtype)
            self.along_copy(ring).start()

    def total(self):
        ring = self.place.ring
        self.over_copy(ring).wait_recv()
        for m in (1, 2, 3):
            pltpu.make_async_remote_copy(
                src_ref=self.sums.at[ring], dst_ref=self.along.at[m - 1],
                send_sem=self.ss.at[3 + m], recv_sem=self.rs.at[3 + m],
                device_id=self.place.other, device_id_type=MESH,
            ).wait_recv()
        return (
            (self.sums[ring].astype(F32) + self.over[ring].astype(F32))
            + (self.along[0].astype(F32) + self.along[1].astype(F32))
            + self.along[2].astype(F32)
        )

    def sib_sent(self):
        for i in range(8):
            self.sib_copy(i).wait_send()

    def sent(self):
        for k in self.left:
            self.over_copy(self.place.near(k)).wait_send()
        for k in (1, 2, 3):
            self.along_copy(self.place.near(k)).wait_send()


def dot_nn(a, b):
    return lax.dot_general(a, b, (((1,), (0,)), ((), ())), preferred_element_type=F32)


def dot_nt(a, b):
    return lax.dot_general(a, b, (((1,), (1,)), ((), ())), preferred_element_type=F32)


def dot_tn(a, b):
    return lax.dot_general(a, b, (((0,), (0,)), ((), ())), preferred_element_type=F32)


def expert_step(place, ring, other, x, g, gates_w, ups_w, downs_w, hid, dgate, dup, in_s, in_t, out_s, out_t):
    i = other * 4 + ring
    rows = pl.ds(pl.multiple_of(place.chip(ring, other) * 256, 256), 256)
    lane = lax.broadcasted_iota(jnp.int32, (256, 128), 1)
    high, low = lane == place.e, lane == place.e + 16
    weight = jnp.sum(
        jnp.where(high | low, x[rows, WIDTH:EXT].astype(F32), 0.0), -1, keepdims=True
    )
    pair_grad = jnp.zeros((256, 1), F32)
    for h in range(2):
        cols = slice(h * 256, (h + 1) * 256)
        gate_pre = dot_nn(x[rows, :WIDTH], gates_w[h][...])
        up_pre = dot_nn(x[rows, :WIDTH], ups_w[h][...])
        back = dot_nt(g[rows, :], downs_w[h][...])
        sig = jax.nn.sigmoid(gate_pre)
        act = gate_pre * sig
        hidden = act * up_pre
        pair_grad = pair_grad + jnp.sum(hidden * back, -1, keepdims=True)
        grad_hidden = back * weight
        hid[rows, cols] = (hidden * weight).astype(BF16)
        dgate[rows, cols] = (grad_hidden * up_pre * (sig + act * (1.0 - sig))).astype(BF16)
        dup[rows, cols] = (grad_hidden * act).astype(BF16)
    coarse = pair_grad.astype(BF16).astype(F32)
    ext = jnp.where(high, coarse, jnp.where(low, pair_grad - coarse, 0.0))
    put(place, i, in_s, in_t, slice(WIDTH, EXT), ext)
    for n in range(4):
        cols = slice(n * 256, (n + 1) * 256)
        value = (
            dot_nt(dgate[rows, 0:256], gates_w[0][cols, :])
            + dot_nt(dgate[rows, 256:512], gates_w[1][cols, :])
            + dot_nt(dup[rows, 0:256], ups_w[0][cols, :])
            + dot_nt(dup[rows, 256:512], ups_w[1][cols, :])
        )
        put(place, i, in_s, in_t, cols, value)
    for n in range(4):
        cols = slice(n * 256, (n + 1) * 256)
        value = dot_nn(hid[rows, 0:256], downs_w[0][:, cols]) + dot_nn(
            hid[rows, 256:512], downs_w[1][:, cols]
        )
        put(place, i, out_s, out_t, cols, value)


def put(place, i, ours, theirs, cols, value):
    half = value.shape[0] // 2
    first, second = value[:half], value[half:]
    is_first = place.core == 0
    ours[i, :, cols] = jnp.where(is_first, first, second).astype(ours.dtype)
    theirs[i, :, cols] = jnp.where(is_first, second, first).astype(theirs.dtype)


def mean_last(v):
    return jnp.sum(v, -1, keepdims=True) * (1.0 / v.shape[-1])


def swapped(v):
    lane = lax.broadcasted_iota(jnp.int32, v.shape, 1)
    return jnp.where(lax.rem(lane, 64) < 32, pltpu.roll(v, 96, 1), pltpu.roll(v, 32, 1))


def doubled(v, half):
    lane = lax.broadcasted_iota(jnp.int32, v.shape, 1)
    one = jnp.where((lane < 64) == (half == 0), v, 0.0)
    return one + pltpu.roll(one, 64, 1)


def stacked(v):
    lane = lax.broadcasted_iota(jnp.int32, v.shape, 1)
    return jnp.concatenate([jnp.where(lane < 64, v, 0.0), jnp.where(lane < 64, 0.0, v)], 0)


def unstacked(v):
    rows = v.shape[0] // 2
    lane = lax.broadcasted_iota(jnp.int32, (rows, 128), 1)
    return jnp.where(lane < 64, v[:rows], v[rows:])


def layer_kernel(
    capacity,
    tokens_ref, cot_ref, gain_one_ref, gain_two_ref, wq_ref, wk_ref, wv_ref, wo_ref, router_ref,
    routes_ref, fill_ref, cos_ref, sin_ref, gate_ref, up_ref, down_ref,
    output_ref, grad_tokens_ref, joint_ref, wo_grad_ref, small_ref,
    ggate_ref, gup_ref, gdown_ref, gate_i, up_i, down_i,
    x, g, gate_p, up_p, down_p, hid, dgate, dup,
    in_s, in_t, in_f, out_s, out_t, out_f, in_1, in_2, out_1, out_2, gate_o, up_o, down_o,
    normed, keys, values, queries, probs, attended, branch_o, branch_i, residual, gates_s, kept_s,
    branch_grad, joint_grad, norm_i, ext_o, ext_i, ext_t, wo_part,
    j_f, j_1, j_2, w_f, w_1, w_2, e_s, e_t, e_f, e_1, e_2, wide_router,
    ag_ss, ag_rs, sc_ss, sc_rs, sib_ss, sib_rs, y_ss, y_rs,
):
    place = Place()
    mine = pl.ds(pl.multiple_of(place.e * BLK, BLK), BLK)
    own = pl.ds(pl.multiple_of(place.t * BLK, BLK), BLK)
    peers = pl.ds(pl.multiple_of((1 - place.t) * BLK, BLK), BLK)
    gx = Gather(place, x, ag_ss.at[0], ag_rs.at[0])
    gg = Gather(place, g, ag_ss.at[1], ag_rs.at[1])
    gj = Gather(place, joint_ref, ag_ss.at[2], ag_rs.at[2])
    gw = Gather(place, wo_grad_ref, ag_ss.at[3], ag_rs.at[3])
    ge = Gather(place, small_ref, ag_ss.at[4], ag_rs.at[4])

    def scatter(n, *refs):
        return Scatter(place, *refs, sib_ss.at[n], sib_rs.at[n], sc_ss.at[n], sc_rs.at[n])

    si = scatter(0, in_s, in_t, in_f, in_1, in_2)
    so = scatter(1, out_s, out_t, out_f, out_1, out_2)
    narrow = lambda ref, start, size, lanes: ref.at[:, pl.ds(start, size), pl.ds(0, lanes)]
    sj = scatter(2, narrow(in_s, 0, 64, WIDTH), narrow(in_t, 0, 64, WIDTH), j_f, j_1, j_2)
    se = scatter(4, e_s, e_t, e_f, e_1, e_2)
    sw = scatter(3, narrow(in_s, 64, 32, WIDTH), narrow(in_t, 64, 32, WIDTH), w_f, w_1, w_2)

    def across(k):
        src, dst = {
            0: (normed.at[own], normed.at[own]),
            1: (gate_ref, gate_p),
            2: (up_ref, up_p),
            3: (down_ref, down_p),
            4: (branch_o, branch_i),
            5: (gate_o, gate_i),
            6: (up_o, up_i),
            7: (down_o, down_i),
            8: (branch_grad.at[own], branch_grad.at[own]),
            9: (ext_o, ext_i),
            10: (branch_o, norm_i),
        }[k]
        return pltpu.make_async_remote_copy(
            src_ref=src, dst_ref=dst, send_sem=y_ss.at[k], recv_sem=y_rs.at[k],
            device_id=place.across, device_id_type=MESH,
        )

    def arrived(k):
        ref = {0: normed, 8: branch_grad}.get(k)
        if ref is None:
            across(k).wait_recv()
        else:
            pltpu.make_async_remote_copy(
                src_ref=ref.at[peers], dst_ref=ref.at[peers], send_sem=y_ss.at[k],
                recv_sem=y_rs.at[k], device_id=place.across, device_id_type=MESH,
            ).wait_recv()

    g[mine, :] = cot_ref[...]
    inputs = tokens_ref[...].astype(F32)
    inv_one = lax.rsqrt(mean_last(inputs * inputs) + EPSILON)
    normed[own, :] = (inputs * inv_one * gain_one_ref[...]).astype(BF16)
    place.barrier()
    across(0).start()
    gg.start()

    lane = lax.broadcasted_iota(jnp.int32, (BLK, BLK), 1)
    row = lax.broadcasted_iota(jnp.int32, (BLK, BLK), 0)
    named = jnp.zeros((BLK, BLK), F32)
    routes = routes_ref[...]
    for j in range(routes.shape[0]):
        named = named + (routes[j : j + 1, :] == row).astype(F32)
    named = named.T
    wide_router[0 : router_ref.shape[0], :] = router_ref[...]
    wide_router[router_ref.shape[0] :, :] = jnp.zeros((BLK - router_ref.shape[0], WIDTH), BF16)
    place_of = (fill_ref[...] == row).astype(F32).astype(BF16)
    ordered = dot_tn(place_of, named.astype(BF16))
    earlier = (row > lane).astype(F32).astype(BF16)
    before = dot_nn(earlier, ordered.astype(BF16))
    rank = dot_nn(place_of, before.astype(BF16))
    kept = jnp.where(rank < capacity, named, 0.0)
    kept_s[...] = kept

    def project(rows):
        cos, sin = cos_ref[rows, :], sin_ref[rows, :]
        for n in range(2):
            part = dot_nn(normed[rows, :], wq_ref[:, n * 256 : (n + 1) * 256])
            for m in range(2):
                one = part[:, m * 128 : (m + 1) * 128]
                queries[rows, n * 256 + m * 128 : n * 256 + (m + 1) * 128] = (
                    one * cos + swapped(one) * sin
                ).astype(BF16)
        part = dot_nn(normed[rows, :], wk_ref[...])
        for m in range(2):
            one = part[:, m * 128 : (m + 1) * 128]
            keys[rows, m * 128 : (m + 1) * 128] = (one * cos + swapped(one) * sin).astype(BF16)
        values[rows, :] = dot_nn(normed[rows, :], wv_ref[...]).astype(BF16)

    project(own)
    arrived(0)
    across(1).start()
    project(peers)
    gg.arrive(0)
    gg.arrive_over(0)

    scale = HEAD_DIM ** (-0.5)

    def heads_of(m, half):
        cols = pl.ds(pl.multiple_of(m * 128, 128), 128)
        key = doubled(keys[:, cols].astype(F32), half).astype(BF16)
        value = doubled(values[:, cols].astype(F32), half).astype(BF16)
        j = m * 2 + half
        wide = pl.ds(pl.multiple_of(j * 128, 128), 128)
        query = stacked(queries[:, wide].astype(F32)).astype(BF16)
        return j, wide, key, value, query

    def attend(m, carry):
        place_q = lax.rem(lax.broadcasted_iota(jnp.int32, (512, 256), 0), 256)
        place_k = lax.broadcasted_iota(jnp.int32, (512, 256), 1)
        for half in range(2):
            j, wide, key, value, query = heads_of(m, half)
            scores = jnp.where(place_q >= place_k, dot_nt(query, key) * scale, MASKED)
            raised = jnp.exp(scores - jnp.max(scores, -1, keepdims=True))
            share = raised / jnp.sum(raised, -1, keepdims=True)
            probs[j] = share
            attended[:, wide] = unstacked(dot_nn(share.astype(BF16), value)).astype(BF16)
        return carry

    lax.fori_loop(0, 2, attend, 0)
    gg.arrive(1)
    gg.arrive_over(1, 2)
    branch_o[...] = dot_nn(attended[peers, :], wo_ref[...]).astype(BF16)
    across(4).start()
    own_branch = dot_nn(attended[own, :], wo_ref[...])
    gg.arrive(2)
    gg.arrive_over(3, 4)
    across(4).wait_recv()
    across(2).start()
    across(3).start()
    resid = tokens_ref[...].astype(F32) + own_branch + branch_i[...].astype(F32)
    residual[...] = resid
    inv_two = lax.rsqrt(mean_last(resid * resid) + EPSILON)
    moe_in = (resid * inv_two * gain_two_ref[...]).astype(BF16)
    logits = dot_nt(moe_in, wide_router[...])
    is_named = named > 0.0
    top = jnp.max(jnp.where(is_named, logits, MASKED), -1, keepdims=True)
    raised = jnp.where(is_named, jnp.exp(jnp.minimum(logits - top, 0.0)), 0.0)
    gates = raised / jnp.sum(raised, -1, keepdims=True)
    gates_s[...] = gates
    weights = gates * kept
    coarse = weights.astype(BF16).astype(F32)
    x[mine, :WIDTH] = moe_in
    x[mine, WIDTH:] = (coarse + pltpu.roll(weights - coarse, 16, 1)).astype(BF16)

    gx.start()
    gg.arrive_over(5, 6)
    gates_w, ups_w, downs_w = (gate_ref, gate_p), (up_ref, up_p), (down_ref, down_p)
    gx.arrive(0)
    gx.arrive_over(0)
    gx.arrive(1)
    gx.arrive_over(1, 2)
    gg.from_sib(0, *range(7))
    gg.from_sib(1, *range(7))
    gx.from_sib(0, 0, 1, 2)
    gx.from_sib(1, 0, 1, 2)
    for k in (1, 2, 3):
        across(k).wait_recv()

    def joined(i):
        ring, other = place.step(i, EXPERT_ORDER)
        si.join(other * 4 + ring)
        so.join(other * 4 + ring)

        @pl.when(other == 1)
        def _():
            si.over_copy(ring).start()

    def chip_step(i, carry):
        @pl.when(i == 2)
        def _():
            gx.arrive(2)
            gx.arrive_over(3, 4)
            gx.from_sib(0, 3, 4)
            gx.from_sib(1, 3, 4)

        @pl.when(i == 4)
        def _():
            gx.arrive_over(5, 6)
            gx.from_sib(0, 5, 6)
            gx.from_sib(1, 5, 6)

        ring, other = place.step(i, EXPERT_ORDER)
        expert_step(
            place, ring, other, x, g, gates_w, ups_w, downs_w, hid, dgate, dup, in_s, in_t, out_s, out_t
        )
        si.sib_copy(other * 4 + ring).start()
        so.sib_copy(other * 4 + ring).start()

        @pl.when(i >= 1)
        def _():
            joined(i - 1)

        return carry

    lax.fori_loop(0, 8, chip_step, 0)

    def grad_step(i, carry):
        @pl.when(i == 0)
        def _():
            joined(jnp.int32(7))

        @pl.when(i == 1)
        def _():
            si.relay(1)

        @pl.when(i == 3)
        def _():
            si.relay(2)

        @pl.when(i == 5)
        def _():
            si.relay(3)

        @pl.when((i >= 2))
        def _():
            cols = pl.ds(pl.multiple_of((i - 2) * 256, 256), 256)
            turned = x[:, cols].T
            both = dot_nn(turned, dgate[...])
            ggate_ref[cols, :] = both[:, :256]
            gate_o[cols, :] = both[:, 256:].astype(BF16)
            both = dot_nn(turned, dup[...])
            gup_ref[cols, :] = both[:, :256]
            up_o[cols, :] = both[:, 256:].astype(BF16)

        @pl.when(i == 0)
        def _():
            down_o[...] = dot_nn(hid[:, 256:].T, g[...]).astype(BF16)

        @pl.when(i == 1)
        def _():
            across(7).start()
            gdown_ref[...] = dot_nn(hid[:, :256].T, g[...])

        return carry

    lax.fori_loop(0, 6, grad_step, 0)
    across(5).start()
    for k in (3, 2, 1, 0):
        so.over_copy(place.near(k)).start()

    from_experts = si.total()
    pairs = from_experts[:, WIDTH:]
    gates = gates_s[...]
    grad_gates = (pairs + pltpu.roll(pairs, 112, 1)) * kept_s[...]
    grad_logits = (gates * (grad_gates - jnp.sum(gates * grad_gates, -1, keepdims=True))).astype(BF16)
    grad_moe_in = from_experts[:, :WIDTH] + dot_nn(grad_logits, wide_router[...])
    resid = residual[...]
    inv_two = lax.rsqrt(mean_last(resid * resid) + EPSILON)
    grad_n = grad_moe_in * gain_two_ref[...]
    grad_residual = (
        cot_ref[...].astype(F32)
        + inv_two * grad_n
        - resid * (inv_two * inv_two * inv_two * mean_last(grad_n * resid))
    )
    branch_grad[own, :] = grad_residual.astype(BF16)
    across(8).start()
    grad_tokens_ref[...] = grad_residual
    small = dot_tn(grad_logits, x[mine, :WIDTH])
    ext_o[0:16, :] = small[0:16, :]
    ext_o[16:17, :] = jnp.sum(grad_moe_in * resid * inv_two, 0, keepdims=True)

    def grad_attended(rows):
        joint_grad[rows, :512] = dot_nt(branch_grad[rows, :], wo_ref[...]).astype(BF16)

    grad_attended(own)
    arrived(8)
    across(6).start()
    grad_attended(peers)
    wo_part[...] = dot_tn(attended[...], branch_grad[...]).astype(BF16)

    si.sib_sent()
    si.sent()

    def share_out(n, carry):
        ring, other = place.step(n, PAIR_FIRST)
        start = pl.multiple_of(place.chip(ring, other) * 64, 64)
        i = other * 4 + ring
        put(place, i, sw.sums, sw.theirs, slice(0, WIDTH), wo_part[pl.ds(start, 64), :])
        sw.sib_copy(i).start()
        return carry

    lax.fori_loop(0, 8, share_out, 0)

    def attend_back(m, carry):
        cols = pl.ds(pl.multiple_of(m * 128, 128), 128)
        cos, sin = cos_ref[...], sin_ref[...]
        from_values, from_keys = [], []
        for half in range(2):
            j, wide, key, value, query = heads_of(m, half)
            grad_mixed = stacked(joint_grad[:, wide].astype(F32)).astype(BF16)
            share = probs[j]
            grad_probs = dot_nt(grad_mixed, value)
            grad_scores = (
                share * (grad_probs - jnp.sum(share * grad_probs, -1, keepdims=True)) * scale
            ).astype(BF16)
            grad_query = unstacked(dot_nn(grad_scores, key))
            joint_grad[:, wide] = (grad_query * cos - swapped(grad_query) * sin).astype(BF16)
            one = dot_tn(share.astype(BF16), grad_mixed)
            from_values.append(one + pltpu.roll(one, 64, 1))
            one = dot_tn(grad_scores, query)
            from_keys.append(one + pltpu.roll(one, 64, 1))
        low_lanes = lax.broadcasted_iota(jnp.int32, (256, 128), 1) < 64
        grad_key = jnp.where(low_lanes, from_keys[0], from_keys[1])
        at_key = pl.ds(pl.multiple_of(512 + m * 128, 128), 128)
        at_value = pl.ds(pl.multiple_of(768 + m * 128, 128), 128)
        joint_grad[:, at_key] = (grad_key * cos - swapped(grad_key) * sin).astype(BF16)
        joint_grad[:, at_value] = jnp.where(low_lanes, from_values[0], from_values[1]).astype(BF16)
        return carry

    lax.fori_loop(0, 2, attend_back, 0)

    def share_joint(n, carry):
        ring, other = place.step(n, PAIR_FIRST)
        i = other * 4 + ring
        cols = pl.ds(pl.multiple_of(place.chip(ring, other) * 128, 128), 128)
        value = dot_nn(normed[:, cols].T, joint_grad[...])
        put(place, i, sj.sums, sj.theirs, slice(0, WIDTH), value)
        sj.sib_copy(i).start()
        return carry

    lax.fori_loop(0, 8, share_joint, 0)

    def grad_normed(rows):
        grads = joint_grad[rows, :]
        parts = []
        for n in range(4):
            at = slice(n * 256, (n + 1) * 256)
            parts.append(
                dot_nt(grads[:, :512], wq_ref[at, :])
                + dot_nt(grads[:, 512:768], wk_ref[at, :])
                + dot_nt(grads[:, 768:], wv_ref[at, :])
            )
        return jnp.concatenate(parts, 1)

    part = grad_normed(peers)
    across(4).wait_send()
    branch_o[...] = part.astype(BF16)
    gain_sum = jnp.sum(part * normed[peers, :].astype(F32), 0, keepdims=True)
    sj.join_all()
    own_part = grad_normed(own)
    gain_sum = gain_sum + jnp.sum(own_part * normed[own, :].astype(F32), 0, keepdims=True)
    ext_o[17:18, :] = gain_sum / gain_one_ref[...]
    ext_o[18:24, :] = jnp.zeros((6, WIDTH), F32)
    across(9).start()
    across(10).start()
    sw.join_all()
    sj.relay(3, 2)
    across(9).wait_recv()
    ext = ext_o[...] + ext_i[...]
    ext_t[...] = jnp.concatenate([ext, jnp.zeros((104, WIDTH), F32)], 0).T

    def share_ext(n, carry):
        ring, other = place.step(n, PAIR_FIRST)
        rows = pl.ds(pl.multiple_of(place.chip(ring, other) * 128, 128), 128)
        i = other * 4 + ring
        put(place, i, se.sums, se.theirs, slice(0, BLK), ext_t[rows, :])
        se.sib_copy(i).start()
        return carry

    lax.fori_loop(0, 8, share_ext, 0)
    sj.relay(1)
    sw.relay(3, 2, 1)
    so.relay(3, 2)
    se.join_all()
    block = pl.ds(pl.multiple_of(place.e * 64, 64), 64)
    joint_ref[block, :] = sj.total().astype(BF16)
    gj.start()
    block = pl.ds(pl.multiple_of(place.e * 32, 32), 32)
    wo_grad_ref[block, :] = sw.total().astype(BF16)
    gw.start()
    se.relay(3, 2, 1)
    so.relay(1)

    across(10).wait_recv()
    grad_n = (own_part + norm_i[...].astype(F32)) * gain_one_ref[...]
    inputs = tokens_ref[...].astype(F32)
    inv_one = lax.rsqrt(mean_last(inputs * inputs) + EPSILON)
    grad_tokens_ref[...] = (
        grad_tokens_ref[...]
        + inv_one * grad_n
        - inputs * (inv_one * inv_one * inv_one * mean_last(grad_n * inputs))
    )
    gj.arrive(0)
    gj.arrive_over(0)
    gw.arrive(0)
    gw.arrive_over(0)
    block = pl.ds(pl.multiple_of(place.e * 64, 64), 64)
    small_ref[block, :] = se.total()
    ge.start()
    gj.arrive(1)
    gj.arrive_over(1, 2)
    gw.arrive(1)
    gw.arrive_over(1, 2)
    ge.arrive(0)
    ge.arrive_over(0)
    gj.arrive(2)
    gj.arrive_over(3, 4)
    gw.arrive(2)
    gw.arrive_over(3, 4)
    ge.arrive(1)
    ge.arrive_over(1, 2)
    output_ref[...] = (residual[...] + so.total()).astype(BF16)
    gj.arrive_over(5, 6)
    gw.arrive_over(5, 6)
    ge.arrive(2)
    ge.arrive_over(3, 4, 5, 6)
    for tree in (gj, gw, ge):
        tree.from_sib(0, *range(7))
        tree.from_sib(1, *range(7))
    for k in (5, 6, 7):
        across(k).wait_recv()
    for k in (0, 1, 2, 3, 5, 6, 7, 8, 9, 10):
        across(k).wait_send()
    for tree in (so, sj, sw, se):
        tree.sib_sent()
    for tree in (gx, gg, gj, gw, ge, so, sj, sw, se):
        tree.sent()


def layer_call(capacity, *operands):
    vm, dma = pltpu.VMEM, pltpu.SemaphoreType.DMA
    spec = pl.BlockSpec(memory_space=pltpu.VMEM)
    sds = jax.ShapeDtypeStruct

    def body(*refs):
        return layer_kernel(capacity, *refs)

    outs = (
        sds((BLK, WIDTH), BF16),
        sds((BLK, WIDTH), F32),
        sds((WIDTH, WIDTH), BF16),
        sds((HALF, WIDTH), BF16),
        sds((WIDTH, BLK), F32),
        sds((WIDTH, 256), F32),
        sds((WIDTH, 256), F32),
        sds((256, WIDTH), F32),
        sds((WIDTH, 256), BF16),
        sds((WIDTH, 256), BF16),
        sds((256, WIDTH), BF16),
    )
    return pl.pallas_call(
        body,
        out_shape=outs,
        in_specs=[spec] * len(operands),
        out_specs=[spec] * len(outs),
        scratch_shapes=[
            vm((2048, EXT), BF16), vm((2048, WIDTH), BF16),
            vm((WIDTH, 256), BF16), vm((WIDTH, 256), BF16), vm((256, WIDTH), BF16),
            vm((2048, 512), BF16), vm((2048, 512), BF16), vm((2048, 512), BF16),
            vm((8, BLK, EXT), BF16), vm((8, BLK, EXT), BF16), vm((8, BLK, EXT), BF16),
            vm((8, BLK, WIDTH), BF16), vm((8, BLK, WIDTH), BF16), vm((8, BLK, WIDTH), BF16),
            vm((4, BLK, EXT), BF16), vm((3, BLK, EXT), BF16),
            vm((4, BLK, WIDTH), BF16), vm((3, BLK, WIDTH), BF16),
            vm((WIDTH, 256), BF16), vm((WIDTH, 256), BF16), vm((256, WIDTH), BF16),
            vm((256, WIDTH), BF16), vm((256, 256), BF16), vm((256, 256), BF16), vm((256, 512), BF16),
            vm((4, 512, 256), F32), vm((256, 512), BF16),
            vm((BLK, WIDTH), BF16), vm((BLK, WIDTH), BF16), vm((BLK, WIDTH), F32),
            vm((BLK, BLK), F32), vm((BLK, BLK), F32),
            vm((256, WIDTH), BF16), vm((256, WIDTH), BF16),
            vm((BLK, WIDTH), BF16),
            vm((24, WIDTH), F32), vm((24, WIDTH), F32), vm((WIDTH, BLK), F32), vm((512, WIDTH), BF16),
            vm((8, 64, WIDTH), BF16), vm((4, 64, WIDTH), BF16), vm((3, 64, WIDTH), BF16),
            vm((8, 32, WIDTH), BF16), vm((4, 32, WIDTH), BF16), vm((3, 32, WIDTH), BF16),
            vm((8, 64, BLK), F32), vm((8, 64, BLK), F32), vm((8, 64, BLK), F32),
            vm((4, 64, BLK), F32), vm((3, 64, BLK), F32), vm((BLK, WIDTH), BF16),
            dma((5, 27)), dma((5, 27)), dma((5, 7)), dma((5, 7)), dma((5, 8)), dma((5, 8)),
            dma((11,)), dma((11,)),
        ],
        compiler_params=pltpu.CompilerParams(
            collective_id=1, has_side_effects=True, vmem_limit_bytes=63 * 2**20
        ),
        cost_estimate=pl.CostEstimate(flops=24 * 10**9, bytes_accessed=10**7, transcendentals=10**6),
        name="layer",
    )(*operands)


def finish_kernel(
    joint_ref, wo_ref, small_ref, gate_ref, up_ref, down_ref, gate_i, up_i, down_i,
    query_out, key_out, value_out, wo_out, small_out, gate_out, up_out, down_out,
):
    query_out[...] = joint_ref[:, :512].astype(F32)
    key_out[...] = joint_ref[:, 512:768].astype(F32)
    value_out[...] = joint_ref[:, 768:].astype(F32)
    wo_out[...] = wo_ref[...].astype(F32)
    small_out[...] = small_ref[...].T[:24, :]
    gate_out[...] = gate_ref[...] + gate_i[...].astype(F32)
    up_out[...] = up_ref[...] + up_i[...].astype(F32)
    down_out[...] = down_ref[...] + down_i[...].astype(F32)


def finish_call(*operands):
    steps = 4
    sds = jax.ShapeDtypeStruct

    def rows(shape):
        return pl.BlockSpec((shape[0] // steps, shape[1]), lambda i: (i, 0))

    outs = (
        (WIDTH, 512), (WIDTH, 256), (WIDTH, 256), (HALF, WIDTH), (24, WIDTH),
        (WIDTH, 256), (WIDTH, 256), (256, WIDTH),
    )
    out_specs = [rows(shape) for shape in outs]
    out_specs[4] = pl.BlockSpec((24, WIDTH // steps), lambda i: (0, i))
    return pl.pallas_call(
        finish_kernel,
        out_shape=tuple(sds(shape, F32) for shape in outs),
        grid=(steps,),
        in_specs=[rows(a.shape) for a in operands],
        out_specs=out_specs,
        compiler_params=pltpu.CompilerParams(vmem_limit_bytes=40 * 2**20),
        cost_estimate=pl.CostEstimate(flops=10**6, bytes_accessed=18 * 10**6, transcendentals=0),
        name="finish",
    )(*operands)


def tables(rows):
    half = HEAD_DIM // 2
    freqs = np.exp(np.arange(half, dtype=np.float32) * np.float32(-2.0 * math.log(THETA_BASE) / HEAD_DIM))
    angles = np.arange(rows, dtype=np.float32)[:, None] * freqs[None, :]
    cos, sin = np.cos(angles), np.sin(angles)
    return (
        np.concatenate([cos] * 4, 1).astype(np.float32),
        np.concatenate([-sin, sin] * 2, 1).astype(np.float32),
    )


def on_device(
    tokens,
    gain_attn,
    w_query,
    w_key,
    w_value,
    w_out,
    gain_moe,
    router,
    expert_gate,
    expert_up,
    expert_down,
    routes,
    fill_order,
    cotangent,
):
    tok_rows, width = tokens.shape
    tensor_size = lax.axis_size("tensor")
    seq_rows = tok_rows * tensor_size
    head_size = HEAD_DIM
    q_cols = w_query.shape[1]
    kv_cols = w_key.shape[1]
    q_heads = q_cols // head_size
    kv_heads = kv_cols // head_size
    q_group = q_heads // kv_heads
    score_scale = head_size ** (-0.5)
    local_experts = expert_gate.shape[0]
    expert_groups = lax.axis_size("expert")
    experts = local_experts * expert_groups
    top_k = routes.shape[1]
    capacity = (5 * tok_rows * top_k + 4 * experts - 1) // (4 * experts)
    gate_w, up_w, down_w = (expert_gate, expert_up, expert_down)
    inputs = tokens.astype(jnp.float32)
    inv_one = lax.rsqrt(jnp.mean(inputs * inputs, -1, keepdims=True) + EPSILON)
    normed = (inputs * inv_one * gain_attn).astype(jnp.bfloat16)
    normed_all = lax.all_gather(normed, "tensor", axis=0, tiled=True)
    w_joint = jnp.concatenate([w_query, w_key, w_value], 1)
    joint = jnp.dot(normed_all, w_joint, preferred_element_type=jnp.float32)
    angles = angles_of(seq_rows, head_size)
    queries = rotate(joint[:, :q_cols].reshape(seq_rows, q_heads, head_size), angles, 1.0).astype(
        jnp.bfloat16
    )
    key_rows = rotate(
        joint[:, q_cols : q_cols + kv_cols].reshape(seq_rows, kv_heads, head_size), angles, 1.0
    ).astype(jnp.bfloat16)
    value_rows = (
        joint[:, q_cols + kv_cols :].astype(jnp.bfloat16).reshape(seq_rows, kv_heads, head_size)
    )
    q_size = min(512, seq_rows)
    blocks = seq_rows // q_size
    key_pos = jnp.arange(seq_rows)

    def scores_of(q_block, row_start):
        grouped = q_block.reshape(q_size, kv_heads, q_group, head_size)
        raw_scores = (
            jnp.einsum("qkgd,tkd->kgqt", grouped, key_rows, preferred_element_type=jnp.float32)
            * score_scale
        )
        allowed = (row_start + jnp.arange(q_size))[:, None] >= key_pos[None, :]
        return (grouped, jnp.where(allowed, raw_scores, MASKED))

    def forward_block(block_args):
        q_block, row_start = block_args
        grouped, scores = scores_of(q_block, row_start)
        top_score = jnp.max(scores, -1, keepdims=True)
        exp_scores = jnp.exp(scores - top_score)
        row_total = jnp.sum(exp_scores, -1, keepdims=True)
        attn_probs = (exp_scores / row_total).astype(jnp.bfloat16)
        mixed_rows = jnp.einsum(
            "kgqt,tkd->qkgd", attn_probs, value_rows, preferred_element_type=jnp.float32
        )
        return (mixed_rows.astype(jnp.bfloat16).reshape(q_size, q_cols), top_score, row_total)

    q_blocks = queries.reshape(blocks, q_size, q_heads, head_size)
    starts = jnp.arange(blocks) * q_size
    attended, maxima, totals = lax.map(forward_block, (q_blocks, starts))
    attended = attended.reshape(seq_rows, q_cols)
    row_block = attended
    branch = lax.psum_scatter(
        jnp.dot(row_block, w_out, preferred_element_type=jnp.float32),
        "tensor",
        scatter_dimension=0,
        tiled=True,
    )
    residual = inputs + branch
    inv_two = lax.rsqrt(jnp.mean(residual * residual, -1, keepdims=True) + EPSILON)
    scaled = residual * inv_two
    moe_in = (scaled * gain_moe).astype(jnp.bfloat16)
    logits = jnp.dot(moe_in, router, preferred_element_type=jnp.float32)
    expert_ids = jnp.arange(experts, dtype=jnp.int32)
    named = jnp.sum((routes[:, :, None] == expert_ids[None, None, :]).astype(jnp.float32), 1)
    place_of = (fill_order[0][:, None] == jnp.arange(tok_rows)[None, :]).astype(jnp.bfloat16)
    ordered = jnp.dot(place_of, named.astype(jnp.bfloat16), preferred_element_type=jnp.float32)
    earlier = (jnp.arange(tok_rows)[:, None] > jnp.arange(tok_rows)[None, :]).astype(jnp.bfloat16)
    before = jnp.dot(earlier, ordered.astype(jnp.bfloat16), preferred_element_type=jnp.float32)
    rank = contract_first(place_of, before.astype(jnp.bfloat16))
    kept = named * (rank < capacity).astype(jnp.float32)
    top_logit = jnp.max(jnp.where(named > 0, logits, MASKED), -1, keepdims=True)
    exp_logits = jnp.where(named > 0, jnp.exp(jnp.minimum(logits - top_logit, 0.0)), 0.0)
    gates = exp_logits / jnp.sum(exp_logits, -1, keepdims=True)
    weights = gates * kept

    gate_all = lax.all_gather(gate_w[0], "tensor", axis=1, tiled=True)
    up_all = lax.all_gather(up_w[0], "tensor", axis=1, tiled=True)
    down_all = lax.all_gather(down_w[0], "tensor", axis=0, tiled=True)
    grad_out = cotangent.astype(jnp.float32)
    plane_cot = lax.all_gather(cotangent, "expert", axis=0, tiled=True)
    plane_in = lax.all_gather(moe_in, "expert", axis=0, tiled=True)
    plane_weights = lax.all_gather(weights, "expert", axis=0, tiled=True)
    mine = (expert_ids == lax.axis_index("expert")).astype(jnp.float32)
    my_weight = jnp.sum(plane_weights * mine[None, :], -1, keepdims=True)

    gate_pre = jnp.dot(plane_in, gate_all, preferred_element_type=jnp.float32)
    up_pre = jnp.dot(plane_in, up_all, preferred_element_type=jnp.float32)
    back_down = contract_last(plane_cot, down_all)
    gate_sigmoid = jax.nn.sigmoid(gate_pre)
    active = gate_pre * gate_sigmoid
    hidden = active * up_pre
    pair_grad = jnp.sum(hidden * back_down, -1, keepdims=True)
    hidden_w = (hidden * my_weight).astype(jnp.bfloat16)
    grad_hidden = back_down * my_weight
    grad_gate_pre = (
        grad_hidden * up_pre * gate_sigmoid * (1.0 + gate_pre * (1.0 - gate_sigmoid))
    ).astype(jnp.bfloat16)
    grad_up_pre = (grad_hidden * active).astype(jnp.bfloat16)
    out_part = jnp.dot(hidden_w, down_all, preferred_element_type=jnp.float32)
    in_part = contract_last(grad_gate_pre, gate_all) + contract_last(grad_up_pre, up_all)
    out_sum = lax.psum_scatter(
        out_part.astype(jnp.bfloat16), "expert", scatter_dimension=0, tiled=True
    )
    in_sum = lax.psum_scatter(
        in_part.astype(jnp.bfloat16), "expert", scatter_dimension=0, tiled=True
    )
    grad_gates = lax.psum_scatter(
        pair_grad * mine[None, :], "expert", scatter_dimension=0, tiled=True
    ) * kept
    grad_down = lax.psum_scatter(
        contract_first(hidden_w, plane_cot).astype(jnp.bfloat16),
        "tensor", scatter_dimension=0, tiled=True,
    ).astype(jnp.float32)[None]
    grad_gate = lax.psum_scatter(
        contract_first(plane_in, grad_gate_pre).astype(jnp.bfloat16),
        "tensor", scatter_dimension=1, tiled=True,
    ).astype(jnp.float32)[None]
    grad_up = lax.psum_scatter(
        contract_first(plane_in, grad_up_pre).astype(jnp.bfloat16),
        "tensor", scatter_dimension=1, tiled=True,
    ).astype(jnp.float32)[None]
    output_rows = residual + out_sum.astype(jnp.float32)
    grad_logits = (
        gates * (grad_gates - jnp.sum(gates * grad_gates, -1, keepdims=True))
    ).astype(jnp.bfloat16)
    grad_moe_in = in_sum.astype(jnp.float32) + contract_last(grad_logits, router)
    grad_router = contract_first(moe_in, grad_logits)
    grad_gain_moe = jnp.sum(grad_moe_in * scaled, 0)
    grad_norm_two = grad_moe_in * gain_moe
    grad_residual = (
        grad_out
        + inv_two * grad_norm_two
        - residual * inv_two**3 * jnp.mean(grad_norm_two * residual, -1, keepdims=True)
    )
    grad_branch = grad_residual.astype(jnp.bfloat16)
    shard_piece = lax.all_gather(grad_branch, "tensor", axis=0, tiled=True)
    grad_part = contract_last(shard_piece, w_out).astype(jnp.bfloat16)
    grad_mixed = grad_part
    grad_wout = contract_first(attended, shard_piece)
    grad_mixed, grad_w_out = (grad_mixed, grad_wout)
    grad_blocks = grad_mixed.reshape(blocks, q_size, q_heads, head_size)

    def backward_block(carry, block_args):
        grad_keys, grad_values = carry
        q_block, grad_block, row_start, top_score, row_total = block_args
        grouped, scores = scores_of(q_block, row_start)
        attn_probs = jnp.exp(scores - top_score) / row_total
        grad_grouped = grad_block.reshape(q_size, kv_heads, q_group, head_size)
        grad_probs = jnp.einsum(
            "qkgd,tkd->kgqt", grad_grouped, value_rows, preferred_element_type=jnp.float32
        )
        grad_values = grad_values + jnp.einsum(
            "kgqt,qkgd->tkd",
            attn_probs.astype(jnp.bfloat16),
            grad_grouped,
            preferred_element_type=jnp.float32,
        )
        grad_scores = (
            attn_probs
            * (grad_probs - jnp.sum(attn_probs * grad_probs, -1, keepdims=True))
            * score_scale
        ).astype(jnp.bfloat16)
        grad_query = jnp.einsum(
            "kgqt,tkd->qkgd", grad_scores, key_rows, preferred_element_type=jnp.float32
        ).reshape(q_size, q_heads, head_size)
        grad_keys = grad_keys + jnp.einsum(
            "kgqt,qkgd->tkd", grad_scores, grouped, preferred_element_type=jnp.float32
        )
        return ((grad_keys, grad_values), grad_query)

    zero_rows = jnp.zeros((seq_rows, kv_heads, head_size), jnp.float32)
    (grad_keys, grad_values), grad_queries = lax.scan(
        backward_block, (zero_rows, zero_rows), (q_blocks, grad_blocks, starts, maxima, totals)
    )
    grad_queries = grad_queries.reshape(seq_rows, q_heads, head_size)
    grad_q = rotate(grad_queries, angles, -1.0).astype(jnp.bfloat16).reshape(seq_rows, q_cols)
    grad_k = rotate(grad_keys, angles, -1.0).astype(jnp.bfloat16).reshape(seq_rows, kv_cols)
    grad_v = grad_values.astype(jnp.bfloat16).reshape(seq_rows, kv_cols)
    grad_joint = jnp.concatenate([grad_q, grad_k, grad_v], 1)
    grad_w_joint = contract_first(normed_all, grad_joint)
    row_block = grad_joint
    grad_normed = lax.psum_scatter(
        contract_last(row_block, w_joint), "tensor", scatter_dimension=0, tiled=True
    )
    grad_gain_attn = jnp.sum(grad_normed * inputs * inv_one, 0)
    grad_norm_one = grad_normed * gain_attn
    grad_tokens = (
        grad_residual
        + inv_one * grad_norm_one
        - inputs * inv_one**3 * jnp.mean(grad_norm_one * inputs, -1, keepdims=True)
    )
    summed_joint, summed_out = lax.psum((grad_w_joint, grad_w_out), "expert")
    summed_gain_attn, summed_gain_moe, summed_router = lax.psum(
        (grad_gain_attn, grad_gain_moe, grad_router), ("expert", "tensor")
    )
    return (
        output_rows.astype(jnp.bfloat16),
        grad_tokens,
        summed_gain_attn,
        summed_joint[:, :q_cols],
        summed_joint[:, q_cols : q_cols + kv_cols],
        summed_joint[:, q_cols + kv_cols :],
        summed_out,
        summed_gain_moe,
        summed_router,
        grad_gate,
        grad_up,
        grad_down,
    )


def by_kernel(
    tokens,
    gain_attn,
    w_query,
    w_key,
    w_value,
    w_out,
    gain_moe,
    router,
    expert_gate,
    expert_up,
    expert_down,
    routes,
    fill_order,
    cotangent,
):
    tok_rows = tokens.shape[0]
    experts = router.shape[1]
    capacity = (5 * tok_rows * routes.shape[1] + 4 * experts - 1) // (4 * experts)
    cos, sin = tables(tok_rows * 2)
    out, grad_tokens, joint, wo_grad, small, *expert_grads = layer_call(
        capacity,
        tokens, cotangent, gain_attn[None], gain_moe[None], w_query, w_key, w_value, w_out,
        router.T, routes.T, fill_order, jnp.asarray(cos), jnp.asarray(sin),
        expert_gate[0], expert_up[0], expert_down[0],
    )
    gq, gk, gv, gwo, small, ggate, gup, gdown = finish_call(joint, wo_grad, small, *expert_grads)
    return (
        out,
        grad_tokens,
        small[experts + 1],
        gq,
        gk,
        gv,
        gwo,
        small[experts],
        small[:experts].T,
        ggate[None],
        gup[None],
        gdown[None],
    )


def kernel_fits(mesh_shape, shapes):
    return mesh_shape == (16, 2) and shapes == (
        (128, 1024), (1024,), (1024, 512), (1024, 256), (1024, 256), (512, 1024), (1024,), (1024, 16),
        (1, 1024, 256), (1, 1024, 256), (1, 256, 1024), (128, 8), (1, 128), (128, 1024),
    )


def on_any(*operands):
    sizes = (lax.axis_size("expert"), lax.axis_size("tensor"))
    if kernel_fits(sizes, tuple(a.shape for a in operands)):
        return by_kernel(*operands)
    return on_device(*operands)


def solution(mesh):
    placed = (
        P(("expert", "tensor"), None),
        P(),
        P(None, "tensor"),
        P(None, "tensor"),
        P(None, "tensor"),
        P("tensor", None),
        P(),
        P(),
        P("expert", None, "tensor"),
        P("expert", None, "tensor"),
        P("expert", "tensor", None),
        P(("expert", "tensor"), None),
        P(("expert", "tensor"), None),
        P(("expert", "tensor"), None),
    )
    return jax.shard_map(
        on_any,
        mesh=mesh,
        in_specs=placed,
        out_specs=(
            P(("expert", "tensor"), None),
            P(("expert", "tensor"), None),
            P(),
            P(None, "tensor"),
            P(None, "tensor"),
            P(None, "tensor"),
            P("tensor", None),
            P(),
            P(),
            P("expert", None, "tensor"),
            P("expert", None, "tensor"),
            P("expert", "tensor", None),
        ),
        check_vma=False,
    )
```

```python
import math

import jax
import jax.numpy as jnp
import numpy as np
from jax import lax
from jax.experimental import pallas as pl
from jax.experimental.pallas import tpu as pltpu
from jax.sharding import PartitionSpec as P

HEAD_DIM = 64


EPSILON = 1e-06
THETA_BASE = 10000.0
MASKED = -1e30


def angles_of(row_count, head_size):
    half = head_size // 2
    freqs = jnp.exp(jnp.arange(half, dtype=jnp.float32) * (-2.0 * math.log(THETA_BASE) / head_size))
    return jnp.arange(row_count, dtype=jnp.float32)[:, None] * freqs[None, :]


def rotate(vectors, angles, sign):
    half = vectors.shape[-1] // 2
    cosine = jnp.cos(angles)[:, None, :]
    sine = sign * jnp.sin(angles)[:, None, :]
    first = vectors[..., :half]
    second = vectors[..., half:]
    return jnp.concatenate([first * cosine - second * sine, second * cosine + first * sine], -1)


def contract_last(left, right):
    return lax.dot_general(
        left, right, (((1,), (1,)), ((), ())), preferred_element_type=jnp.float32
    )


def contract_first(left, right):
    return lax.dot_general(
        left, right, (((0,), (0,)), ((), ())), preferred_element_type=jnp.float32
    )


F32 = jnp.float32
BF16 = jnp.bfloat16
MESH = pl.DeviceIdType.MESH
BLK = 128
WIDTH = 1024
EXT = 1152
HALF = 512
NEAREST = (0, 1, 2, 3, 1, 0, 2, 3, 2, 3, 1, 0, 3, 2, 1, 0)
EXPERT_ORDER = ((0, 0), (1, 1), (1, 0), (0, 1), (3, 1), (3, 0), (2, 1), (2, 0))
PAIR_FIRST = ((3, 1), (2, 1), (1, 1), (0, 1), (3, 0), (2, 0), (1, 0), (0, 0))


def pick(i, values):
    out = jnp.int32(values[-1])
    for n in range(len(values) - 2, -1, -1):
        out = jnp.where(i == n, jnp.int32(values[n]), out)
    return out


class Place:
    def __init__(self):
        e = lax.axis_index("expert")
        t = lax.axis_index("tensor")
        self.e = e
        self.t = t
        self.core = lax.rem(e, 2)
        self.pair = lax.rem(e // 2, 2)
        self.ring = e // 4
        self.other = (e + 2 - 4 * self.pair, t)
        self.sib = (e + 1 - 2 * self.core, t)
        self.across = (e, 1 - t)

    def at(self, ring):
        return (ring * 4 + lax.rem(self.e, 4), self.t)

    def chip(self, ring, other):
        return ring * 2 + (self.pair + other - 2 * self.pair * other)

    def step(self, i, order):
        ring = self.near(pick(i, [k for k, _ in order]))
        return ring, pick(i, [other for _, other in order])

    def near(self, k):
        return pick(self.ring * 4 + k, NEAREST)

    def barrier(self):
        bar = pltpu.get_barrier_semaphore()
        for dest in [self.at(lax.rem(self.ring + m, 4)) for m in (1, 2, 3)] + [
            self.other, self.sib, self.across,
        ]:
            pl.semaphore_signal(bar, inc=1, device_id=dest, device_id_type=MESH)
        pl.semaphore_wait(bar, 6)


def if_(condition, action):
    if condition is True:
        action()
    else:
        pl.when(condition)(action)


class Gather:
    def __init__(self, place, buf, send_sems, recv_sems):
        self.place, self.buf, self.ss, self.rs = place, buf, send_sems, recv_sems
        self.size = buf.shape[0] // 16

    def where(self, n):
        r = self.place.ring
        if n == 0:
            return r, True
        j = (n - 1) // 2
        return (r - 1 - j, r > j) if n % 2 else (r + 1 + j, 3 - r > j)

    def copy(self, ring, other, core, sem, dest):
        block = self.place.chip(ring, other) * 2 + core
        ref = self.buf.at[pl.ds(pl.multiple_of(block * self.size, self.size), self.size)]
        return pltpu.make_async_remote_copy(
            src_ref=ref, dst_ref=ref, send_sem=self.ss.at[sem], recv_sem=self.rs.at[sem],
            device_id=dest, device_id_type=MESH,
        )

    def up(self, k):
        r = self.place.ring
        return self.copy(r - k, 0, self.place.core, k, self.place.at(r + 1))

    def down(self, k):
        r = self.place.ring
        return self.copy(r + k, 0, self.place.core, 3 + k, self.place.at(r - 1))

    def over(self, n, arriving=0):
        return self.copy(self.where(n)[0], arriving, self.place.core, 6 + n, self.place.other)

    def to_sib(self, n, other, arriving=False):
        core = 1 - self.place.core if arriving else self.place.core
        return self.copy(self.where(n)[0], other, core, 13 + 7 * other + n, self.place.sib)

    def start(self):
        r = self.place.ring
        if_(r < 3, lambda: self.up(0).start())
        if_(r > 0, lambda: self.down(0).start())
        self.over(0).start()
        self.to_sib(0, 0).start()

    def arrive(self, j):
        r = self.place.ring

        def from_below():
            self.copy(r - 1 - j, 0, self.place.core, j, self.place.other).wait_recv()
            if j < 2:
                if_(r < 3, lambda: self.up(j + 1).start())
            self.over(1 + 2 * j).start()
            self.to_sib(1 + 2 * j, 0).start()

        def from_above():
            self.copy(r + 1 + j, 0, self.place.core, 3 + j, self.place.other).wait_recv()
            if j < 2:
                if_(r > 0, lambda: self.down(j + 1).start())
            self.over(2 + 2 * j).start()
            self.to_sib(2 + 2 * j, 0).start()

        if_(r > j, from_below)
        if_(3 - r > j, from_above)

    def arrive_over(self, *numbers):
        for n in numbers:

            def taken(n=n):
                self.over(n, 1).wait_recv()
                self.to_sib(n, 1).start()

            if_(self.where(n)[1], taken)

    def from_sib(self, other, *numbers):
        for n in numbers:
            if_(self.where(n)[1], lambda n=n: self.to_sib(n, other, True).wait_recv())

    def sent(self):
        r = self.place.ring
        for k in range(3):
            if_((r < 3) & (r >= k), lambda k=k: self.up(k).wait_send())
            if_((r > 0) & (3 - r >= k), lambda k=k: self.down(k).wait_send())
        for n in range(7):

            def all_of(n=n):
                self.over(n).wait_send()
                self.to_sib(n, 0).wait_send()
                self.to_sib(n, 1).wait_send()

            if_(self.where(n)[1], all_of)


class GatherDirect(Gather):
    def span(self, k, sending):
        ring = self.place.near(k)
        r = self.place.ring
        m = lax.rem((ring - r if sending else r - ring) + 4, 4)
        source = r if sending else ring
        return self.copy(source, 0, self.place.core, m - 1, self.place.at(ring))

    def over(self, k, arriving=0):
        return self.copy(self.place.near(k), arriving, self.place.core, 3 + k, self.place.other)

    def to_sib(self, k, other, arriving=False):
        core = 1 - self.place.core if arriving else self.place.core
        return self.copy(self.place.near(k), other, core, 7 + 4 * other + k, self.place.sib)

    def start(self):
        for k in (1, 2, 3):
            self.span(k, True).start()
        self.over(0).start()
        self.to_sib(0, 0).start()

    def arrive(self, *ks):
        for k in ks:
            self.span(k, False).wait_recv()
            self.over(k).start()
            self.to_sib(k, 0).start()

    def arrive_over(self, *ks):
        for k in ks:
            self.over(k, 1).wait_recv()
            self.to_sib(k, 1).start()

    def from_sib(self):
        for other in range(2):
            for k in range(4):
                self.to_sib(k, other, True).wait_recv()

    def sent(self):
        for k in range(4):
            if k:
                self.span(k, True).wait_send()
            self.over(k).wait_send()
            self.to_sib(k, 0).wait_send()
            self.to_sib(k, 1).wait_send()


class Scatter:
    def __init__(self, place, sums, theirs, from_sib, over, along, sib_ss, sib_rs, ss, rs):
        self.place, self.sums, self.theirs, self.from_sib = place, sums, theirs, from_sib
        self.over, self.along = over, along
        self.sib_ss, self.sib_rs, self.ss, self.rs = sib_ss, sib_rs, ss, rs

    def sib_copy(self, i):
        return pltpu.make_async_remote_copy(
            src_ref=self.theirs.at[i], dst_ref=self.from_sib.at[i],
            send_sem=self.sib_ss.at[i], recv_sem=self.sib_rs.at[i],
            device_id=self.place.sib, device_id_type=MESH,
        )

    def join(self, i):
        self.sib_copy(i).wait_recv()
        total = self.sums[i].astype(F32) + self.from_sib[i].astype(F32)
        self.sums[i] = total.astype(self.from_sib.dtype)

    def join_all(self):
        for k, other in PAIR_FIRST:
            ring = self.place.near(k)
            self.join(other * 4 + ring)
            if other:
                self.over_copy(ring).start()

    def over_copy(self, ring):
        return pltpu.make_async_remote_copy(
            src_ref=self.sums.at[4 + ring], dst_ref=self.over.at[ring],
            send_sem=self.ss.at[ring], recv_sem=self.rs.at[ring],
            device_id=self.place.other, device_id_type=MESH,
        )

    def along_copy(self, k, ring, slot):
        return pltpu.make_async_remote_copy(
            src_ref=self.sums.at[self.place.near(k)], dst_ref=self.along.at[slot],
            send_sem=self.ss.at[3 + k], recv_sem=self.rs.at[4 + slot],
            device_id=self.place.at(ring), device_id_type=MESH,
        )

    def relay(self, *ks):
        r = self.place.ring
        at_end = (r == 0) | (r == 3)
        beside = self.place.near(1)
        for k in ks:
            ring = self.place.near(k)

            def add(*others, ring=ring):
                total = self.sums[ring].astype(F32)
                for other in others:
                    total = total + other.astype(F32)
                self.sums[ring] = total.astype(self.over.dtype)

            self.over_copy(ring).wait_recv()
            if k == 1:
                add(self.over[ring])
                self.along_copy(1, ring, 0).start()
                continue

            @pl.when(at_end)
            def _(k=k, ring=ring):
                add(self.over[ring])
                self.along_copy(k, beside, k).start()

            @pl.when(jnp.logical_not(at_end))
            def _(k=k, ring=ring):
                self.along_copy(k, beside, k).wait_recv()
                add(self.over[ring], self.along[k])
                self.along_copy(k, ring, 1).start()

    def total(self):
        ring = self.place.ring
        self.over_copy(ring).wait_recv()
        for slot in (0, 1):
            self.along_copy(1, self.place.near(1), slot).wait_recv()
        return (self.sums[ring].astype(F32) + self.over[ring].astype(F32)) + (
            self.along[0].astype(F32) + self.along[1].astype(F32)
        )

    def sib_sent(self):
        for i in range(8):
            self.sib_copy(i).wait_send()

    def sent(self):
        for ring in range(4):
            self.over_copy(ring).wait_send()
        for k in (1, 2, 3):
            self.along_copy(k, self.place.near(k), 0).wait_send()


def dot_nn(a, b):
    return lax.dot_general(a, b, (((1,), (0,)), ((), ())), preferred_element_type=F32)


def dot_nt(a, b):
    return lax.dot_general(a, b, (((1,), (1,)), ((), ())), preferred_element_type=F32)


def dot_tn(a, b):
    return lax.dot_general(a, b, (((0,), (0,)), ((), ())), preferred_element_type=F32)


def expert_step(place, ring, other, x, g, gates_w, ups_w, downs_w, hid, dgate, dup, in_s, in_t, out_s, out_t):
    i = other * 4 + ring
    rows = pl.ds(pl.multiple_of(place.chip(ring, other) * 256, 256), 256)
    lane = lax.broadcasted_iota(jnp.int32, (256, 128), 1)
    high, low = lane == place.e, lane == place.e + 16
    weight = jnp.sum(
        jnp.where(high | low, x[rows, WIDTH:EXT].astype(F32), 0.0), -1, keepdims=True
    )
    pair_grad = jnp.zeros((256, 1), F32)
    for h in range(2):
        cols = slice(h * 256, (h + 1) * 256)
        gate_pre = dot_nn(x[rows, :WIDTH], gates_w[h][...])
        up_pre = dot_nn(x[rows, :WIDTH], ups_w[h][...])
        back = dot_nt(g[rows, :], downs_w[h][...])
        sig = jax.nn.sigmoid(gate_pre)
        act = gate_pre * sig
        hidden = act * up_pre
        pair_grad = pair_grad + jnp.sum(hidden * back, -1, keepdims=True)
        grad_hidden = back * weight
        hid[rows, cols] = (hidden * weight).astype(BF16)
        dgate[rows, cols] = (grad_hidden * up_pre * (sig + act * (1.0 - sig))).astype(BF16)
        dup[rows, cols] = (grad_hidden * act).astype(BF16)
    coarse = pair_grad.astype(BF16).astype(F32)
    ext = jnp.where(high, coarse, jnp.where(low, pair_grad - coarse, 0.0))
    put(place, i, in_s, in_t, slice(WIDTH, EXT), ext)
    for n in range(4):
        cols = slice(n * 256, (n + 1) * 256)
        value = (
            dot_nt(dgate[rows, 0:256], gates_w[0][cols, :])
            + dot_nt(dgate[rows, 256:512], gates_w[1][cols, :])
            + dot_nt(dup[rows, 0:256], ups_w[0][cols, :])
            + dot_nt(dup[rows, 256:512], ups_w[1][cols, :])
        )
        put(place, i, in_s, in_t, cols, value)
    for n in range(4):
        cols = slice(n * 256, (n + 1) * 256)
        value = dot_nn(hid[rows, 0:256], downs_w[0][:, cols]) + dot_nn(
            hid[rows, 256:512], downs_w[1][:, cols]
        )
        put(place, i, out_s, out_t, cols, value)


def put(place, i, ours, theirs, cols, value):
    half = value.shape[0] // 2
    first, second = value[:half], value[half:]
    is_first = place.core == 0
    ours[i, :, cols] = jnp.where(is_first, first, second).astype(ours.dtype)
    theirs[i, :, cols] = jnp.where(is_first, second, first).astype(theirs.dtype)


def mean_last(v):
    return jnp.sum(v, -1, keepdims=True) * (1.0 / v.shape[-1])


def swapped(v):
    lane = lax.broadcasted_iota(jnp.int32, v.shape, 1)
    return jnp.where(lax.rem(lane, 64) < 32, pltpu.roll(v, 96, 1), pltpu.roll(v, 32, 1))


def doubled(v, half):
    lane = lax.broadcasted_iota(jnp.int32, v.shape, 1)
    one = jnp.where((lane < 64) == (half == 0), v, 0.0)
    return one + pltpu.roll(one, 64, 1)


def stacked(v):
    lane = lax.broadcasted_iota(jnp.int32, v.shape, 1)
    return jnp.concatenate([jnp.where(lane < 64, v, 0.0), jnp.where(lane < 64, 0.0, v)], 0)


def unstacked(v):
    rows = v.shape[0] // 2
    lane = lax.broadcasted_iota(jnp.int32, (rows, 128), 1)
    return jnp.where(lane < 64, v[:rows], v[rows:])


def layer_kernel(
    capacity,
    tokens_ref, cot_ref, gain_one_ref, gain_two_ref, wq_ref, wk_ref, wv_ref, wo_ref, router_ref,
    routes_ref, fill_ref, cos_ref, sin_ref, gate_ref, up_ref, down_ref,
    output_ref, grad_tokens_ref, joint_ref, wo_grad_ref, small_ref,
    ggate_ref, gup_ref, gdown_ref, gate_i, up_i, down_i,
    x, g, gate_p, up_p, down_p, hid, dgate, dup,
    in_s, in_t, in_f, out_s, out_t, out_f, in_1, in_2, out_1, out_2, gate_o, up_o, down_o,
    normed, keys, values, queries, probs, attended, branch_o, branch_i, residual, gates_s, kept_s,
    branch_grad, joint_grad, ext_o, ext_t, small_o, small_i, wo_part,
    j_f, j_1, j_2, w_f, w_1, w_2, e_s, e_t, e_f, e_1, e_2, wide_router,
    ag_ss, ag_rs, sc_ss, sc_rs, sib_ss, sib_rs, y_ss, y_rs,
):
    place = Place()
    mine = pl.ds(pl.multiple_of(place.e * BLK, BLK), BLK)
    own = pl.ds(pl.multiple_of(place.t * BLK, BLK), BLK)
    peers = pl.ds(pl.multiple_of((1 - place.t) * BLK, BLK), BLK)
    gx = Gather(place, x, ag_ss.at[0], ag_rs.at[0])
    gg = Gather(place, g, ag_ss.at[1], ag_rs.at[1])
    gj = Gather(place, joint_ref, ag_ss.at[2], ag_rs.at[2])
    gw = Gather(place, wo_grad_ref, ag_ss.at[3], ag_rs.at[3])
    ge = GatherDirect(place, small_ref, ag_ss.at[4], ag_rs.at[4])

    def scatter(n, *refs):
        return Scatter(place, *refs, sib_ss.at[n], sib_rs.at[n], sc_ss.at[n], sc_rs.at[n])

    si = scatter(0, in_s, in_t, in_f, in_1, in_2)
    so = scatter(1, out_s, out_t, out_f, out_1, out_2)
    narrow = lambda ref, start, size, lanes: ref.at[:, pl.ds(start, size), pl.ds(0, lanes)]
    sj = scatter(2, narrow(in_s, 0, 64, WIDTH), narrow(in_t, 0, 64, WIDTH), j_f, j_1, j_2)
    se = scatter(4, e_s, e_t, e_f, e_1, e_2)
    sw = scatter(3, narrow(in_s, 64, 32, WIDTH), narrow(in_t, 64, 32, WIDTH), w_f, w_1, w_2)

    def across(k):
        src, dst = {
            0: (normed.at[own], normed.at[own]),
            1: (gate_ref, gate_p),
            2: (up_ref, up_p),
            3: (down_ref, down_p),
            4: (branch_o, branch_i),
            5: (gate_o, gate_i),
            6: (up_o, up_i),
            7: (down_o, down_i),
            8: (branch_grad.at[own], branch_grad.at[own]),
            9: (small_o, small_i),
            10: (branch_o, branch_i),
        }[k]
        return pltpu.make_async_remote_copy(
            src_ref=src, dst_ref=dst, send_sem=y_ss.at[k], recv_sem=y_rs.at[k],
            device_id=place.across, device_id_type=MESH,
        )

    def arrived(k):
        ref = {0: normed, 8: branch_grad}.get(k)
        if ref is None:
            across(k).wait_recv()
        else:
            pltpu.make_async_remote_copy(
                src_ref=ref.at[peers], dst_ref=ref.at[peers], send_sem=y_ss.at[k],
                recv_sem=y_rs.at[k], device_id=place.across, device_id_type=MESH,
            ).wait_recv()

    g[mine, :] = cot_ref[...]
    inputs = tokens_ref[...].astype(F32)
    inv_one = lax.rsqrt(mean_last(inputs * inputs) + EPSILON)
    normed[own, :] = (inputs * inv_one * gain_one_ref[...]).astype(BF16)
    place.barrier()
    across(0).start()
    gg.start()

    lane = lax.broadcasted_iota(jnp.int32, (BLK, BLK), 1)
    row = lax.broadcasted_iota(jnp.int32, (BLK, BLK), 0)
    named = jnp.zeros((BLK, BLK), F32)
    routes = routes_ref[...]
    for j in range(routes.shape[0]):
        named = named + (routes[j : j + 1, :] == row).astype(F32)
    named = named.T
    wide_router[0 : router_ref.shape[0], :] = router_ref[...]
    wide_router[router_ref.shape[0] :, :] = jnp.zeros((BLK - router_ref.shape[0], WIDTH), BF16)
    place_of = (fill_ref[...] == row).astype(F32).astype(BF16)
    ordered = dot_tn(place_of, named.astype(BF16))
    earlier = (row > lane).astype(F32).astype(BF16)
    before = dot_nn(earlier, ordered.astype(BF16))
    rank = dot_nn(place_of, before.astype(BF16))
    kept = jnp.where(rank < capacity, named, 0.0)
    kept_s[...] = kept

    def project(rows):
        cos, sin = cos_ref[rows, :], sin_ref[rows, :]
        for n in range(2):
            part = dot_nn(normed[rows, :], wq_ref[:, n * 256 : (n + 1) * 256])
            for m in range(2):
                one = part[:, m * 128 : (m + 1) * 128]
                queries[rows, n * 256 + m * 128 : n * 256 + (m + 1) * 128] = (
                    one * cos + swapped(one) * sin
                ).astype(BF16)
        part = dot_nn(normed[rows, :], wk_ref[...])
        for m in range(2):
            one = part[:, m * 128 : (m + 1) * 128]
            keys[rows, m * 128 : (m + 1) * 128] = (one * cos + swapped(one) * sin).astype(BF16)
        values[rows, :] = dot_nn(normed[rows, :], wv_ref[...]).astype(BF16)

    project(own)
    arrived(0)
    across(1).start()
    project(peers)
    gg.arrive(0)
    gg.arrive_over(0)

    scale = HEAD_DIM ** (-0.5)

    def heads_of(m, half):
        cols = pl.ds(pl.multiple_of(m * 128, 128), 128)
        key = doubled(keys[:, cols].astype(F32), half).astype(BF16)
        value = doubled(values[:, cols].astype(F32), half).astype(BF16)
        j = m * 2 + half
        wide = pl.ds(pl.multiple_of(j * 128, 128), 128)
        query = stacked(queries[:, wide].astype(F32)).astype(BF16)
        return j, wide, key, value, query

    def attend(m, carry):
        place_q = lax.rem(lax.broadcasted_iota(jnp.int32, (512, 256), 0), 256)
        place_k = lax.broadcasted_iota(jnp.int32, (512, 256), 1)
        for half in range(2):
            j, wide, key, value, query = heads_of(m, half)
            scores = jnp.where(place_q >= place_k, dot_nt(query, key) * scale, MASKED)
            raised = jnp.exp(scores - jnp.max(scores, -1, keepdims=True))
            share = raised / jnp.sum(raised, -1, keepdims=True)
            probs[j] = share
            attended[:, wide] = unstacked(dot_nn(share.astype(BF16), value)).astype(BF16)
        return carry

    lax.fori_loop(0, 2, attend, 0)
    gg.arrive(1)
    gg.arrive_over(1, 2)
    branch_o[...] = dot_nn(attended[peers, :], wo_ref[...]).astype(BF16)
    across(4).start()
    own_branch = dot_nn(attended[own, :], wo_ref[...])
    gg.arrive(2)
    gg.arrive_over(3, 4)
    across(4).wait_recv()
    across(2).start()
    across(3).start()
    resid = tokens_ref[...].astype(F32) + own_branch + branch_i[...].astype(F32)
    residual[...] = resid
    inv_two = lax.rsqrt(mean_last(resid * resid) + EPSILON)
    moe_in = (resid * inv_two * gain_two_ref[...]).astype(BF16)
    logits = dot_nt(moe_in, wide_router[...])
    is_named = named > 0.0
    top = jnp.max(jnp.where(is_named, logits, MASKED), -1, keepdims=True)
    raised = jnp.where(is_named, jnp.exp(jnp.minimum(logits - top, 0.0)), 0.0)
    gates = raised / jnp.sum(raised, -1, keepdims=True)
    gates_s[...] = gates
    weights = gates * kept
    coarse = weights.astype(BF16).astype(F32)
    x[mine, :WIDTH] = moe_in
    x[mine, WIDTH:] = (coarse + pltpu.roll(weights - coarse, 16, 1)).astype(BF16)

    gx.start()
    gg.arrive_over(5, 6)
    gates_w, ups_w, downs_w = (gate_ref, gate_p), (up_ref, up_p), (down_ref, down_p)
    gx.arrive(0)
    gx.arrive_over(0)
    gx.arrive(1)
    gx.arrive_over(1, 2)
    gg.from_sib(0, *range(7))
    gg.from_sib(1, *range(7))
    gx.from_sib(0, 0, 1, 2)
    gx.from_sib(1, 0, 1, 2)
    for k in (1, 2, 3):
        across(k).wait_recv()

    def joined(i):
        ring, other = place.step(i, EXPERT_ORDER)
        si.join(other * 4 + ring)
        so.join(other * 4 + ring)

        @pl.when((other == 1) & (i != 3))
        def _():
            si.over_copy(ring).start()

    def chip_step(i, carry):
        @pl.when(i == 2)
        def _():
            gx.arrive(2)
            gx.arrive_over(3, 4)

        @pl.when(i == 4)
        def _():
            gx.arrive_over(5, 6)
            gx.from_sib(0, *range(3, 7))
            gx.from_sib(1, *range(3, 7))

        ring, other = place.step(i, EXPERT_ORDER)
        expert_step(
            place, ring, other, x, g, gates_w, ups_w, downs_w, hid, dgate, dup, in_s, in_t, out_s, out_t
        )
        si.sib_copy(other * 4 + ring).start()
        so.sib_copy(other * 4 + ring).start()

        @pl.when(i >= 1)
        def _():
            joined(i - 1)

        return carry

    lax.fori_loop(0, 8, chip_step, 0)
    joined(jnp.int32(7))
    si.over_copy(place.near(0)).start()
    si.relay(1)

    def grad_step(i, carry):
        @pl.when(i == 3)
        def _():
            si.relay(3)

        @pl.when(i == 5)
        def _():
            si.relay(2)

        @pl.when((i >= 2))
        def _():
            cols = pl.ds(pl.multiple_of((i - 2) * 256, 256), 256)
            turned = x[:, cols].T
            both = dot_nn(turned, dgate[...])
            ggate_ref[cols, :] = both[:, :256]
            gate_o[cols, :] = both[:, 256:].astype(BF16)
            both = dot_nn(turned, dup[...])
            gup_ref[cols, :] = both[:, :256]
            up_o[cols, :] = both[:, 256:].astype(BF16)

        @pl.when(i == 0)
        def _():
            down_o[...] = dot_nn(hid[:, 256:].T, g[...]).astype(BF16)

        @pl.when(i == 1)
        def _():
            across(7).start()
            gdown_ref[...] = dot_nn(hid[:, :256].T, g[...])

        return carry

    lax.fori_loop(0, 6, grad_step, 0)
    across(5).start()
    for k in (3, 2, 1, 0):
        so.over_copy(place.near(k)).start()

    so.relay(3)
    from_experts = si.total()
    pairs = from_experts[:, WIDTH:]
    gates = gates_s[...]
    grad_gates = (pairs + pltpu.roll(pairs, 112, 1)) * kept_s[...]
    grad_logits = (gates * (grad_gates - jnp.sum(gates * grad_gates, -1, keepdims=True))).astype(BF16)
    grad_moe_in = from_experts[:, :WIDTH] + dot_nn(grad_logits, wide_router[...])
    resid = residual[...]
    inv_two = lax.rsqrt(mean_last(resid * resid) + EPSILON)
    grad_n = grad_moe_in * gain_two_ref[...]
    grad_residual = (
        cot_ref[...].astype(F32)
        + inv_two * grad_n
        - resid * (inv_two * inv_two * inv_two * mean_last(grad_n * resid))
    )
    branch_grad[own, :] = grad_residual.astype(BF16)
    across(8).start()
    grad_tokens_ref[...] = grad_residual
    small = dot_tn(grad_logits, x[mine, :WIDTH])
    ext_o[0:16, :] = small[0:16, :]
    ext_o[16:17, :] = jnp.sum(grad_moe_in * resid * inv_two, 0, keepdims=True)

    def grad_attended(rows):
        joint_grad[rows, :512] = dot_nt(branch_grad[rows, :], wo_ref[...]).astype(BF16)

    grad_attended(own)
    so.relay(2)
    arrived(8)
    across(6).start()
    grad_attended(peers)
    wo_part[...] = dot_tn(attended[...], branch_grad[...]).astype(BF16)

    si.sib_sent()
    si.sent()

    def share_out(n, carry):
        ring, other = place.step(n, PAIR_FIRST)
        start = pl.multiple_of(place.chip(ring, other) * 64, 64)
        i = other * 4 + ring
        put(place, i, sw.sums, sw.theirs, slice(0, WIDTH), wo_part[pl.ds(start, 64), :])
        sw.sib_copy(i).start()
        return carry

    lax.fori_loop(0, 8, share_out, 0)

    def attend_back(m, carry):
        cols = pl.ds(pl.multiple_of(m * 128, 128), 128)
        cos, sin = cos_ref[...], sin_ref[...]
        from_values, from_keys = [], []
        for half in range(2):
            j, wide, key, value, query = heads_of(m, half)
            grad_mixed = stacked(joint_grad[:, wide].astype(F32)).astype(BF16)
            share = probs[j]
            grad_probs = dot_nt(grad_mixed, value)
            grad_scores = (
                share * (grad_probs - jnp.sum(share * grad_probs, -1, keepdims=True)) * scale
            ).astype(BF16)
            grad_query = unstacked(dot_nn(grad_scores, key))
            joint_grad[:, wide] = (grad_query * cos - swapped(grad_query) * sin).astype(BF16)
            one = dot_tn(share.astype(BF16), grad_mixed)
            from_values.append(one + pltpu.roll(one, 64, 1))
            one = dot_tn(grad_scores, query)
            from_keys.append(one + pltpu.roll(one, 64, 1))
        low_lanes = lax.broadcasted_iota(jnp.int32, (256, 128), 1) < 64
        grad_key = jnp.where(low_lanes, from_keys[0], from_keys[1])
        at_key = pl.ds(pl.multiple_of(512 + m * 128, 128), 128)
        at_value = pl.ds(pl.multiple_of(768 + m * 128, 128), 128)
        joint_grad[:, at_key] = (grad_key * cos - swapped(grad_key) * sin).astype(BF16)
        joint_grad[:, at_value] = jnp.where(low_lanes, from_values[0], from_values[1]).astype(BF16)
        return carry

    so.relay(1)
    lax.fori_loop(0, 2, attend_back, 0)

    def share_joint(n, carry):
        ring, other = place.step(n, PAIR_FIRST)
        i = other * 4 + ring
        cols = pl.ds(pl.multiple_of(place.chip(ring, other) * 128, 128), 128)
        value = dot_nn(normed[:, cols].T, joint_grad[...])
        put(place, i, sj.sums, sj.theirs, slice(0, WIDTH), value)
        sj.sib_copy(i).start()
        return carry

    lax.fori_loop(0, 8, share_joint, 0)

    def grad_normed(rows):
        grads = joint_grad[rows, :]
        parts = []
        for n in range(4):
            at = slice(n * 256, (n + 1) * 256)
            parts.append(
                dot_nt(grads[:, :512], wq_ref[at, :])
                + dot_nt(grads[:, 512:768], wk_ref[at, :])
                + dot_nt(grads[:, 768:], wv_ref[at, :])
            )
        return jnp.concatenate(parts, 1)

    part = grad_normed(peers)
    across(4).wait_send()
    branch_o[...] = part.astype(BF16)
    gain_sum = jnp.sum(part * normed[peers, :].astype(F32), 0, keepdims=True)
    sj.join_all()
    own_part = grad_normed(own)
    gain_sum = gain_sum + jnp.sum(own_part * normed[own, :].astype(F32), 0, keepdims=True)
    ext_o[17:18, :] = gain_sum / gain_one_ref[...]
    ext_o[18:, :] = jnp.zeros((6, WIDTH), F32)
    across(10).start()
    ext_t[...] = jnp.concatenate([ext_o[...], jnp.zeros((BLK - 24, WIDTH), F32)], 0).T

    def share_ext(n, carry):
        ring, other = place.step(n, PAIR_FIRST)
        rows = pl.ds(pl.multiple_of(place.chip(ring, other) * 128, 128), 128)
        i = other * 4 + ring
        put(place, i, se.sums, se.theirs, slice(0, BLK), ext_t[rows, :])
        se.sib_copy(i).start()
        return carry

    lax.fori_loop(0, 8, share_ext, 0)
    sw.join_all()
    sj.relay(3)
    se.join_all()
    sj.relay(2, 1)
    block = pl.ds(pl.multiple_of(place.e * 64, 64), 64)
    joint_ref[block, :] = sj.total().astype(BF16)
    gj.start()
    sw.relay(3, 2, 1)
    se.relay(3, 2, 1)
    block = pl.ds(pl.multiple_of(place.e * 32, 32), 32)
    wo_grad_ref[block, :] = sw.total().astype(BF16)
    gw.start()
    gj.arrive(0)
    gj.arrive_over(0)
    small_o[...] = se.total()
    across(9).start()
    gj.arrive(1)
    gj.arrive_over(1, 2)
    gw.arrive(0)
    gw.arrive_over(0)

    across(10).wait_recv()
    grad_n = (own_part + branch_i[...].astype(F32)) * gain_one_ref[...]
    inputs = tokens_ref[...].astype(F32)
    inv_one = lax.rsqrt(mean_last(inputs * inputs) + EPSILON)
    grad_tokens_ref[...] = (
        grad_tokens_ref[...]
        + inv_one * grad_n
        - inputs * (inv_one * inv_one * inv_one * mean_last(grad_n * inputs))
    )
    block = pl.ds(pl.multiple_of(place.e * 64, 64), 64)
    across(9).wait_recv()
    small_ref[block, :] = small_o[...] + small_i[...]
    ge.start()
    gj.arrive(2)
    gj.arrive_over(3, 4)
    gw.arrive(1)
    gw.arrive_over(1, 2)
    ge.arrive(1, 2, 3)
    output_ref[...] = (residual[...] + so.total()).astype(BF16)
    gj.arrive_over(5, 6)
    gw.arrive(2)
    gw.arrive_over(3, 4)
    ge.arrive_over(0, 1, 2, 3)
    gw.arrive_over(5, 6)
    for tree in (gj, gw):
        tree.from_sib(0, *range(7))
        tree.from_sib(1, *range(7))
    ge.from_sib()
    for k in (5, 6, 7):
        across(k).wait_recv()
    for k in (0, 1, 2, 3, 5, 6, 7, 8, 9, 10):
        across(k).wait_send()
    for tree in (so, sj, sw, se):
        tree.sib_sent()
    for tree in (gx, gg, gj, gw, ge, so, sj, sw, se):
        tree.sent()


def layer_call(capacity, *operands):
    vm, dma = pltpu.VMEM, pltpu.SemaphoreType.DMA
    spec = pl.BlockSpec(memory_space=pltpu.VMEM)
    sds = jax.ShapeDtypeStruct

    def body(*refs):
        return layer_kernel(capacity, *refs)

    outs = (
        sds((BLK, WIDTH), BF16),
        sds((BLK, WIDTH), F32),
        sds((WIDTH, WIDTH), BF16),
        sds((HALF, WIDTH), BF16),
        sds((WIDTH, BLK), F32),
        sds((WIDTH, 256), F32),
        sds((WIDTH, 256), F32),
        sds((256, WIDTH), F32),
        sds((WIDTH, 256), BF16),
        sds((WIDTH, 256), BF16),
        sds((256, WIDTH), BF16),
    )
    return pl.pallas_call(
        body,
        out_shape=outs,
        in_specs=[spec] * len(operands),
        out_specs=[spec] * len(outs),
        scratch_shapes=[
            vm((2048, EXT), BF16), vm((2048, WIDTH), BF16),
            vm((WIDTH, 256), BF16), vm((WIDTH, 256), BF16), vm((256, WIDTH), BF16),
            vm((2048, 512), BF16), vm((2048, 512), BF16), vm((2048, 512), BF16),
            vm((8, BLK, EXT), BF16), vm((8, BLK, EXT), BF16), vm((8, BLK, EXT), BF16),
            vm((8, BLK, WIDTH), BF16), vm((8, BLK, WIDTH), BF16), vm((8, BLK, WIDTH), BF16),
            vm((4, BLK, EXT), BF16), vm((4, BLK, EXT), BF16),
            vm((4, BLK, WIDTH), BF16), vm((4, BLK, WIDTH), BF16),
            vm((WIDTH, 256), BF16), vm((WIDTH, 256), BF16), vm((256, WIDTH), BF16),
            vm((256, WIDTH), BF16), vm((256, 256), BF16), vm((256, 256), BF16), vm((256, 512), BF16),
            vm((4, 512, 256), F32), vm((256, 512), BF16),
            vm((BLK, WIDTH), BF16), vm((BLK, WIDTH), BF16), vm((BLK, WIDTH), F32),
            vm((BLK, BLK), F32), vm((BLK, BLK), F32),
            vm((256, WIDTH), BF16), vm((256, WIDTH), BF16),
            vm((24, WIDTH), F32), vm((WIDTH, BLK), F32), vm((64, BLK), F32), vm((64, BLK), F32), vm((512, WIDTH), BF16),
            vm((8, 64, WIDTH), BF16), vm((4, 64, WIDTH), BF16), vm((4, 64, WIDTH), BF16),
            vm((8, 32, WIDTH), BF16), vm((4, 32, WIDTH), BF16), vm((4, 32, WIDTH), BF16),
            vm((8, 64, BLK), F32), vm((8, 64, BLK), F32), vm((8, 64, BLK), F32),
            vm((4, 64, BLK), F32), vm((4, 64, BLK), F32), vm((BLK, WIDTH), BF16),
            dma((5, 27)), dma((5, 27)), dma((5, 7)), dma((5, 8)), dma((5, 8)), dma((5, 8)),
            dma((11,)), dma((11,)),
        ],
        compiler_params=pltpu.CompilerParams(
            collective_id=1, has_side_effects=True, vmem_limit_bytes=63 * 2**20
        ),
        cost_estimate=pl.CostEstimate(flops=24 * 10**9, bytes_accessed=10**7, transcendentals=10**6),
        name="layer",
    )(*operands)


def finish_kernel(
    joint_ref, wo_ref, small_ref, gate_ref, up_ref, down_ref, gate_i, up_i, down_i,
    query_out, key_out, value_out, wo_out, small_out, gate_out, up_out, down_out,
):
    query_out[...] = joint_ref[:, :512].astype(F32)
    key_out[...] = joint_ref[:, 512:768].astype(F32)
    value_out[...] = joint_ref[:, 768:].astype(F32)
    wo_out[...] = wo_ref[...].astype(F32)
    small_out[...] = small_ref[...].T[:24, :]
    gate_out[...] = gate_ref[...] + gate_i[...].astype(F32)
    up_out[...] = up_ref[...] + up_i[...].astype(F32)
    down_out[...] = down_ref[...] + down_i[...].astype(F32)


def finish_call(*operands):
    steps = 4
    sds = jax.ShapeDtypeStruct

    def rows(shape):
        return pl.BlockSpec((shape[0] // steps, shape[1]), lambda i: (i, 0))

    outs = (
        (WIDTH, 512), (WIDTH, 256), (WIDTH, 256), (HALF, WIDTH), (24, WIDTH),
        (WIDTH, 256), (WIDTH, 256), (256, WIDTH),
    )
    out_specs = [rows(shape) for shape in outs]
    out_specs[4] = pl.BlockSpec((24, WIDTH // steps), lambda i: (0, i))
    return pl.pallas_call(
        finish_kernel,
        out_shape=tuple(sds(shape, F32) for shape in outs),
        grid=(steps,),
        in_specs=[rows(a.shape) for a in operands],
        out_specs=out_specs,
        compiler_params=pltpu.CompilerParams(vmem_limit_bytes=62 * 2**20),
        cost_estimate=pl.CostEstimate(flops=10**6, bytes_accessed=18 * 10**6, transcendentals=0),
        name="finish",
    )(*operands)


def tables(rows):
    half = HEAD_DIM // 2
    freqs = np.exp(np.arange(half, dtype=np.float32) * np.float32(-2.0 * math.log(THETA_BASE) / HEAD_DIM))
    angles = np.arange(rows, dtype=np.float32)[:, None] * freqs[None, :]
    cos, sin = np.cos(angles), np.sin(angles)
    return (
        np.concatenate([cos] * 4, 1).astype(np.float32),
        np.concatenate([-sin, sin] * 2, 1).astype(np.float32),
    )


def on_device(
    tokens,
    gain_attn,
    w_query,
    w_key,
    w_value,
    w_out,
    gain_moe,
    router,
    expert_gate,
    expert_up,
    expert_down,
    routes,
    fill_order,
    cotangent,
):
    tok_rows, width = tokens.shape
    tensor_size = lax.axis_size("tensor")
    seq_rows = tok_rows * tensor_size
    head_size = HEAD_DIM
    q_cols = w_query.shape[1]
    kv_cols = w_key.shape[1]
    q_heads = q_cols // head_size
    kv_heads = kv_cols // head_size
    q_group = q_heads // kv_heads
    score_scale = head_size ** (-0.5)
    local_experts = expert_gate.shape[0]
    expert_groups = lax.axis_size("expert")
    experts = local_experts * expert_groups
    top_k = routes.shape[1]
    capacity = (5 * tok_rows * top_k + 4 * experts - 1) // (4 * experts)
    gate_w, up_w, down_w = (expert_gate, expert_up, expert_down)
    inputs = tokens.astype(jnp.float32)
    inv_one = lax.rsqrt(jnp.mean(inputs * inputs, -1, keepdims=True) + EPSILON)
    normed = (inputs * inv_one * gain_attn).astype(jnp.bfloat16)
    normed_all = lax.all_gather(normed, "tensor", axis=0, tiled=True)
    w_joint = jnp.concatenate([w_query, w_key, w_value], 1)
    joint = jnp.dot(normed_all, w_joint, preferred_element_type=jnp.float32)
    angles = angles_of(seq_rows, head_size)
    queries = rotate(joint[:, :q_cols].reshape(seq_rows, q_heads, head_size), angles, 1.0).astype(
        jnp.bfloat16
    )
    key_rows = rotate(
        joint[:, q_cols : q_cols + kv_cols].reshape(seq_rows, kv_heads, head_size), angles, 1.0
    ).astype(jnp.bfloat16)
    value_rows = (
        joint[:, q_cols + kv_cols :].astype(jnp.bfloat16).reshape(seq_rows, kv_heads, head_size)
    )
    q_size = min(512, seq_rows)
    blocks = seq_rows // q_size
    key_pos = jnp.arange(seq_rows)

    def scores_of(q_block, row_start):
        grouped = q_block.reshape(q_size, kv_heads, q_group, head_size)
        raw_scores = (
            jnp.einsum("qkgd,tkd->kgqt", grouped, key_rows, preferred_element_type=jnp.float32)
            * score_scale
        )
        allowed = (row_start + jnp.arange(q_size))[:, None] >= key_pos[None, :]
        return (grouped, jnp.where(allowed, raw_scores, MASKED))

    def forward_block(block_args):
        q_block, row_start = block_args
        grouped, scores = scores_of(q_block, row_start)
        top_score = jnp.max(scores, -1, keepdims=True)
        exp_scores = jnp.exp(scores - top_score)
        row_total = jnp.sum(exp_scores, -1, keepdims=True)
        attn_probs = (exp_scores / row_total).astype(jnp.bfloat16)
        mixed_rows = jnp.einsum(
            "kgqt,tkd->qkgd", attn_probs, value_rows, preferred_element_type=jnp.float32
        )
        return (mixed_rows.astype(jnp.bfloat16).reshape(q_size, q_cols), top_score, row_total)

    q_blocks = queries.reshape(blocks, q_size, q_heads, head_size)
    starts = jnp.arange(blocks) * q_size
    attended, maxima, totals = lax.map(forward_block, (q_blocks, starts))
    attended = attended.reshape(seq_rows, q_cols)
    row_block = attended
    branch = lax.psum_scatter(
        jnp.dot(row_block, w_out, preferred_element_type=jnp.float32),
        "tensor",
        scatter_dimension=0,
        tiled=True,
    )
    residual = inputs + branch
    inv_two = lax.rsqrt(jnp.mean(residual * residual, -1, keepdims=True) + EPSILON)
    scaled = residual * inv_two
    moe_in = (scaled * gain_moe).astype(jnp.bfloat16)
    logits = jnp.dot(moe_in, router, preferred_element_type=jnp.float32)
    expert_ids = jnp.arange(experts, dtype=jnp.int32)
    named = jnp.sum((routes[:, :, None] == expert_ids[None, None, :]).astype(jnp.float32), 1)
    place_of = (fill_order[0][:, None] == jnp.arange(tok_rows)[None, :]).astype(jnp.bfloat16)
    ordered = jnp.dot(place_of, named.astype(jnp.bfloat16), preferred_element_type=jnp.float32)
    earlier = (jnp.arange(tok_rows)[:, None] > jnp.arange(tok_rows)[None, :]).astype(jnp.bfloat16)
    before = jnp.dot(earlier, ordered.astype(jnp.bfloat16), preferred_element_type=jnp.float32)
    rank = contract_first(place_of, before.astype(jnp.bfloat16))
    kept = named * (rank < capacity).astype(jnp.float32)
    top_logit = jnp.max(jnp.where(named > 0, logits, MASKED), -1, keepdims=True)
    exp_logits = jnp.where(named > 0, jnp.exp(jnp.minimum(logits - top_logit, 0.0)), 0.0)
    gates = exp_logits / jnp.sum(exp_logits, -1, keepdims=True)
    weights = gates * kept

    gate_all = lax.all_gather(gate_w[0], "tensor", axis=1, tiled=True)
    up_all = lax.all_gather(up_w[0], "tensor", axis=1, tiled=True)
    down_all = lax.all_gather(down_w[0], "tensor", axis=0, tiled=True)
    grad_out = cotangent.astype(jnp.float32)
    plane_cot = lax.all_gather(cotangent, "expert", axis=0, tiled=True)
    plane_in = lax.all_gather(moe_in, "expert", axis=0, tiled=True)
    plane_weights = lax.all_gather(weights, "expert", axis=0, tiled=True)
    mine = (expert_ids == lax.axis_index("expert")).astype(jnp.float32)
    my_weight = jnp.sum(plane_weights * mine[None, :], -1, keepdims=True)

    gate_pre = jnp.dot(plane_in, gate_all, preferred_element_type=jnp.float32)
    up_pre = jnp.dot(plane_in, up_all, preferred_element_type=jnp.float32)
    back_down = contract_last(plane_cot, down_all)
    gate_sigmoid = jax.nn.sigmoid(gate_pre)
    active = gate_pre * gate_sigmoid
    hidden = active * up_pre
    pair_grad = jnp.sum(hidden * back_down, -1, keepdims=True)
    hidden_w = (hidden * my_weight).astype(jnp.bfloat16)
    grad_hidden = back_down * my_weight
    grad_gate_pre = (
        grad_hidden * up_pre * gate_sigmoid * (1.0 + gate_pre * (1.0 - gate_sigmoid))
    ).astype(jnp.bfloat16)
    grad_up_pre = (grad_hidden * active).astype(jnp.bfloat16)
    out_part = jnp.dot(hidden_w, down_all, preferred_element_type=jnp.float32)
    in_part = contract_last(grad_gate_pre, gate_all) + contract_last(grad_up_pre, up_all)
    out_sum = lax.psum_scatter(
        out_part.astype(jnp.bfloat16), "expert", scatter_dimension=0, tiled=True
    )
    in_sum = lax.psum_scatter(
        in_part.astype(jnp.bfloat16), "expert", scatter_dimension=0, tiled=True
    )
    grad_gates = lax.psum_scatter(
        pair_grad * mine[None, :], "expert", scatter_dimension=0, tiled=True
    ) * kept
    grad_down = lax.psum_scatter(
        contract_first(hidden_w, plane_cot).astype(jnp.bfloat16),
        "tensor", scatter_dimension=0, tiled=True,
    ).astype(jnp.float32)[None]
    grad_gate = lax.psum_scatter(
        contract_first(plane_in, grad_gate_pre).astype(jnp.bfloat16),
        "tensor", scatter_dimension=1, tiled=True,
    ).astype(jnp.float32)[None]
    grad_up = lax.psum_scatter(
        contract_first(plane_in, grad_up_pre).astype(jnp.bfloat16),
        "tensor", scatter_dimension=1, tiled=True,
    ).astype(jnp.float32)[None]
    output_rows = residual + out_sum.astype(jnp.float32)
    grad_logits = (
        gates * (grad_gates - jnp.sum(gates * grad_gates, -1, keepdims=True))
    ).astype(jnp.bfloat16)
    grad_moe_in = in_sum.astype(jnp.float32) + contract_last(grad_logits, router)
    grad_router = contract_first(moe_in, grad_logits)
    grad_gain_moe = jnp.sum(grad_moe_in * scaled, 0)
    grad_norm_two = grad_moe_in * gain_moe
    grad_residual = (
        grad_out
        + inv_two * grad_norm_two
        - residual * inv_two**3 * jnp.mean(grad_norm_two * residual, -1, keepdims=True)
    )
    grad_branch = grad_residual.astype(jnp.bfloat16)
    shard_piece = lax.all_gather(grad_branch, "tensor", axis=0, tiled=True)
    grad_part = contract_last(shard_piece, w_out).astype(jnp.bfloat16)
    grad_mixed = grad_part
    grad_wout = contract_first(attended, shard_piece)
    grad_mixed, grad_w_out = (grad_mixed, grad_wout)
    grad_blocks = grad_mixed.reshape(blocks, q_size, q_heads, head_size)

    def backward_block(carry, block_args):
        grad_keys, grad_values = carry
        q_block, grad_block, row_start, top_score, row_total = block_args
        grouped, scores = scores_of(q_block, row_start)
        attn_probs = jnp.exp(scores - top_score) / row_total
        grad_grouped = grad_block.reshape(q_size, kv_heads, q_group, head_size)
        grad_probs = jnp.einsum(
            "qkgd,tkd->kgqt", grad_grouped, value_rows, preferred_element_type=jnp.float32
        )
        grad_values = grad_values + jnp.einsum(
            "kgqt,qkgd->tkd",
            attn_probs.astype(jnp.bfloat16),
            grad_grouped,
            preferred_element_type=jnp.float32,
        )
        grad_scores = (
            attn_probs
            * (grad_probs - jnp.sum(attn_probs * grad_probs, -1, keepdims=True))
            * score_scale
        ).astype(jnp.bfloat16)
        grad_query = jnp.einsum(
            "kgqt,tkd->qkgd", grad_scores, key_rows, preferred_element_type=jnp.float32
        ).reshape(q_size, q_heads, head_size)
        grad_keys = grad_keys + jnp.einsum(
            "kgqt,qkgd->tkd", grad_scores, grouped, preferred_element_type=jnp.float32
        )
        return ((grad_keys, grad_values), grad_query)

    zero_rows = jnp.zeros((seq_rows, kv_heads, head_size), jnp.float32)
    (grad_keys, grad_values), grad_queries = lax.scan(
        backward_block, (zero_rows, zero_rows), (q_blocks, grad_blocks, starts, maxima, totals)
    )
    grad_queries = grad_queries.reshape(seq_rows, q_heads, head_size)
    grad_q = rotate(grad_queries, angles, -1.0).astype(jnp.bfloat16).reshape(seq_rows, q_cols)
    grad_k = rotate(grad_keys, angles, -1.0).astype(jnp.bfloat16).reshape(seq_rows, kv_cols)
    grad_v = grad_values.astype(jnp.bfloat16).reshape(seq_rows, kv_cols)
    grad_joint = jnp.concatenate([grad_q, grad_k, grad_v], 1)
    grad_w_joint = contract_first(normed_all, grad_joint)
    row_block = grad_joint
    grad_normed = lax.psum_scatter(
        contract_last(row_block, w_joint), "tensor", scatter_dimension=0, tiled=True
    )
    grad_gain_attn = jnp.sum(grad_normed * inputs * inv_one, 0)
    grad_norm_one = grad_normed * gain_attn
    grad_tokens = (
        grad_residual
        + inv_one * grad_norm_one
        - inputs * inv_one**3 * jnp.mean(grad_norm_one * inputs, -1, keepdims=True)
    )
    summed_joint, summed_out = lax.psum((grad_w_joint, grad_w_out), "expert")
    summed_gain_attn, summed_gain_moe, summed_router = lax.psum(
        (grad_gain_attn, grad_gain_moe, grad_router), ("expert", "tensor")
    )
    return (
        output_rows.astype(jnp.bfloat16),
        grad_tokens,
        summed_gain_attn,
        summed_joint[:, :q_cols],
        summed_joint[:, q_cols : q_cols + kv_cols],
        summed_joint[:, q_cols + kv_cols :],
        summed_out,
        summed_gain_moe,
        summed_router,
        grad_gate,
        grad_up,
        grad_down,
    )


def by_kernel(
    tokens,
    gain_attn,
    w_query,
    w_key,
    w_value,
    w_out,
    gain_moe,
    router,
    expert_gate,
    expert_up,
    expert_down,
    routes,
    fill_order,
    cotangent,
):
    tok_rows = tokens.shape[0]
    experts = router.shape[1]
    capacity = (5 * tok_rows * routes.shape[1] + 4 * experts - 1) // (4 * experts)
    cos, sin = tables(tok_rows * 2)
    out, grad_tokens, joint, wo_grad, small, *expert_grads = layer_call(
        capacity,
        tokens, cotangent, gain_attn[None], gain_moe[None], w_query, w_key, w_value, w_out,
        router.T, routes.T, fill_order, jnp.asarray(cos), jnp.asarray(sin),
        expert_gate[0], expert_up[0], expert_down[0],
    )
    gq, gk, gv, gwo, small, ggate, gup, gdown = finish_call(joint, wo_grad, small, *expert_grads)
    return (
        out,
        grad_tokens,
        small[experts + 1],
        gq,
        gk,
        gv,
        gwo,
        small[experts],
        small[:experts].T,
        ggate[None],
        gup[None],
        gdown[None],
    )


def kernel_fits(mesh_shape, shapes):
    return mesh_shape == (16, 2) and shapes == (
        (128, 1024), (1024,), (1024, 512), (1024, 256), (1024, 256), (512, 1024), (1024,), (1024, 16),
        (1, 1024, 256), (1, 1024, 256), (1, 256, 1024), (128, 8), (1, 128), (128, 1024),
    )


def on_any(*operands):
    sizes = (lax.axis_size("expert"), lax.axis_size("tensor"))
    if kernel_fits(sizes, tuple(a.shape for a in operands)):
        return by_kernel(*operands)
    return on_device(*operands)


def solution(mesh):
    placed = (
        P(("expert", "tensor"), None),
        P(),
        P(None, "tensor"),
        P(None, "tensor"),
        P(None, "tensor"),
        P("tensor", None),
        P(),
        P(),
        P("expert", None, "tensor"),
        P("expert", None, "tensor"),
        P("expert", "tensor", None),
        P(("expert", "tensor"), None),
        P(("expert", "tensor"), None),
        P(("expert", "tensor"), None),
    )
    return jax.shard_map(
        on_any,
        mesh=mesh,
        in_specs=placed,
        out_specs=(
            P(("expert", "tensor"), None),
            P(("expert", "tensor"), None),
            P(),
            P(None, "tensor"),
            P(None, "tensor"),
            P(None, "tensor"),
            P("tensor", None),
            P(),
            P(),
            P("expert", None, "tensor"),
            P("expert", None, "tensor"),
            P("expert", "tensor", None),
        ),
        check_vma=False,
    )
```

```python
import math

import jax
import jax.numpy as jnp
import numpy as np
from jax import lax
from jax.experimental import pallas as pl
from jax.experimental.pallas import tpu as pltpu
from jax.sharding import PartitionSpec as P

HEAD_DIM = 64


EPSILON = 1e-06
THETA_BASE = 10000.0
MASKED = -1e30


def angles_of(row_count, head_size):
    half = head_size // 2
    freqs = jnp.exp(jnp.arange(half, dtype=jnp.float32) * (-2.0 * math.log(THETA_BASE) / head_size))
    return jnp.arange(row_count, dtype=jnp.float32)[:, None] * freqs[None, :]


def rotate(vectors, angles, sign):
    half = vectors.shape[-1] // 2
    cosine = jnp.cos(angles)[:, None, :]
    sine = sign * jnp.sin(angles)[:, None, :]
    first = vectors[..., :half]
    second = vectors[..., half:]
    return jnp.concatenate([first * cosine - second * sine, second * cosine + first * sine], -1)


def contract_last(left, right):
    return lax.dot_general(
        left, right, (((1,), (1,)), ((), ())), preferred_element_type=jnp.float32
    )


def contract_first(left, right):
    return lax.dot_general(
        left, right, (((0,), (0,)), ((), ())), preferred_element_type=jnp.float32
    )


F32 = jnp.float32
BF16 = jnp.bfloat16
MESH = pl.DeviceIdType.MESH
BLK = 128
WIDTH = 1024
EXT = 1152
HALF = 512
NEAREST = (0, 1, 2, 3, 1, 0, 2, 3, 2, 3, 1, 0, 3, 2, 1, 0)
EXPERT_ORDER = ((0, 0), (1, 1), (1, 0), (0, 1), (3, 1), (3, 0), (2, 1), (2, 0))
PAIR_FIRST = ((3, 1), (2, 1), (1, 1), (0, 1), (3, 0), (2, 0), (1, 0), (0, 0))


def pick(i, values):
    out = jnp.int32(values[-1])
    for n in range(len(values) - 2, -1, -1):
        out = jnp.where(i == n, jnp.int32(values[n]), out)
    return out


class Place:
    def __init__(self):
        e = lax.axis_index("expert")
        t = lax.axis_index("tensor")
        self.e = e
        self.t = t
        self.core = lax.rem(e, 2)
        self.pair = lax.rem(e // 2, 2)
        self.ring = e // 4
        self.other = (e + 2 - 4 * self.pair, t)
        self.sib = (e + 1 - 2 * self.core, t)
        self.across = (e, 1 - t)

    def at(self, ring):
        return (ring * 4 + lax.rem(self.e, 4), self.t)

    def chip(self, ring, other):
        return ring * 2 + (self.pair + other - 2 * self.pair * other)

    def step(self, i, order):
        ring = self.near(pick(i, [k for k, _ in order]))
        return ring, pick(i, [other for _, other in order])

    def near(self, k):
        return pick(self.ring * 4 + k, NEAREST)

    def barrier(self):
        bar = pltpu.get_barrier_semaphore()
        for dest in [self.at(lax.rem(self.ring + m, 4)) for m in (1, 2, 3)] + [
            self.other, self.sib, self.across,
        ]:
            pl.semaphore_signal(bar, inc=1, device_id=dest, device_id_type=MESH)
        pl.semaphore_wait(bar, 6)


def if_(condition, action):
    if condition is True:
        action()
    else:
        pl.when(condition)(action)


class Gather:
    def __init__(self, place, buf, send_sems, recv_sems):
        self.place, self.buf, self.ss, self.rs = place, buf, send_sems, recv_sems
        self.size = buf.shape[0] // 16

    def where(self, n):
        r = self.place.ring
        if n == 0:
            return r, True
        j = (n - 1) // 2
        return (r - 1 - j, r > j) if n % 2 else (r + 1 + j, 3 - r > j)

    def copy(self, ring, other, core, sem, dest):
        block = self.place.chip(ring, other) * 2 + core
        ref = self.buf.at[pl.ds(pl.multiple_of(block * self.size, self.size), self.size)]
        return pltpu.make_async_remote_copy(
            src_ref=ref, dst_ref=ref, send_sem=self.ss.at[sem], recv_sem=self.rs.at[sem],
            device_id=dest, device_id_type=MESH,
        )

    def up(self, k):
        r = self.place.ring
        return self.copy(r - k, 0, self.place.core, k, self.place.at(r + 1))

    def down(self, k):
        r = self.place.ring
        return self.copy(r + k, 0, self.place.core, 3 + k, self.place.at(r - 1))

    def over(self, n, arriving=0):
        return self.copy(self.where(n)[0], arriving, self.place.core, 6 + n, self.place.other)

    def to_sib(self, n, other, arriving=False):
        core = 1 - self.place.core if arriving else self.place.core
        return self.copy(self.where(n)[0], other, core, 13 + 7 * other + n, self.place.sib)

    def start(self):
        r = self.place.ring
        if_(r < 3, lambda: self.up(0).start())
        if_(r > 0, lambda: self.down(0).start())
        self.over(0).start()
        self.to_sib(0, 0).start()

    def arrive(self, j):
        r = self.place.ring

        def from_below():
            self.copy(r - 1 - j, 0, self.place.core, j, self.place.other).wait_recv()
            if j < 2:
                if_(r < 3, lambda: self.up(j + 1).start())
            self.over(1 + 2 * j).start()
            self.to_sib(1 + 2 * j, 0).start()

        def from_above():
            self.copy(r + 1 + j, 0, self.place.core, 3 + j, self.place.other).wait_recv()
            if j < 2:
                if_(r > 0, lambda: self.down(j + 1).start())
            self.over(2 + 2 * j).start()
            self.to_sib(2 + 2 * j, 0).start()

        if_(r > j, from_below)
        if_(3 - r > j, from_above)

    def arrive_over(self, *numbers):
        for n in numbers:

            def taken(n=n):
                self.over(n, 1).wait_recv()
                self.to_sib(n, 1).start()

            if_(self.where(n)[1], taken)

    def from_sib(self, other, *numbers):
        for n in numbers:
            if_(self.where(n)[1], lambda n=n: self.to_sib(n, other, True).wait_recv())

    def sent(self):
        r = self.place.ring
        for k in range(3):
            if_((r < 3) & (r >= k), lambda k=k: self.up(k).wait_send())
            if_((r > 0) & (3 - r >= k), lambda k=k: self.down(k).wait_send())
        for n in range(7):

            def all_of(n=n):
                self.over(n).wait_send()
                self.to_sib(n, 0).wait_send()
                self.to_sib(n, 1).wait_send()

            if_(self.where(n)[1], all_of)


class GatherDirect(Gather):
    def span(self, k, sending):
        ring = self.place.near(k)
        r = self.place.ring
        m = lax.rem((ring - r if sending else r - ring) + 4, 4)
        source = r if sending else ring
        return self.copy(source, 0, self.place.core, m - 1, self.place.at(ring))

    def over(self, k, arriving=0):
        return self.copy(self.place.near(k), arriving, self.place.core, 3 + k, self.place.other)

    def to_sib(self, k, other, arriving=False):
        core = 1 - self.place.core if arriving else self.place.core
        return self.copy(self.place.near(k), other, core, 7 + 4 * other + k, self.place.sib)

    def start(self):
        for k in (1, 2, 3):
            self.span(k, True).start()
        self.over(0).start()
        self.to_sib(0, 0).start()

    def arrive(self, *ks):
        for k in ks:
            self.span(k, False).wait_recv()
            self.over(k).start()
            self.to_sib(k, 0).start()

    def arrive_over(self, *ks):
        for k in ks:
            self.over(k, 1).wait_recv()
            self.to_sib(k, 1).start()

    def from_sib(self):
        for other in range(2):
            for k in range(4):
                self.to_sib(k, other, True).wait_recv()

    def sent(self):
        for k in range(4):
            if k:
                self.span(k, True).wait_send()
            self.over(k).wait_send()
            self.to_sib(k, 0).wait_send()
            self.to_sib(k, 1).wait_send()


class Scatter:
    def __init__(self, place, sums, theirs, from_sib, over, along, sib_ss, sib_rs, ss, rs):
        self.place, self.sums, self.theirs, self.from_sib = place, sums, theirs, from_sib
        self.over, self.along = over, along
        self.sib_ss, self.sib_rs, self.ss, self.rs = sib_ss, sib_rs, ss, rs

    def sib_copy(self, i):
        return pltpu.make_async_remote_copy(
            src_ref=self.theirs.at[i], dst_ref=self.from_sib.at[i],
            send_sem=self.sib_ss.at[i], recv_sem=self.sib_rs.at[i],
            device_id=self.place.sib, device_id_type=MESH,
        )

    def join(self, i):
        self.sib_copy(i).wait_recv()
        total = self.sums[i].astype(F32) + self.from_sib[i].astype(F32)
        self.sums[i] = total.astype(self.from_sib.dtype)

    def join_all(self):
        for k, other in PAIR_FIRST:
            ring = self.place.near(k)
            self.join(other * 4 + ring)
            if other:
                self.over_copy(ring).start()

    def over_copy(self, ring):
        return pltpu.make_async_remote_copy(
            src_ref=self.sums.at[4 + ring], dst_ref=self.over.at[ring],
            send_sem=self.ss.at[ring], recv_sem=self.rs.at[ring],
            device_id=self.place.other, device_id_type=MESH,
        )

    def along_copy(self, k, ring, slot):
        return pltpu.make_async_remote_copy(
            src_ref=self.sums.at[self.place.near(k)], dst_ref=self.along.at[slot],
            send_sem=self.ss.at[3 + k], recv_sem=self.rs.at[4 + slot],
            device_id=self.place.at(ring), device_id_type=MESH,
        )

    def relay(self, *ks):
        r = self.place.ring
        at_end = (r == 0) | (r == 3)
        beside = self.place.near(1)
        for k in ks:
            ring = self.place.near(k)

            def add(*others, ring=ring):
                total = self.sums[ring].astype(F32)
                for other in others:
                    total = total + other.astype(F32)
                self.sums[ring] = total.astype(self.over.dtype)

            self.over_copy(ring).wait_recv()
            if k == 1:
                add(self.over[ring])
                self.along_copy(1, ring, 0).start()
                continue

            @pl.when(at_end)
            def _(k=k, ring=ring):
                add(self.over[ring])
                self.along_copy(k, beside, k).start()

            @pl.when(jnp.logical_not(at_end))
            def _(k=k, ring=ring):
                self.along_copy(k, beside, k).wait_recv()
                add(self.over[ring], self.along[k])
                self.along_copy(k, ring, 1).start()

    def total(self):
        ring = self.place.ring
        self.over_copy(ring).wait_recv()
        for slot in (0, 1):
            self.along_copy(1, self.place.near(1), slot).wait_recv()
        return (self.sums[ring].astype(F32) + self.over[ring].astype(F32)) + (
            self.along[0].astype(F32) + self.along[1].astype(F32)
        )

    def sib_sent(self):
        for i in range(8):
            self.sib_copy(i).wait_send()

    def sent(self):
        for ring in range(4):
            self.over_copy(ring).wait_send()
        for k in (1, 2, 3):
            self.along_copy(k, self.place.near(k), 0).wait_send()


def dot_nn(a, b):
    return lax.dot_general(a, b, (((1,), (0,)), ((), ())), preferred_element_type=F32)


def dot_nt(a, b):
    return lax.dot_general(a, b, (((1,), (1,)), ((), ())), preferred_element_type=F32)


def dot_tn(a, b):
    return lax.dot_general(a, b, (((0,), (0,)), ((), ())), preferred_element_type=F32)


def expert_step(place, ring, other, x, g, gates_w, ups_w, downs_w, hid, dgate, dup, in_s, in_t, out_s, out_t):
    i = other * 4 + ring
    rows = pl.ds(pl.multiple_of(place.chip(ring, other) * 256, 256), 256)
    lane = lax.broadcasted_iota(jnp.int32, (256, 128), 1)
    high, low = lane == place.e, lane == place.e + 16
    weight = jnp.sum(
        jnp.where(high | low, x[rows, WIDTH:EXT].astype(F32), 0.0), -1, keepdims=True
    )
    pair_grad = jnp.zeros((256, 1), F32)
    for h in range(2):
        cols = slice(h * 256, (h + 1) * 256)
        gate_pre = dot_nn(x[rows, :WIDTH], gates_w[h][...])
        up_pre = dot_nn(x[rows, :WIDTH], ups_w[h][...])
        back = dot_nt(g[rows, :], downs_w[h][...])
        sig = jax.nn.sigmoid(gate_pre)
        act = gate_pre * sig
        hidden = act * up_pre
        pair_grad = pair_grad + jnp.sum(hidden * back, -1, keepdims=True)
        grad_hidden = back * weight
        hid[rows, cols] = (hidden * weight).astype(BF16)
        dgate[rows, cols] = (grad_hidden * up_pre * (sig + act * (1.0 - sig))).astype(BF16)
        dup[rows, cols] = (grad_hidden * act).astype(BF16)
    coarse = pair_grad.astype(BF16).astype(F32)
    ext = jnp.where(high, coarse, jnp.where(low, pair_grad - coarse, 0.0))
    put(place, i, in_s, in_t, slice(WIDTH, EXT), ext)
    for n in range(4):
        cols = slice(n * 256, (n + 1) * 256)
        value = (
            dot_nt(dgate[rows, 0:256], gates_w[0][cols, :])
            + dot_nt(dgate[rows, 256:512], gates_w[1][cols, :])
            + dot_nt(dup[rows, 0:256], ups_w[0][cols, :])
            + dot_nt(dup[rows, 256:512], ups_w[1][cols, :])
        )
        put(place, i, in_s, in_t, cols, value)
    for n in range(4):
        cols = slice(n * 256, (n + 1) * 256)
        value = dot_nn(hid[rows, 0:256], downs_w[0][:, cols]) + dot_nn(
            hid[rows, 256:512], downs_w[1][:, cols]
        )
        put(place, i, out_s, out_t, cols, value)


def put(place, i, ours, theirs, cols, value):
    half = value.shape[0] // 2
    first, second = value[:half], value[half:]
    is_first = place.core == 0
    ours[i, :, cols] = jnp.where(is_first, first, second).astype(ours.dtype)
    theirs[i, :, cols] = jnp.where(is_first, second, first).astype(theirs.dtype)


def mean_last(v):
    return jnp.sum(v, -1, keepdims=True) * (1.0 / v.shape[-1])


def swapped(v):
    lane = lax.broadcasted_iota(jnp.int32, v.shape, 1)
    return jnp.where(lax.rem(lane, 64) < 32, pltpu.roll(v, 96, 1), pltpu.roll(v, 32, 1))


def doubled(v, half):
    lane = lax.broadcasted_iota(jnp.int32, v.shape, 1)
    one = jnp.where((lane < 64) == (half == 0), v, 0.0)
    return one + pltpu.roll(one, 64, 1)


def stacked(v):
    lane = lax.broadcasted_iota(jnp.int32, v.shape, 1)
    return jnp.concatenate([jnp.where(lane < 64, v, 0.0), jnp.where(lane < 64, 0.0, v)], 0)


def unstacked(v):
    rows = v.shape[0] // 2
    lane = lax.broadcasted_iota(jnp.int32, (rows, 128), 1)
    return jnp.where(lane < 64, v[:rows], v[rows:])


def layer_kernel(
    capacity,
    tokens_ref, cot_ref, gain_one_ref, gain_two_ref, wq_ref, wk_ref, wv_ref, wo_ref, router_ref,
    routes_ref, fill_ref, cos_ref, sin_ref, gate_ref, up_ref, down_ref,
    output_ref, grad_tokens_ref, joint_ref, wo_grad_ref, small_ref,
    ggate_ref, gup_ref, gdown_ref,
    x, g, gate_p, up_p, down_p, hid, dgate, dup,
    in_s, in_t, in_f, out_s, out_t, out_f, in_1, in_2, out_1, out_2, gate_o, up_o, down_o, gate_i, up_i, down_i,
    normed, keys, values, queries, probs, attended, branch_o, branch_i, residual, gates_s, kept_s,
    branch_grad, joint_grad, ext_o, ext_t, small_o, small_i, wo_part,
    j_f, j_1, j_2, w_f, w_1, w_2, e_s, e_t, e_f, e_1, e_2, wide_router,
    ag_ss, ag_rs, sc_ss, sc_rs, sib_ss, sib_rs, y_ss, y_rs,
):
    place = Place()
    mine = pl.ds(pl.multiple_of(place.e * BLK, BLK), BLK)
    own = pl.ds(pl.multiple_of(place.t * BLK, BLK), BLK)
    peers = pl.ds(pl.multiple_of((1 - place.t) * BLK, BLK), BLK)
    gx = Gather(place, x, ag_ss.at[0], ag_rs.at[0])
    gg = Gather(place, g, ag_ss.at[1], ag_rs.at[1])
    gj = Gather(place, joint_ref, ag_ss.at[2], ag_rs.at[2])
    gw = Gather(place, wo_grad_ref, ag_ss.at[3], ag_rs.at[3])
    ge = GatherDirect(place, small_ref, ag_ss.at[4], ag_rs.at[4])

    def scatter(n, *refs):
        return Scatter(place, *refs, sib_ss.at[n], sib_rs.at[n], sc_ss.at[n], sc_rs.at[n])

    si = scatter(0, in_s, in_t, in_f, in_1, in_2)
    so = scatter(1, out_s, out_t, out_f, out_1, out_2)
    narrow = lambda ref, start, size, lanes: ref.at[:, pl.ds(start, size), pl.ds(0, lanes)]
    sj = scatter(2, narrow(in_s, 0, 64, WIDTH), narrow(in_t, 0, 64, WIDTH), j_f, j_1, j_2)
    se = scatter(4, e_s, e_t, e_f, e_1, e_2)
    sw = scatter(3, narrow(in_s, 64, 32, WIDTH), narrow(in_t, 64, 32, WIDTH), w_f, w_1, w_2)

    def across(k):
        src, dst = {
            0: (normed.at[own], normed.at[own]),
            1: (gate_ref, gate_p),
            2: (up_ref, up_p),
            3: (down_ref, down_p),
            4: (branch_o, branch_i),
            5: (gate_o, gate_i),
            6: (up_o, up_i),
            7: (down_o, down_i),
            8: (branch_grad.at[own], branch_grad.at[own]),
            9: (small_o, small_i),
            10: (branch_o, branch_i),
        }[k]
        return pltpu.make_async_remote_copy(
            src_ref=src, dst_ref=dst, send_sem=y_ss.at[k], recv_sem=y_rs.at[k],
            device_id=place.across, device_id_type=MESH,
        )

    def arrived(k):
        ref = {0: normed, 8: branch_grad}.get(k)
        if ref is None:
            across(k).wait_recv()
        else:
            pltpu.make_async_remote_copy(
                src_ref=ref.at[peers], dst_ref=ref.at[peers], send_sem=y_ss.at[k],
                recv_sem=y_rs.at[k], device_id=place.across, device_id_type=MESH,
            ).wait_recv()

    g[mine, :] = cot_ref[...]
    inputs = tokens_ref[...].astype(F32)
    inv_one = lax.rsqrt(mean_last(inputs * inputs) + EPSILON)
    normed[own, :] = (inputs * inv_one * gain_one_ref[...]).astype(BF16)
    place.barrier()
    across(0).start()
    gg.start()

    lane = lax.broadcasted_iota(jnp.int32, (BLK, BLK), 1)
    row = lax.broadcasted_iota(jnp.int32, (BLK, BLK), 0)
    named = jnp.zeros((BLK, BLK), F32)
    routes = routes_ref[...]
    for j in range(routes.shape[0]):
        named = named + (routes[j : j + 1, :] == row).astype(F32)
    named = named.T
    wide_router[0 : router_ref.shape[0], :] = router_ref[...]
    wide_router[router_ref.shape[0] :, :] = jnp.zeros((BLK - router_ref.shape[0], WIDTH), BF16)
    place_of = (fill_ref[...] == row).astype(F32).astype(BF16)
    ordered = dot_tn(place_of, named.astype(BF16))
    earlier = (row > lane).astype(F32).astype(BF16)
    before = dot_nn(earlier, ordered.astype(BF16))
    rank = dot_nn(place_of, before.astype(BF16))
    kept = jnp.where(rank < capacity, named, 0.0)
    kept_s[...] = kept

    def project(rows):
        cos, sin = cos_ref[rows, :], sin_ref[rows, :]
        for n in range(2):
            part = dot_nn(normed[rows, :], wq_ref[:, n * 256 : (n + 1) * 256])
            for m in range(2):
                one = part[:, m * 128 : (m + 1) * 128]
                queries[rows, n * 256 + m * 128 : n * 256 + (m + 1) * 128] = (
                    one * cos + swapped(one) * sin
                ).astype(BF16)
        part = dot_nn(normed[rows, :], wk_ref[...])
        for m in range(2):
            one = part[:, m * 128 : (m + 1) * 128]
            keys[rows, m * 128 : (m + 1) * 128] = (one * cos + swapped(one) * sin).astype(BF16)
        values[rows, :] = dot_nn(normed[rows, :], wv_ref[...]).astype(BF16)

    project(own)
    arrived(0)
    across(1).start()
    project(peers)
    gg.arrive(0)
    gg.arrive_over(0)

    scale = HEAD_DIM ** (-0.5)

    def heads_of(m, half):
        cols = pl.ds(pl.multiple_of(m * 128, 128), 128)
        key = doubled(keys[:, cols].astype(F32), half).astype(BF16)
        value = doubled(values[:, cols].astype(F32), half).astype(BF16)
        j = m * 2 + half
        wide = pl.ds(pl.multiple_of(j * 128, 128), 128)
        query = stacked(queries[:, wide].astype(F32)).astype(BF16)
        return j, wide, key, value, query

    def attend(m, carry):
        place_q = lax.rem(lax.broadcasted_iota(jnp.int32, (512, 256), 0), 256)
        place_k = lax.broadcasted_iota(jnp.int32, (512, 256), 1)
        for half in range(2):
            j, wide, key, value, query = heads_of(m, half)
            scores = jnp.where(place_q >= place_k, dot_nt(query, key) * scale, MASKED)
            raised = jnp.exp(scores - jnp.max(scores, -1, keepdims=True))
            share = raised / jnp.sum(raised, -1, keepdims=True)
            probs[j] = share
            attended[:, wide] = unstacked(dot_nn(share.astype(BF16), value)).astype(BF16)
        return carry

    lax.fori_loop(0, 2, attend, 0)
    gg.arrive(1)
    gg.arrive_over(1, 2)
    branch_o[...] = dot_nn(attended[peers, :], wo_ref[...]).astype(BF16)
    across(4).start()
    own_branch = dot_nn(attended[own, :], wo_ref[...])
    gg.arrive(2)
    gg.arrive_over(3, 4)
    across(4).wait_recv()
    across(2).start()
    across(3).start()
    resid = tokens_ref[...].astype(F32) + own_branch + branch_i[...].astype(F32)
    residual[...] = resid
    inv_two = lax.rsqrt(mean_last(resid * resid) + EPSILON)
    moe_in = (resid * inv_two * gain_two_ref[...]).astype(BF16)
    logits = dot_nt(moe_in, wide_router[...])
    is_named = named > 0.0
    top = jnp.max(jnp.where(is_named, logits, MASKED), -1, keepdims=True)
    raised = jnp.where(is_named, jnp.exp(jnp.minimum(logits - top, 0.0)), 0.0)
    gates = raised / jnp.sum(raised, -1, keepdims=True)
    gates_s[...] = gates
    weights = gates * kept
    coarse = weights.astype(BF16).astype(F32)
    x[mine, :WIDTH] = moe_in
    x[mine, WIDTH:] = (coarse + pltpu.roll(weights - coarse, 16, 1)).astype(BF16)

    gx.start()
    gg.arrive_over(5, 6)
    gates_w, ups_w, downs_w = (gate_ref, gate_p), (up_ref, up_p), (down_ref, down_p)
    gx.arrive(0)
    gx.arrive_over(0)
    gx.arrive(1)
    gx.arrive_over(1, 2)
    gg.from_sib(0, *range(7))
    gg.from_sib(1, *range(7))
    gx.from_sib(0, 0, 1, 2)
    gx.from_sib(1, 0, 1, 2)
    for k in (1, 2, 3):
        across(k).wait_recv()

    def joined(i):
        ring, other = place.step(i, EXPERT_ORDER)
        si.join(other * 4 + ring)
        so.join(other * 4 + ring)

        @pl.when((other == 1) & (i != 3))
        def _():
            si.over_copy(ring).start()

    def chip_step(i, carry):
        @pl.when(i == 2)
        def _():
            gx.arrive(2)
            gx.arrive_over(3, 4)

        @pl.when(i == 4)
        def _():
            gx.arrive_over(5, 6)
            gx.from_sib(0, *range(3, 7))
            gx.from_sib(1, *range(3, 7))

        ring, other = place.step(i, EXPERT_ORDER)
        expert_step(
            place, ring, other, x, g, gates_w, ups_w, downs_w, hid, dgate, dup, in_s, in_t, out_s, out_t
        )
        si.sib_copy(other * 4 + ring).start()
        so.sib_copy(other * 4 + ring).start()

        @pl.when(i >= 1)
        def _():
            joined(i - 1)

        return carry

    lax.fori_loop(0, 8, chip_step, 0)
    joined(jnp.int32(7))
    si.over_copy(place.near(0)).start()
    si.relay(1)

    def grad_step(i, carry):
        @pl.when(i == 3)
        def _():
            si.relay(3)

        @pl.when(i == 5)
        def _():
            si.relay(2)

        @pl.when((i >= 2))
        def _():
            cols = pl.ds(pl.multiple_of((i - 2) * 256, 256), 256)
            turned = x[:, cols].T
            both = dot_nn(turned, dgate[...])
            ggate_ref[cols, :] = both[:, :256].astype(BF16)
            gate_o[cols, :] = both[:, 256:].astype(BF16)
            both = dot_nn(turned, dup[...])
            gup_ref[cols, :] = both[:, :256].astype(BF16)
            up_o[cols, :] = both[:, 256:].astype(BF16)

        @pl.when(i == 0)
        def _():
            down_o[...] = dot_nn(hid[:, 256:].T, g[...]).astype(BF16)

        @pl.when(i == 1)
        def _():
            across(7).start()
            gdown_ref[...] = dot_nn(hid[:, :256].T, g[...]).astype(BF16)

        return carry

    lax.fori_loop(0, 6, grad_step, 0)
    across(5).start()
    for k in (3, 2, 1, 0):
        so.over_copy(place.near(k)).start()

    so.relay(3)
    from_experts = si.total()
    pairs = from_experts[:, WIDTH:]
    gates = gates_s[...]
    grad_gates = (pairs + pltpu.roll(pairs, 112, 1)) * kept_s[...]
    grad_logits = (gates * (grad_gates - jnp.sum(gates * grad_gates, -1, keepdims=True))).astype(BF16)
    grad_moe_in = from_experts[:, :WIDTH] + dot_nn(grad_logits, wide_router[...])
    resid = residual[...]
    inv_two = lax.rsqrt(mean_last(resid * resid) + EPSILON)
    grad_n = grad_moe_in * gain_two_ref[...]
    grad_residual = (
        cot_ref[...].astype(F32)
        + inv_two * grad_n
        - resid * (inv_two * inv_two * inv_two * mean_last(grad_n * resid))
    )
    branch_grad[own, :] = grad_residual.astype(BF16)
    across(8).start()
    grad_tokens_ref[...] = grad_residual
    small = dot_tn(grad_logits, x[mine, :WIDTH])
    ext_o[0:16, :] = small[0:16, :]
    ext_o[16:17, :] = jnp.sum(grad_moe_in * resid * inv_two, 0, keepdims=True)

    def grad_attended(rows):
        joint_grad[rows, :512] = dot_nt(branch_grad[rows, :], wo_ref[...]).astype(BF16)

    grad_attended(own)
    so.relay(2)
    arrived(8)
    across(6).start()
    grad_attended(peers)
    wo_part[...] = dot_tn(attended[...], branch_grad[...]).astype(BF16)

    si.sib_sent()
    si.sent()

    def share_out(n, carry):
        ring, other = place.step(n, PAIR_FIRST)
        start = pl.multiple_of(place.chip(ring, other) * 64, 64)
        i = other * 4 + ring
        put(place, i, sw.sums, sw.theirs, slice(0, WIDTH), wo_part[pl.ds(start, 64), :])
        sw.sib_copy(i).start()
        return carry

    lax.fori_loop(0, 8, share_out, 0)

    def attend_back(m, carry):
        cols = pl.ds(pl.multiple_of(m * 128, 128), 128)
        cos, sin = cos_ref[...], sin_ref[...]
        from_values, from_keys = [], []
        for half in range(2):
            j, wide, key, value, query = heads_of(m, half)
            grad_mixed = stacked(joint_grad[:, wide].astype(F32)).astype(BF16)
            share = probs[j]
            grad_probs = dot_nt(grad_mixed, value)
            grad_scores = (
                share * (grad_probs - jnp.sum(share * grad_probs, -1, keepdims=True)) * scale
            ).astype(BF16)
            grad_query = unstacked(dot_nn(grad_scores, key))
            joint_grad[:, wide] = (grad_query * cos - swapped(grad_query) * sin).astype(BF16)
            one = dot_tn(share.astype(BF16), grad_mixed)
            from_values.append(one + pltpu.roll(one, 64, 1))
            one = dot_tn(grad_scores, query)
            from_keys.append(one + pltpu.roll(one, 64, 1))
        low_lanes = lax.broadcasted_iota(jnp.int32, (256, 128), 1) < 64
        grad_key = jnp.where(low_lanes, from_keys[0], from_keys[1])
        at_key = pl.ds(pl.multiple_of(512 + m * 128, 128), 128)
        at_value = pl.ds(pl.multiple_of(768 + m * 128, 128), 128)
        joint_grad[:, at_key] = (grad_key * cos - swapped(grad_key) * sin).astype(BF16)
        joint_grad[:, at_value] = jnp.where(low_lanes, from_values[0], from_values[1]).astype(BF16)
        return carry

    so.relay(1)
    lax.fori_loop(0, 2, attend_back, 0)

    def share_joint(n, carry):
        ring, other = place.step(n, PAIR_FIRST)
        i = other * 4 + ring
        cols = pl.ds(pl.multiple_of(place.chip(ring, other) * 128, 128), 128)
        value = dot_nn(normed[:, cols].T, joint_grad[...])
        put(place, i, sj.sums, sj.theirs, slice(0, WIDTH), value)
        sj.sib_copy(i).start()
        return carry

    lax.fori_loop(0, 8, share_joint, 0)

    def grad_normed(rows):
        grads = joint_grad[rows, :]
        parts = []
        for n in range(4):
            at = slice(n * 256, (n + 1) * 256)
            parts.append(
                dot_nt(grads[:, :512], wq_ref[at, :])
                + dot_nt(grads[:, 512:768], wk_ref[at, :])
                + dot_nt(grads[:, 768:], wv_ref[at, :])
            )
        return jnp.concatenate(parts, 1)

    part = grad_normed(peers)
    across(4).wait_send()
    branch_o[...] = part.astype(BF16)
    gain_sum = jnp.sum(part * normed[peers, :].astype(F32), 0, keepdims=True)
    sj.join_all()
    own_part = grad_normed(own)
    gain_sum = gain_sum + jnp.sum(own_part * normed[own, :].astype(F32), 0, keepdims=True)
    ext_o[17:18, :] = gain_sum / gain_one_ref[...]
    ext_o[18:, :] = jnp.zeros((6, WIDTH), F32)
    across(10).start()
    ext_t[...] = jnp.concatenate([ext_o[...], jnp.zeros((BLK - 24, WIDTH), F32)], 0).T

    def share_ext(n, carry):
        ring, other = place.step(n, PAIR_FIRST)
        rows = pl.ds(pl.multiple_of(place.chip(ring, other) * 128, 128), 128)
        i = other * 4 + ring
        put(place, i, se.sums, se.theirs, slice(0, BLK), ext_t[rows, :])
        se.sib_copy(i).start()
        return carry

    lax.fori_loop(0, 8, share_ext, 0)
    sw.join_all()
    sj.relay(3)
    se.join_all()
    sj.relay(2, 1)
    block = pl.ds(pl.multiple_of(place.e * 64, 64), 64)
    joint_ref[block, :] = sj.total().astype(BF16)
    gj.start()
    sw.relay(3, 2, 1)
    se.relay(3, 2, 1)
    block = pl.ds(pl.multiple_of(place.e * 32, 32), 32)
    wo_grad_ref[block, :] = sw.total().astype(BF16)
    gw.start()
    gj.arrive(0)
    gj.arrive_over(0)
    small_o[...] = se.total()
    across(9).start()
    gj.arrive(1)
    gj.arrive_over(1, 2)
    gw.arrive(0)
    gw.arrive_over(0)

    across(10).wait_recv()
    grad_n = (own_part + branch_i[...].astype(F32)) * gain_one_ref[...]
    inputs = tokens_ref[...].astype(F32)
    inv_one = lax.rsqrt(mean_last(inputs * inputs) + EPSILON)
    grad_tokens_ref[...] = (
        grad_tokens_ref[...]
        + inv_one * grad_n
        - inputs * (inv_one * inv_one * inv_one * mean_last(grad_n * inputs))
    )
    block = pl.ds(pl.multiple_of(place.e * 64, 64), 64)
    across(9).wait_recv()
    small_ref[block, :] = small_o[...] + small_i[...]
    ge.start()
    gj.arrive(2)
    gj.arrive_over(3, 4)
    gw.arrive(1)
    gw.arrive_over(1, 2)
    ge.arrive(1, 2, 3)
    output_ref[...] = (residual[...] + so.total()).astype(BF16)
    for k, total, part in ((7, gdown_ref, down_i), (5, ggate_ref, gate_i), (6, gup_ref, up_i)):
        across(k).wait_recv()
        total[...] = (total[...].astype(F32) + part[...].astype(F32)).astype(BF16)
    gj.arrive_over(5, 6)
    gw.arrive(2)
    gw.arrive_over(3, 4)
    ge.arrive_over(0, 1, 2, 3)
    gw.arrive_over(5, 6)
    for tree in (gj, gw):
        tree.from_sib(0, *range(7))
        tree.from_sib(1, *range(7))
    ge.from_sib()
    for k in (0, 1, 2, 3, 5, 6, 7, 8, 9, 10):
        across(k).wait_send()
    for tree in (so, sj, sw, se):
        tree.sib_sent()
    for tree in (gx, gg, gj, gw, ge, so, sj, sw, se):
        tree.sent()


def layer_call(capacity, *operands):
    vm, dma = pltpu.VMEM, pltpu.SemaphoreType.DMA
    spec = pl.BlockSpec(memory_space=pltpu.VMEM)
    sds = jax.ShapeDtypeStruct

    def body(*refs):
        return layer_kernel(capacity, *refs)

    outs = (
        sds((BLK, WIDTH), BF16),
        sds((BLK, WIDTH), F32),
        sds((WIDTH, WIDTH), BF16),
        sds((HALF, WIDTH), BF16),
        sds((WIDTH, BLK), F32),
        sds((WIDTH, 256), BF16),
        sds((WIDTH, 256), BF16),
        sds((256, WIDTH), BF16),
    )
    return pl.pallas_call(
        body,
        out_shape=outs,
        in_specs=[spec] * len(operands),
        out_specs=[spec] * len(outs),
        scratch_shapes=[
            vm((2048, EXT), BF16), vm((2048, WIDTH), BF16),
            vm((WIDTH, 256), BF16), vm((WIDTH, 256), BF16), vm((256, WIDTH), BF16),
            vm((2048, 512), BF16), vm((2048, 512), BF16), vm((2048, 512), BF16),
            vm((8, BLK, EXT), BF16), vm((8, BLK, EXT), BF16), vm((8, BLK, EXT), BF16),
            vm((8, BLK, WIDTH), BF16), vm((8, BLK, WIDTH), BF16), vm((8, BLK, WIDTH), BF16),
            vm((4, BLK, EXT), BF16), vm((4, BLK, EXT), BF16),
            vm((4, BLK, WIDTH), BF16), vm((4, BLK, WIDTH), BF16),
            vm((WIDTH, 256), BF16), vm((WIDTH, 256), BF16), vm((256, WIDTH), BF16),
            vm((WIDTH, 256), BF16), vm((WIDTH, 256), BF16), vm((256, WIDTH), BF16),
            vm((256, WIDTH), BF16), vm((256, 256), BF16), vm((256, 256), BF16), vm((256, 512), BF16),
            vm((4, 512, 256), F32), vm((256, 512), BF16),
            vm((BLK, WIDTH), BF16), vm((BLK, WIDTH), BF16), vm((BLK, WIDTH), F32),
            vm((BLK, BLK), F32), vm((BLK, BLK), F32),
            vm((256, WIDTH), BF16), vm((256, WIDTH), BF16),
            vm((24, WIDTH), F32), vm((WIDTH, BLK), F32), vm((64, BLK), F32), vm((64, BLK), F32), vm((512, WIDTH), BF16),
            vm((8, 64, WIDTH), BF16), vm((4, 64, WIDTH), BF16), vm((4, 64, WIDTH), BF16),
            vm((8, 32, WIDTH), BF16), vm((4, 32, WIDTH), BF16), vm((4, 32, WIDTH), BF16),
            vm((8, 64, BLK), F32), vm((8, 64, BLK), F32), vm((8, 64, BLK), F32),
            vm((4, 64, BLK), F32), vm((4, 64, BLK), F32), vm((BLK, WIDTH), BF16),
            dma((5, 27)), dma((5, 27)), dma((5, 7)), dma((5, 8)), dma((5, 8)), dma((5, 8)),
            dma((11,)), dma((11,)),
        ],
        compiler_params=pltpu.CompilerParams(
            collective_id=1, has_side_effects=True, vmem_limit_bytes=63 * 2**20
        ),
        cost_estimate=pl.CostEstimate(flops=24 * 10**9, bytes_accessed=10**7, transcendentals=10**6),
        name="layer",
    )(*operands)


def finish_kernel(
    joint_ref, wo_ref, small_ref, *refs,
):
    copied = refs[:5]
    query_out, key_out, value_out, wo_out, router_out, gain_one_out, gain_two_out = refs[5:12]
    query_out[...] = joint_ref[:, :512].astype(F32)
    key_out[...] = joint_ref[:, 512:768].astype(F32)
    value_out[...] = joint_ref[:, 768:].astype(F32)
    wo_out[...] = wo_ref[...].astype(F32)
    small = small_ref[...].T
    experts = router_out.shape[0]
    router_out[...] = small[:experts, :]
    gain_two_out[...] = small[experts : experts + 1, :]
    gain_one_out[...] = small[experts + 1 : experts + 2, :]
    for source, out in zip(copied, refs[12:]):
        out[...] = source[...].astype(out.dtype)


def finish_call(*operands):
    steps = 4
    sds = jax.ShapeDtypeStruct

    def rows(shape):
        if shape[0] < BLK:
            return pl.BlockSpec((shape[0], shape[1] // steps), lambda i: (0, i))
        return pl.BlockSpec((shape[0] // steps, shape[1]), lambda i: (i, 0))

    outs = [
        sds(shape, F32)
        for shape in (
            (WIDTH, 512), (WIDTH, 256), (WIDTH, 256), (HALF, WIDTH), (16, WIDTH), (1, WIDTH), (1, WIDTH),
            (WIDTH, 256), (WIDTH, 256), (256, WIDTH), (BLK, WIDTH),
        )
    ] + [sds((BLK, WIDTH), BF16)]
    return pl.pallas_call(
        finish_kernel,
        out_shape=outs,
        grid=(steps,),
        in_specs=[rows(a.shape) for a in operands],
        out_specs=[rows(a.shape) for a in outs],
        compiler_params=pltpu.CompilerParams(vmem_limit_bytes=62 * 2**20),
        cost_estimate=pl.CostEstimate(flops=10**6, bytes_accessed=16 * 10**6, transcendentals=0),
        name="finish",
    )(*operands)


def tables(rows):
    half = HEAD_DIM // 2
    freqs = np.exp(np.arange(half, dtype=np.float32) * np.float32(-2.0 * math.log(THETA_BASE) / HEAD_DIM))
    angles = np.arange(rows, dtype=np.float32)[:, None] * freqs[None, :]
    cos, sin = np.cos(angles), np.sin(angles)
    return (
        np.concatenate([cos] * 4, 1).astype(np.float32),
        np.concatenate([-sin, sin] * 2, 1).astype(np.float32),
    )


def on_device(
    tokens,
    gain_attn,
    w_query,
    w_key,
    w_value,
    w_out,
    gain_moe,
    router,
    expert_gate,
    expert_up,
    expert_down,
    routes,
    fill_order,
    cotangent,
):
    tok_rows, width = tokens.shape
    tensor_size = lax.axis_size("tensor")
    seq_rows = tok_rows * tensor_size
    head_size = HEAD_DIM
    q_cols = w_query.shape[1]
    kv_cols = w_key.shape[1]
    q_heads = q_cols // head_size
    kv_heads = kv_cols // head_size
    q_group = q_heads // kv_heads
    score_scale = head_size ** (-0.5)
    local_experts = expert_gate.shape[0]
    expert_groups = lax.axis_size("expert")
    experts = local_experts * expert_groups
    top_k = routes.shape[1]
    capacity = (5 * tok_rows * top_k + 4 * experts - 1) // (4 * experts)
    gate_w, up_w, down_w = (expert_gate, expert_up, expert_down)
    inputs = tokens.astype(jnp.float32)
    inv_one = lax.rsqrt(jnp.mean(inputs * inputs, -1, keepdims=True) + EPSILON)
    normed = (inputs * inv_one * gain_attn).astype(jnp.bfloat16)
    normed_all = lax.all_gather(normed, "tensor", axis=0, tiled=True)
    w_joint = jnp.concatenate([w_query, w_key, w_value], 1)
    joint = jnp.dot(normed_all, w_joint, preferred_element_type=jnp.float32)
    angles = angles_of(seq_rows, head_size)
    queries = rotate(joint[:, :q_cols].reshape(seq_rows, q_heads, head_size), angles, 1.0).astype(
        jnp.bfloat16
    )
    key_rows = rotate(
        joint[:, q_cols : q_cols + kv_cols].reshape(seq_rows, kv_heads, head_size), angles, 1.0
    ).astype(jnp.bfloat16)
    value_rows = (
        joint[:, q_cols + kv_cols :].astype(jnp.bfloat16).reshape(seq_rows, kv_heads, head_size)
    )
    q_size = min(512, seq_rows)
    blocks = seq_rows // q_size
    key_pos = jnp.arange(seq_rows)

    def scores_of(q_block, row_start):
        grouped = q_block.reshape(q_size, kv_heads, q_group, head_size)
        raw_scores = (
            jnp.einsum("qkgd,tkd->kgqt", grouped, key_rows, preferred_element_type=jnp.float32)
            * score_scale
        )
        allowed = (row_start + jnp.arange(q_size))[:, None] >= key_pos[None, :]
        return (grouped, jnp.where(allowed, raw_scores, MASKED))

    def forward_block(block_args):
        q_block, row_start = block_args
        grouped, scores = scores_of(q_block, row_start)
        top_score = jnp.max(scores, -1, keepdims=True)
        exp_scores = jnp.exp(scores - top_score)
        row_total = jnp.sum(exp_scores, -1, keepdims=True)
        attn_probs = (exp_scores / row_total).astype(jnp.bfloat16)
        mixed_rows = jnp.einsum(
            "kgqt,tkd->qkgd", attn_probs, value_rows, preferred_element_type=jnp.float32
        )
        return (mixed_rows.astype(jnp.bfloat16).reshape(q_size, q_cols), top_score, row_total)

    q_blocks = queries.reshape(blocks, q_size, q_heads, head_size)
    starts = jnp.arange(blocks) * q_size
    attended, maxima, totals = lax.map(forward_block, (q_blocks, starts))
    attended = attended.reshape(seq_rows, q_cols)
    row_block = attended
    branch = lax.psum_scatter(
        jnp.dot(row_block, w_out, preferred_element_type=jnp.float32),
        "tensor",
        scatter_dimension=0,
        tiled=True,
    )
    residual = inputs + branch
    inv_two = lax.rsqrt(jnp.mean(residual * residual, -1, keepdims=True) + EPSILON)
    scaled = residual * inv_two
    moe_in = (scaled * gain_moe).astype(jnp.bfloat16)
    logits = jnp.dot(moe_in, router, preferred_element_type=jnp.float32)
    expert_ids = jnp.arange(experts, dtype=jnp.int32)
    named = jnp.sum((routes[:, :, None] == expert_ids[None, None, :]).astype(jnp.float32), 1)
    place_of = (fill_order[0][:, None] == jnp.arange(tok_rows)[None, :]).astype(jnp.bfloat16)
    ordered = jnp.dot(place_of, named.astype(jnp.bfloat16), preferred_element_type=jnp.float32)
    earlier = (jnp.arange(tok_rows)[:, None] > jnp.arange(tok_rows)[None, :]).astype(jnp.bfloat16)
    before = jnp.dot(earlier, ordered.astype(jnp.bfloat16), preferred_element_type=jnp.float32)
    rank = contract_first(place_of, before.astype(jnp.bfloat16))
    kept = named * (rank < capacity).astype(jnp.float32)
    top_logit = jnp.max(jnp.where(named > 0, logits, MASKED), -1, keepdims=True)
    exp_logits = jnp.where(named > 0, jnp.exp(jnp.minimum(logits - top_logit, 0.0)), 0.0)
    gates = exp_logits / jnp.sum(exp_logits, -1, keepdims=True)
    weights = gates * kept

    gate_all = lax.all_gather(gate_w[0], "tensor", axis=1, tiled=True)
    up_all = lax.all_gather(up_w[0], "tensor", axis=1, tiled=True)
    down_all = lax.all_gather(down_w[0], "tensor", axis=0, tiled=True)
    grad_out = cotangent.astype(jnp.float32)
    plane_cot = lax.all_gather(cotangent, "expert", axis=0, tiled=True)
    plane_in = lax.all_gather(moe_in, "expert", axis=0, tiled=True)
    plane_weights = lax.all_gather(weights, "expert", axis=0, tiled=True)
    mine = (expert_ids == lax.axis_index("expert")).astype(jnp.float32)
    my_weight = jnp.sum(plane_weights * mine[None, :], -1, keepdims=True)

    gate_pre = jnp.dot(plane_in, gate_all, preferred_element_type=jnp.float32)
    up_pre = jnp.dot(plane_in, up_all, preferred_element_type=jnp.float32)
    back_down = contract_last(plane_cot, down_all)
    gate_sigmoid = jax.nn.sigmoid(gate_pre)
    active = gate_pre * gate_sigmoid
    hidden = active * up_pre
    pair_grad = jnp.sum(hidden * back_down, -1, keepdims=True)
    hidden_w = (hidden * my_weight).astype(jnp.bfloat16)
    grad_hidden = back_down * my_weight
    grad_gate_pre = (
        grad_hidden * up_pre * gate_sigmoid * (1.0 + gate_pre * (1.0 - gate_sigmoid))
    ).astype(jnp.bfloat16)
    grad_up_pre = (grad_hidden * active).astype(jnp.bfloat16)
    out_part = jnp.dot(hidden_w, down_all, preferred_element_type=jnp.float32)
    in_part = contract_last(grad_gate_pre, gate_all) + contract_last(grad_up_pre, up_all)
    out_sum = lax.psum_scatter(
        out_part.astype(jnp.bfloat16), "expert", scatter_dimension=0, tiled=True
    )
    in_sum = lax.psum_scatter(
        in_part.astype(jnp.bfloat16), "expert", scatter_dimension=0, tiled=True
    )
    grad_gates = lax.psum_scatter(
        pair_grad * mine[None, :], "expert", scatter_dimension=0, tiled=True
    ) * kept
    grad_down = lax.psum_scatter(
        contract_first(hidden_w, plane_cot).astype(jnp.bfloat16),
        "tensor", scatter_dimension=0, tiled=True,
    ).astype(jnp.float32)[None]
    grad_gate = lax.psum_scatter(
        contract_first(plane_in, grad_gate_pre).astype(jnp.bfloat16),
        "tensor", scatter_dimension=1, tiled=True,
    ).astype(jnp.float32)[None]
    grad_up = lax.psum_scatter(
        contract_first(plane_in, grad_up_pre).astype(jnp.bfloat16),
        "tensor", scatter_dimension=1, tiled=True,
    ).astype(jnp.float32)[None]
    output_rows = residual + out_sum.astype(jnp.float32)
    grad_logits = (
        gates * (grad_gates - jnp.sum(gates * grad_gates, -1, keepdims=True))
    ).astype(jnp.bfloat16)
    grad_moe_in = in_sum.astype(jnp.float32) + contract_last(grad_logits, router)
    grad_router = contract_first(moe_in, grad_logits)
    grad_gain_moe = jnp.sum(grad_moe_in * scaled, 0)
    grad_norm_two = grad_moe_in * gain_moe
    grad_residual = (
        grad_out
        + inv_two * grad_norm_two
        - residual * inv_two**3 * jnp.mean(grad_norm_two * residual, -1, keepdims=True)
    )
    grad_branch = grad_residual.astype(jnp.bfloat16)
    shard_piece = lax.all_gather(grad_branch, "tensor", axis=0, tiled=True)
    grad_part = contract_last(shard_piece, w_out).astype(jnp.bfloat16)
    grad_mixed = grad_part
    grad_wout = contract_first(attended, shard_piece)
    grad_mixed, grad_w_out = (grad_mixed, grad_wout)
    grad_blocks = grad_mixed.reshape(blocks, q_size, q_heads, head_size)

    def backward_block(carry, block_args):
        grad_keys, grad_values = carry
        q_block, grad_block, row_start, top_score, row_total = block_args
        grouped, scores = scores_of(q_block, row_start)
        attn_probs = jnp.exp(scores - top_score) / row_total
        grad_grouped = grad_block.reshape(q_size, kv_heads, q_group, head_size)
        grad_probs = jnp.einsum(
            "qkgd,tkd->kgqt", grad_grouped, value_rows, preferred_element_type=jnp.float32
        )
        grad_values = grad_values + jnp.einsum(
            "kgqt,qkgd->tkd",
            attn_probs.astype(jnp.bfloat16),
            grad_grouped,
            preferred_element_type=jnp.float32,
        )
        grad_scores = (
            attn_probs
            * (grad_probs - jnp.sum(attn_probs * grad_probs, -1, keepdims=True))
            * score_scale
        ).astype(jnp.bfloat16)
        grad_query = jnp.einsum(
            "kgqt,tkd->qkgd", grad_scores, key_rows, preferred_element_type=jnp.float32
        ).reshape(q_size, q_heads, head_size)
        grad_keys = grad_keys + jnp.einsum(
            "kgqt,qkgd->tkd", grad_scores, grouped, preferred_element_type=jnp.float32
        )
        return ((grad_keys, grad_values), grad_query)

    zero_rows = jnp.zeros((seq_rows, kv_heads, head_size), jnp.float32)
    (grad_keys, grad_values), grad_queries = lax.scan(
        backward_block, (zero_rows, zero_rows), (q_blocks, grad_blocks, starts, maxima, totals)
    )
    grad_queries = grad_queries.reshape(seq_rows, q_heads, head_size)
    grad_q = rotate(grad_queries, angles, -1.0).astype(jnp.bfloat16).reshape(seq_rows, q_cols)
    grad_k = rotate(grad_keys, angles, -1.0).astype(jnp.bfloat16).reshape(seq_rows, kv_cols)
    grad_v = grad_values.astype(jnp.bfloat16).reshape(seq_rows, kv_cols)
    grad_joint = jnp.concatenate([grad_q, grad_k, grad_v], 1)
    grad_w_joint = contract_first(normed_all, grad_joint)
    row_block = grad_joint
    grad_normed = lax.psum_scatter(
        contract_last(row_block, w_joint), "tensor", scatter_dimension=0, tiled=True
    )
    grad_gain_attn = jnp.sum(grad_normed * inputs * inv_one, 0)
    grad_norm_one = grad_normed * gain_attn
    grad_tokens = (
        grad_residual
        + inv_one * grad_norm_one
        - inputs * inv_one**3 * jnp.mean(grad_norm_one * inputs, -1, keepdims=True)
    )
    summed_joint, summed_out = lax.psum((grad_w_joint, grad_w_out), "expert")
    summed_gain_attn, summed_gain_moe, summed_router = lax.psum(
        (grad_gain_attn, grad_gain_moe, grad_router), ("expert", "tensor")
    )
    return (
        output_rows.astype(jnp.bfloat16),
        grad_tokens,
        summed_gain_attn,
        summed_joint[:, :q_cols],
        summed_joint[:, q_cols : q_cols + kv_cols],
        summed_joint[:, q_cols + kv_cols :],
        summed_out,
        summed_gain_moe,
        summed_router,
        grad_gate,
        grad_up,
        grad_down,
    )


def by_kernel(
    tokens,
    gain_attn,
    w_query,
    w_key,
    w_value,
    w_out,
    gain_moe,
    router,
    expert_gate,
    expert_up,
    expert_down,
    routes,
    fill_order,
    cotangent,
):
    tok_rows = tokens.shape[0]
    experts = router.shape[1]
    capacity = (5 * tok_rows * routes.shape[1] + 4 * experts - 1) // (4 * experts)
    cos, sin = tables(tok_rows * 2)
    out, grad_tokens, joint, wo_grad, small, *expert_grads = layer_call(
        capacity,
        tokens, cotangent, gain_attn[None], gain_moe[None], w_query, w_key, w_value, w_out,
        router.T, routes.T, fill_order, jnp.asarray(cos), jnp.asarray(sin),
        expert_gate[0], expert_up[0], expert_down[0],
    )
    gq, gk, gv, gwo, grad_router, grad_one, grad_two, ggate, gup, gdown, grad_tokens, out = finish_call(
        joint, wo_grad, small, *expert_grads, grad_tokens, out
    )
    return (
        out,
        grad_tokens,
        grad_one[0],
        gq,
        gk,
        gv,
        gwo,
        grad_two[0],
        grad_router.T,
        ggate[None],
        gup[None],
        gdown[None],
    )


def kernel_fits(mesh_shape, shapes):
    return mesh_shape == (16, 2) and shapes == (
        (128, 1024), (1024,), (1024, 512), (1024, 256), (1024, 256), (512, 1024), (1024,), (1024, 16),
        (1, 1024, 256), (1, 1024, 256), (1, 256, 1024), (128, 8), (1, 128), (128, 1024),
    )


def on_any(*operands):
    sizes = (lax.axis_size("expert"), lax.axis_size("tensor"))
    if kernel_fits(sizes, tuple(a.shape for a in operands)):
        return by_kernel(*operands)
    return on_device(*operands)


def solution(mesh):
    placed = (
        P(("expert", "tensor"), None),
        P(),
        P(None, "tensor"),
        P(None, "tensor"),
        P(None, "tensor"),
        P("tensor", None),
        P(),
        P(),
        P("expert", None, "tensor"),
        P("expert", None, "tensor"),
        P("expert", "tensor", None),
        P(("expert", "tensor"), None),
        P(("expert", "tensor"), None),
        P(("expert", "tensor"), None),
    )
    return jax.shard_map(
        on_any,
        mesh=mesh,
        in_specs=placed,
        out_specs=(
            P(("expert", "tensor"), None),
            P(("expert", "tensor"), None),
            P(),
            P(None, "tensor"),
            P(None, "tensor"),
            P(None, "tensor"),
            P("tensor", None),
            P(),
            P(),
            P("expert", None, "tensor"),
            P("expert", None, "tensor"),
            P("expert", "tensor", None),
        ),
        check_vma=False,
    )
```

```python
import math

import jax
import jax.numpy as jnp
import numpy as np
from jax import lax
from jax.experimental import pallas as pl
from jax.experimental.pallas import tpu as pltpu
from jax.sharding import PartitionSpec as P

HEAD_DIM = 64


EPSILON = 1e-06
THETA_BASE = 10000.0
MASKED = -1e30


def angles_of(row_count, head_size):
    half = head_size // 2
    freqs = jnp.exp(jnp.arange(half, dtype=jnp.float32) * (-2.0 * math.log(THETA_BASE) / head_size))
    return jnp.arange(row_count, dtype=jnp.float32)[:, None] * freqs[None, :]


def rotate(vectors, angles, sign):
    half = vectors.shape[-1] // 2
    cosine = jnp.cos(angles)[:, None, :]
    sine = sign * jnp.sin(angles)[:, None, :]
    first = vectors[..., :half]
    second = vectors[..., half:]
    return jnp.concatenate([first * cosine - second * sine, second * cosine + first * sine], -1)


def contract_last(left, right):
    return lax.dot_general(
        left, right, (((1,), (1,)), ((), ())), preferred_element_type=jnp.float32
    )


def contract_first(left, right):
    return lax.dot_general(
        left, right, (((0,), (0,)), ((), ())), preferred_element_type=jnp.float32
    )


F32 = jnp.float32
BF16 = jnp.bfloat16
MESH = pl.DeviceIdType.MESH
BLK = 128
WIDTH = 1024
EXT = 1152
HALF = 512
NEAREST = (0, 1, 2, 3, 1, 0, 2, 3, 2, 3, 1, 0, 3, 2, 1, 0)
EXPERT_ORDER = ((0, 0), (1, 1), (1, 0), (0, 1), (3, 1), (3, 0), (2, 1), (2, 0))
PAIR_FIRST = ((3, 1), (2, 1), (1, 1), (0, 1), (3, 0), (2, 0), (1, 0), (0, 0))


def pick(i, values):
    out = jnp.int32(values[-1])
    for n in range(len(values) - 2, -1, -1):
        out = jnp.where(i == n, jnp.int32(values[n]), out)
    return out


class Place:
    def __init__(self):
        e = lax.axis_index("expert")
        t = lax.axis_index("tensor")
        self.e = e
        self.t = t
        self.core = lax.rem(e, 2)
        self.pair = lax.rem(e // 2, 2)
        self.ring = e // 4
        self.other = (e + 2 - 4 * self.pair, t)
        self.sib = (e + 1 - 2 * self.core, t)
        self.across = (e, 1 - t)

    def at(self, ring):
        return (ring * 4 + lax.rem(self.e, 4), self.t)

    def chip(self, ring, other):
        return ring * 2 + (self.pair + other - 2 * self.pair * other)

    def step(self, i, order):
        ring = self.near(pick(i, [k for k, _ in order]))
        return ring, pick(i, [other for _, other in order])

    def near(self, k):
        return pick(self.ring * 4 + k, NEAREST)

    def barrier(self):
        bar = pltpu.get_barrier_semaphore()
        for dest in [self.at(lax.rem(self.ring + m, 4)) for m in (1, 2, 3)] + [
            self.other, self.sib, self.across,
        ]:
            pl.semaphore_signal(bar, inc=1, device_id=dest, device_id_type=MESH)
        pl.semaphore_wait(bar, 6)


def if_(condition, action):
    if condition is True:
        action()
    else:
        pl.when(condition)(action)


class Gather:
    def __init__(self, place, buf, send_sems, recv_sems):
        self.place, self.buf, self.ss, self.rs = place, buf, send_sems, recv_sems
        self.size = buf.shape[0] // 16

    def where(self, n):
        r = self.place.ring
        if n == 0:
            return r, True
        j = (n - 1) // 2
        return (r - 1 - j, r > j) if n % 2 else (r + 1 + j, 3 - r > j)

    def copy(self, ring, other, core, sem, dest):
        block = self.place.chip(ring, other) * 2 + core
        ref = self.buf.at[pl.ds(pl.multiple_of(block * self.size, self.size), self.size)]
        return pltpu.make_async_remote_copy(
            src_ref=ref, dst_ref=ref, send_sem=self.ss.at[sem], recv_sem=self.rs.at[sem],
            device_id=dest, device_id_type=MESH,
        )

    def up(self, k):
        r = self.place.ring
        return self.copy(r - k, 0, self.place.core, k, self.place.at(r + 1))

    def down(self, k):
        r = self.place.ring
        return self.copy(r + k, 0, self.place.core, 3 + k, self.place.at(r - 1))

    def over(self, n, arriving=0):
        return self.copy(self.where(n)[0], arriving, self.place.core, 6 + n, self.place.other)

    def to_sib(self, n, other, arriving=False):
        core = 1 - self.place.core if arriving else self.place.core
        return self.copy(self.where(n)[0], other, core, 13 + 7 * other + n, self.place.sib)

    def start(self):
        r = self.place.ring
        if_(r < 3, lambda: self.up(0).start())
        if_(r > 0, lambda: self.down(0).start())
        self.over(0).start()
        self.to_sib(0, 0).start()

    def arrive(self, j):
        r = self.place.ring

        def from_below():
            self.copy(r - 1 - j, 0, self.place.core, j, self.place.other).wait_recv()
            if j < 2:
                if_(r < 3, lambda: self.up(j + 1).start())
            self.over(1 + 2 * j).start()
            self.to_sib(1 + 2 * j, 0).start()

        def from_above():
            self.copy(r + 1 + j, 0, self.place.core, 3 + j, self.place.other).wait_recv()
            if j < 2:
                if_(r > 0, lambda: self.down(j + 1).start())
            self.over(2 + 2 * j).start()
            self.to_sib(2 + 2 * j, 0).start()

        if_(r > j, from_below)
        if_(3 - r > j, from_above)

    def arrive_over(self, *numbers):
        for n in numbers:

            def taken(n=n):
                self.over(n, 1).wait_recv()
                self.to_sib(n, 1).start()

            if_(self.where(n)[1], taken)

    def from_sib(self, other, *numbers):
        for n in numbers:
            if_(self.where(n)[1], lambda n=n: self.to_sib(n, other, True).wait_recv())

    def sent(self):
        r = self.place.ring
        for k in range(3):
            if_((r < 3) & (r >= k), lambda k=k: self.up(k).wait_send())
            if_((r > 0) & (3 - r >= k), lambda k=k: self.down(k).wait_send())
        for n in range(7):

            def all_of(n=n):
                self.over(n).wait_send()
                self.to_sib(n, 0).wait_send()
                self.to_sib(n, 1).wait_send()

            if_(self.where(n)[1], all_of)


class GatherDirect(Gather):
    def span(self, k, sending):
        ring = self.place.near(k)
        r = self.place.ring
        m = lax.rem((ring - r if sending else r - ring) + 4, 4)
        source = r if sending else ring
        return self.copy(source, 0, self.place.core, m - 1, self.place.at(ring))

    def over(self, k, arriving=0):
        return self.copy(self.place.near(k), arriving, self.place.core, 3 + k, self.place.other)

    def to_sib(self, k, other, arriving=False):
        core = 1 - self.place.core if arriving else self.place.core
        return self.copy(self.place.near(k), other, core, 7 + 4 * other + k, self.place.sib)

    def start(self):
        for k in (1, 2, 3):
            self.span(k, True).start()
        self.over(0).start()
        self.to_sib(0, 0).start()

    def arrive(self, *ks):
        for k in ks:
            self.span(k, False).wait_recv()
            self.over(k).start()
            self.to_sib(k, 0).start()

    def arrive_over(self, *ks):
        for k in ks:
            self.over(k, 1).wait_recv()
            self.to_sib(k, 1).start()

    def from_sib(self):
        for other in range(2):
            for k in range(4):
                self.to_sib(k, other, True).wait_recv()

    def sent(self):
        for k in range(4):
            if k:
                self.span(k, True).wait_send()
            self.over(k).wait_send()
            self.to_sib(k, 0).wait_send()
            self.to_sib(k, 1).wait_send()


class Scatter:
    def __init__(self, place, sums, theirs, from_sib, over, along, sib_ss, sib_rs, ss, rs):
        self.place, self.sums, self.theirs, self.from_sib = place, sums, theirs, from_sib
        self.over, self.along = over, along
        self.sib_ss, self.sib_rs, self.ss, self.rs = sib_ss, sib_rs, ss, rs

    def sib_copy(self, i):
        return pltpu.make_async_remote_copy(
            src_ref=self.theirs.at[i], dst_ref=self.from_sib.at[i],
            send_sem=self.sib_ss.at[i], recv_sem=self.sib_rs.at[i],
            device_id=self.place.sib, device_id_type=MESH,
        )

    def join(self, i):
        self.sib_copy(i).wait_recv()
        total = self.sums[i].astype(F32) + self.from_sib[i].astype(F32)
        self.sums[i] = total.astype(self.from_sib.dtype)

    def join_all(self):
        for k, other in PAIR_FIRST:
            ring = self.place.near(k)
            self.join(other * 4 + ring)
            if other:
                self.over_copy(ring).start()

    def over_copy(self, ring):
        return pltpu.make_async_remote_copy(
            src_ref=self.sums.at[4 + ring], dst_ref=self.over.at[ring],
            send_sem=self.ss.at[ring], recv_sem=self.rs.at[ring],
            device_id=self.place.other, device_id_type=MESH,
        )

    def along_copy(self, k, ring, slot):
        return pltpu.make_async_remote_copy(
            src_ref=self.sums.at[self.place.near(k)], dst_ref=self.along.at[slot],
            send_sem=self.ss.at[3 + k], recv_sem=self.rs.at[4 + slot],
            device_id=self.place.at(ring), device_id_type=MESH,
        )

    def relay(self, *ks):
        r = self.place.ring
        at_end = (r == 0) | (r == 3)
        beside = self.place.near(1)
        for k in ks:
            ring = self.place.near(k)

            def add(*others, ring=ring):
                total = self.sums[ring].astype(F32)
                for other in others:
                    total = total + other.astype(F32)
                self.sums[ring] = total.astype(self.over.dtype)

            self.over_copy(ring).wait_recv()
            if k == 1:
                add(self.over[ring])
                self.along_copy(1, ring, 0).start()
                continue

            @pl.when(at_end)
            def _(k=k, ring=ring):
                add(self.over[ring])
                self.along_copy(k, beside, k).start()

            @pl.when(jnp.logical_not(at_end))
            def _(k=k, ring=ring):
                self.along_copy(k, beside, k).wait_recv()
                add(self.over[ring], self.along[k])
                self.along_copy(k, ring, 1).start()

    def total(self):
        ring = self.place.ring
        self.over_copy(ring).wait_recv()
        for slot in (0, 1):
            self.along_copy(1, self.place.near(1), slot).wait_recv()
        return (self.sums[ring].astype(F32) + self.over[ring].astype(F32)) + (
            self.along[0].astype(F32) + self.along[1].astype(F32)
        )

    def sib_sent(self):
        for i in range(8):
            self.sib_copy(i).wait_send()

    def sent(self):
        for ring in range(4):
            self.over_copy(ring).wait_send()
        for k in (1, 2, 3):
            self.along_copy(k, self.place.near(k), 0).wait_send()


def dot_nn(a, b):
    return lax.dot_general(a, b, (((1,), (0,)), ((), ())), preferred_element_type=F32)


def dot_nt(a, b):
    return lax.dot_general(a, b, (((1,), (1,)), ((), ())), preferred_element_type=F32)


def dot_tn(a, b):
    return lax.dot_general(a, b, (((0,), (0,)), ((), ())), preferred_element_type=F32)


def expert_step(place, ring, other, x, g, gates_w, ups_w, downs_w, hid, dgate, dup, in_s, in_t, out_s, out_t):
    i = other * 4 + ring
    rows = pl.ds(pl.multiple_of(place.chip(ring, other) * 256, 256), 256)
    lane = lax.broadcasted_iota(jnp.int32, (256, 128), 1)
    high, low = lane == place.e, lane == place.e + 16
    weight = jnp.sum(
        jnp.where(high | low, x[rows, WIDTH:EXT].astype(F32), 0.0), -1, keepdims=True
    )
    pair_grad = jnp.zeros((256, 1), F32)
    for h in range(2):
        cols = slice(h * 256, (h + 1) * 256)
        gate_pre = dot_nn(x[rows, :WIDTH], gates_w[h][...])
        up_pre = dot_nn(x[rows, :WIDTH], ups_w[h][...])
        back = dot_nt(g[rows, :], downs_w[h][...])
        sig = jax.nn.sigmoid(gate_pre)
        act = gate_pre * sig
        hidden = act * up_pre
        pair_grad = pair_grad + jnp.sum(hidden * back, -1, keepdims=True)
        grad_hidden = back * weight
        hid[rows, cols] = (hidden * weight).astype(BF16)
        dgate[rows, cols] = (grad_hidden * up_pre * (sig + act * (1.0 - sig))).astype(BF16)
        dup[rows, cols] = (grad_hidden * act).astype(BF16)
    coarse = pair_grad.astype(BF16).astype(F32)
    ext = jnp.where(high, coarse, jnp.where(low, pair_grad - coarse, 0.0))
    put(place, i, in_s, in_t, slice(WIDTH, EXT), ext)
    for n in range(4):
        cols = slice(n * 256, (n + 1) * 256)
        value = (
            dot_nt(dgate[rows, 0:256], gates_w[0][cols, :])
            + dot_nt(dgate[rows, 256:512], gates_w[1][cols, :])
            + dot_nt(dup[rows, 0:256], ups_w[0][cols, :])
            + dot_nt(dup[rows, 256:512], ups_w[1][cols, :])
        )
        put(place, i, in_s, in_t, cols, value)
    for n in range(4):
        cols = slice(n * 256, (n + 1) * 256)
        value = dot_nn(hid[rows, 0:256], downs_w[0][:, cols]) + dot_nn(
            hid[rows, 256:512], downs_w[1][:, cols]
        )
        put(place, i, out_s, out_t, cols, value)


def put(place, i, ours, theirs, cols, value):
    half = value.shape[0] // 2
    first, second = value[:half], value[half:]
    is_first = place.core == 0
    ours[i, :, cols] = jnp.where(is_first, first, second).astype(ours.dtype)
    theirs[i, :, cols] = jnp.where(is_first, second, first).astype(theirs.dtype)


def mean_last(v):
    return jnp.sum(v, -1, keepdims=True) * (1.0 / v.shape[-1])


def swapped(v):
    lane = lax.broadcasted_iota(jnp.int32, v.shape, 1)
    return jnp.where(lax.rem(lane, 64) < 32, pltpu.roll(v, 96, 1), pltpu.roll(v, 32, 1))


def doubled(v, half):
    lane = lax.broadcasted_iota(jnp.int32, v.shape, 1)
    one = jnp.where((lane < 64) == (half == 0), v, 0.0)
    return one + pltpu.roll(one, 64, 1)


def stacked(v):
    lane = lax.broadcasted_iota(jnp.int32, v.shape, 1)
    return jnp.concatenate([jnp.where(lane < 64, v, 0.0), jnp.where(lane < 64, 0.0, v)], 0)


def unstacked(v):
    rows = v.shape[0] // 2
    lane = lax.broadcasted_iota(jnp.int32, (rows, 128), 1)
    return jnp.where(lane < 64, v[:rows], v[rows:])


def layer_kernel(
    capacity,
    tokens_ref, cot_ref, gain_one_ref, gain_two_ref, wq_ref, wk_ref, wv_ref, wo_ref, router_ref,
    routes_ref, fill_ref, cos_ref, sin_ref, gate_ref, up_ref, down_ref,
    output_ref, grad_tokens_ref, joint_ref, wo_grad_ref, small_ref,
    ggate_ref, gup_ref, gdown_ref,
    x, g, gate_p, up_p, down_p, hid, dgate, dup,
    in_s, in_t, in_f, out_s, out_t, out_f, in_1, in_2, out_1, out_2, gate_o, up_o, down_o, gate_i, up_i, down_i,
    normed, keys, values, queries, probs, attended, branch_o, branch_i, residual, gates_s, kept_s,
    branch_grad, joint_grad, ext_o, ext_t, small_o, small_i, wo_part,
    j_f, j_1, j_2, w_f, w_1, w_2, e_s, e_t, e_f, e_1, e_2, wide_router,
    ag_ss, ag_rs, sc_ss, sc_rs, sib_ss, sib_rs, y_ss, y_rs,
):
    place = Place()
    mine = pl.ds(pl.multiple_of(place.e * BLK, BLK), BLK)
    own = pl.ds(pl.multiple_of(place.t * BLK, BLK), BLK)
    peers = pl.ds(pl.multiple_of((1 - place.t) * BLK, BLK), BLK)
    gx = Gather(place, x, ag_ss.at[0], ag_rs.at[0])
    gg = Gather(place, g, ag_ss.at[1], ag_rs.at[1])
    gj = Gather(place, joint_ref, ag_ss.at[2], ag_rs.at[2])
    gw = Gather(place, wo_grad_ref, ag_ss.at[3], ag_rs.at[3])
    ge = GatherDirect(place, small_ref, ag_ss.at[4], ag_rs.at[4])

    def scatter(n, *refs):
        return Scatter(place, *refs, sib_ss.at[n], sib_rs.at[n], sc_ss.at[n], sc_rs.at[n])

    si = scatter(0, in_s, in_t, in_f, in_1, in_2)
    so = scatter(1, out_s, out_t, out_f, out_1, out_2)
    narrow = lambda ref, start, size, lanes: ref.at[:, pl.ds(start, size), pl.ds(0, lanes)]
    sj = scatter(2, narrow(in_s, 0, 64, WIDTH), narrow(in_t, 0, 64, WIDTH), j_f, j_1, j_2)
    se = scatter(4, e_s, e_t, e_f, e_1, e_2)
    sw = scatter(3, narrow(in_s, 64, 32, WIDTH), narrow(in_t, 64, 32, WIDTH), w_f, w_1, w_2)

    def across(k):
        src, dst = {
            0: (normed.at[own], normed.at[own]),
            1: (gate_ref, gate_p),
            2: (up_ref, up_p),
            3: (down_ref, down_p),
            4: (branch_o, branch_i),
            5: (gate_o, gate_i),
            6: (up_o, up_i),
            7: (down_o, down_i),
            8: (branch_grad.at[own], branch_grad.at[own]),
            9: (small_o, small_i),
            10: (branch_o, branch_i),
        }[k]
        return pltpu.make_async_remote_copy(
            src_ref=src, dst_ref=dst, send_sem=y_ss.at[k], recv_sem=y_rs.at[k],
            device_id=place.across, device_id_type=MESH,
        )

    def arrived(k):
        ref = {0: normed, 8: branch_grad}.get(k)
        if ref is None:
            across(k).wait_recv()
        else:
            pltpu.make_async_remote_copy(
                src_ref=ref.at[peers], dst_ref=ref.at[peers], send_sem=y_ss.at[k],
                recv_sem=y_rs.at[k], device_id=place.across, device_id_type=MESH,
            ).wait_recv()

    g[mine, :] = cot_ref[...]
    inputs = tokens_ref[...].astype(F32)
    inv_one = lax.rsqrt(mean_last(inputs * inputs) + EPSILON)
    normed[own, :] = (inputs * inv_one * gain_one_ref[...]).astype(BF16)
    place.barrier()
    across(0).start()
    gg.start()

    lane = lax.broadcasted_iota(jnp.int32, (BLK, BLK), 1)
    row = lax.broadcasted_iota(jnp.int32, (BLK, BLK), 0)
    named = jnp.zeros((BLK, BLK), F32)
    routes = routes_ref[...]
    for j in range(routes.shape[0]):
        named = named + (routes[j : j + 1, :] == row).astype(F32)
    named = named.T
    wide_router[0 : router_ref.shape[0], :] = router_ref[...]
    wide_router[router_ref.shape[0] :, :] = jnp.zeros((BLK - router_ref.shape[0], WIDTH), BF16)
    place_of = (fill_ref[...] == row).astype(F32).astype(BF16)
    ordered = dot_tn(place_of, named.astype(BF16))
    earlier = (row > lane).astype(F32).astype(BF16)
    before = dot_nn(earlier, ordered.astype(BF16))
    rank = dot_nn(place_of, before.astype(BF16))
    kept = jnp.where(rank < capacity, named, 0.0)
    kept_s[...] = kept

    def project(rows):
        cos, sin = cos_ref[rows, :], sin_ref[rows, :]
        for n in range(2):
            part = dot_nn(normed[rows, :], wq_ref[:, n * 256 : (n + 1) * 256])
            for m in range(2):
                one = part[:, m * 128 : (m + 1) * 128]
                queries[rows, n * 256 + m * 128 : n * 256 + (m + 1) * 128] = (
                    one * cos + swapped(one) * sin
                ).astype(BF16)
        part = dot_nn(normed[rows, :], wk_ref[...])
        for m in range(2):
            one = part[:, m * 128 : (m + 1) * 128]
            keys[rows, m * 128 : (m + 1) * 128] = (one * cos + swapped(one) * sin).astype(BF16)
        values[rows, :] = dot_nn(normed[rows, :], wv_ref[...]).astype(BF16)

    project(own)
    arrived(0)
    across(1).start()
    project(peers)
    gg.arrive(0)
    gg.arrive_over(0)

    scale = HEAD_DIM ** (-0.5)

    def heads_of(m, half):
        cols = pl.ds(pl.multiple_of(m * 128, 128), 128)
        key = doubled(keys[:, cols].astype(F32), half).astype(BF16)
        value = doubled(values[:, cols].astype(F32), half).astype(BF16)
        j = m * 2 + half
        wide = pl.ds(pl.multiple_of(j * 128, 128), 128)
        query = stacked(queries[:, wide].astype(F32)).astype(BF16)
        return j, wide, key, value, query

    def attend(m, carry):
        place_q = lax.rem(lax.broadcasted_iota(jnp.int32, (512, 256), 0), 256)
        place_k = lax.broadcasted_iota(jnp.int32, (512, 256), 1)
        for half in range(2):
            j, wide, key, value, query = heads_of(m, half)
            scores = jnp.where(place_q >= place_k, dot_nt(query, key) * scale, MASKED)
            raised = jnp.exp(scores - jnp.max(scores, -1, keepdims=True))
            share = raised / jnp.sum(raised, -1, keepdims=True)
            probs[j] = share
            attended[:, wide] = unstacked(dot_nn(share.astype(BF16), value)).astype(BF16)
        return carry

    lax.fori_loop(0, 2, attend, 0)
    gg.arrive(1)
    gg.arrive_over(1, 2)
    branch_o[...] = dot_nn(attended[peers, :], wo_ref[...]).astype(BF16)
    across(4).start()
    own_branch = dot_nn(attended[own, :], wo_ref[...])
    gg.arrive(2)
    gg.arrive_over(3, 4)
    across(4).wait_recv()
    across(2).start()
    across(3).start()
    resid = tokens_ref[...].astype(F32) + own_branch + branch_i[...].astype(F32)
    residual[...] = resid
    inv_two = lax.rsqrt(mean_last(resid * resid) + EPSILON)
    moe_in = (resid * inv_two * gain_two_ref[...]).astype(BF16)
    logits = dot_nt(moe_in, wide_router[...])
    is_named = named > 0.0
    top = jnp.max(jnp.where(is_named, logits, MASKED), -1, keepdims=True)
    raised = jnp.where(is_named, jnp.exp(jnp.minimum(logits - top, 0.0)), 0.0)
    gates = raised / jnp.sum(raised, -1, keepdims=True)
    gates_s[...] = gates
    weights = gates * kept
    coarse = weights.astype(BF16).astype(F32)
    x[mine, :WIDTH] = moe_in
    x[mine, WIDTH:] = (coarse + pltpu.roll(weights - coarse, 16, 1)).astype(BF16)

    gx.start()
    gg.arrive_over(5, 6)
    gates_w, ups_w, downs_w = (gate_ref, gate_p), (up_ref, up_p), (down_ref, down_p)
    gx.arrive(0)
    gx.arrive_over(0)
    gx.arrive(1)
    gx.arrive_over(1, 2)
    gg.from_sib(0, *range(7))
    gg.from_sib(1, *range(7))
    gx.from_sib(0, 0, 1, 2)
    gx.from_sib(1, 0, 1, 2)
    for k in (1, 2, 3):
        across(k).wait_recv()

    def joined(i):
        ring, other = place.step(i, EXPERT_ORDER)
        si.join(other * 4 + ring)
        so.join(other * 4 + ring)

        @pl.when((other == 1) & (i != 3))
        def _():
            si.over_copy(ring).start()

    def chip_step(i, carry):
        @pl.when(i == 2)
        def _():
            gx.arrive(2)
            gx.arrive_over(3, 4)

        @pl.when(i == 4)
        def _():
            gx.arrive_over(5, 6)
            gx.from_sib(0, *range(3, 7))
            gx.from_sib(1, *range(3, 7))

        ring, other = place.step(i, EXPERT_ORDER)
        expert_step(
            place, ring, other, x, g, gates_w, ups_w, downs_w, hid, dgate, dup, in_s, in_t, out_s, out_t
        )
        si.sib_copy(other * 4 + ring).start()
        so.sib_copy(other * 4 + ring).start()

        @pl.when(i >= 1)
        def _():
            joined(i - 1)

        return carry

    lax.fori_loop(0, 8, chip_step, 0)
    joined(jnp.int32(7))
    si.over_copy(place.near(0)).start()
    si.relay(1)
    for k in (3, 2, 1, 0):
        so.over_copy(place.near(k)).start()

    def grad_step(i, carry):
        @pl.when(i == 5)
        def _():
            si.relay(3)

        @pl.when((i >= 2))
        def _():
            cols = pl.ds(pl.multiple_of((i - 2) * 256, 256), 256)
            turned = x[:, cols].T
            both = dot_nn(turned, dgate[...])
            ggate_ref[cols, :] = both[:, :256].astype(BF16)
            gate_o[cols, :] = both[:, 256:].astype(BF16)
            both = dot_nn(turned, dup[...])
            gup_ref[cols, :] = both[:, :256].astype(BF16)
            up_o[cols, :] = both[:, 256:].astype(BF16)

        @pl.when(i == 0)
        def _():
            down_o[...] = dot_nn(hid[:, 256:].T, g[...]).astype(BF16)

        @pl.when(i == 1)
        def _():
            across(7).start()
            gdown_ref[...] = dot_nn(hid[:, :256].T, g[...]).astype(BF16)

        return carry

    lax.fori_loop(0, 6, grad_step, 0)
    si.relay(2)
    across(5).start()

    from_experts = si.total()
    pairs = from_experts[:, WIDTH:]
    gates = gates_s[...]
    grad_gates = (pairs + pltpu.roll(pairs, 112, 1)) * kept_s[...]
    grad_logits = (gates * (grad_gates - jnp.sum(gates * grad_gates, -1, keepdims=True))).astype(BF16)
    grad_moe_in = from_experts[:, :WIDTH] + dot_nn(grad_logits, wide_router[...])
    resid = residual[...]
    inv_two = lax.rsqrt(mean_last(resid * resid) + EPSILON)
    grad_n = grad_moe_in * gain_two_ref[...]
    grad_residual = (
        cot_ref[...].astype(F32)
        + inv_two * grad_n
        - resid * (inv_two * inv_two * inv_two * mean_last(grad_n * resid))
    )
    branch_grad[own, :] = grad_residual.astype(BF16)
    across(8).start()
    grad_tokens_ref[...] = grad_residual
    small = dot_tn(grad_logits, x[mine, :WIDTH])
    ext_o[0:16, :] = small[0:16, :]
    ext_o[16:17, :] = jnp.sum(grad_moe_in * resid * inv_two, 0, keepdims=True)

    def grad_attended(rows):
        joint_grad[rows, :512] = dot_nt(branch_grad[rows, :], wo_ref[...]).astype(BF16)

    grad_attended(own)
    so.relay(3, 2)
    arrived(8)
    grad_attended(peers)
    wo_part[...] = dot_tn(attended[...], branch_grad[...]).astype(BF16)

    si.sib_sent()
    si.sent()

    def share_out(n, carry):
        ring, other = place.step(n, PAIR_FIRST)
        start = pl.multiple_of(place.chip(ring, other) * 64, 64)
        i = other * 4 + ring
        put(place, i, sw.sums, sw.theirs, slice(0, WIDTH), wo_part[pl.ds(start, 64), :])
        sw.sib_copy(i).start()
        return carry

    lax.fori_loop(0, 8, share_out, 0)

    def attend_back(m, carry):
        cols = pl.ds(pl.multiple_of(m * 128, 128), 128)
        cos, sin = cos_ref[...], sin_ref[...]
        from_values, from_keys = [], []
        for half in range(2):
            j, wide, key, value, query = heads_of(m, half)
            grad_mixed = stacked(joint_grad[:, wide].astype(F32)).astype(BF16)
            share = probs[j]
            grad_probs = dot_nt(grad_mixed, value)
            grad_scores = (
                share * (grad_probs - jnp.sum(share * grad_probs, -1, keepdims=True)) * scale
            ).astype(BF16)
            grad_query = unstacked(dot_nn(grad_scores, key))
            joint_grad[:, wide] = (grad_query * cos - swapped(grad_query) * sin).astype(BF16)
            one = dot_tn(share.astype(BF16), grad_mixed)
            from_values.append(one + pltpu.roll(one, 64, 1))
            one = dot_tn(grad_scores, query)
            from_keys.append(one + pltpu.roll(one, 64, 1))
        low_lanes = lax.broadcasted_iota(jnp.int32, (256, 128), 1) < 64
        grad_key = jnp.where(low_lanes, from_keys[0], from_keys[1])
        at_key = pl.ds(pl.multiple_of(512 + m * 128, 128), 128)
        at_value = pl.ds(pl.multiple_of(768 + m * 128, 128), 128)
        joint_grad[:, at_key] = (grad_key * cos - swapped(grad_key) * sin).astype(BF16)
        joint_grad[:, at_value] = jnp.where(low_lanes, from_values[0], from_values[1]).astype(BF16)
        return carry

    so.relay(1)
    lax.fori_loop(0, 2, attend_back, 0)
    sw.join_all()

    def share_joint(n, carry):
        ring, other = place.step(n, PAIR_FIRST)
        i = other * 4 + ring
        cols = pl.ds(pl.multiple_of(place.chip(ring, other) * 128, 128), 128)
        value = dot_nn(normed[:, cols].T, joint_grad[...])
        put(place, i, sj.sums, sj.theirs, slice(0, WIDTH), value)
        sj.sib_copy(i).start()
        return carry

    lax.fori_loop(0, 8, share_joint, 0)

    def grad_normed(rows):
        grads = joint_grad[rows, :]
        parts = []
        for n in range(4):
            at = slice(n * 256, (n + 1) * 256)
            parts.append(
                dot_nt(grads[:, :512], wq_ref[at, :])
                + dot_nt(grads[:, 512:768], wk_ref[at, :])
                + dot_nt(grads[:, 768:], wv_ref[at, :])
            )
        return jnp.concatenate(parts, 1)

    part = grad_normed(peers)
    across(4).wait_send()
    branch_o[...] = part.astype(BF16)
    gain_sum = jnp.sum(part * normed[peers, :].astype(F32), 0, keepdims=True)
    sj.join_all()
    own_part = grad_normed(own)
    gain_sum = gain_sum + jnp.sum(own_part * normed[own, :].astype(F32), 0, keepdims=True)
    ext_o[17:18, :] = gain_sum / gain_one_ref[...]
    ext_o[18:, :] = jnp.zeros((6, WIDTH), F32)
    across(10).start()
    across(6).start()
    ext_t[...] = jnp.concatenate([ext_o[...], jnp.zeros((BLK - 24, WIDTH), F32)], 0).T

    def share_ext(n, carry):
        ring, other = place.step(n, PAIR_FIRST)
        rows = pl.ds(pl.multiple_of(place.chip(ring, other) * 128, 128), 128)
        i = other * 4 + ring
        put(place, i, se.sums, se.theirs, slice(0, BLK), ext_t[rows, :])
        se.sib_copy(i).start()
        return carry

    lax.fori_loop(0, 8, share_ext, 0)
    sw.relay(3, 2, 1)
    sj.relay(3)
    se.join_all()
    sj.relay(2, 1)
    block = pl.ds(pl.multiple_of(place.e * 64, 64), 64)
    joint_ref[block, :] = sj.total().astype(BF16)
    gj.start()
    se.relay(3, 2, 1)
    block = pl.ds(pl.multiple_of(place.e * 32, 32), 32)
    wo_grad_ref[block, :] = sw.total().astype(BF16)
    gw.start()
    gj.arrive(0)
    gj.arrive_over(0)
    small_o[...] = se.total()
    across(9).start()
    gj.arrive(1)
    gj.arrive_over(1, 2)
    gw.arrive(0)
    gw.arrive_over(0)

    across(10).wait_recv()
    grad_n = (own_part + branch_i[...].astype(F32)) * gain_one_ref[...]
    inputs = tokens_ref[...].astype(F32)
    inv_one = lax.rsqrt(mean_last(inputs * inputs) + EPSILON)
    grad_tokens_ref[...] = (
        grad_tokens_ref[...]
        + inv_one * grad_n
        - inputs * (inv_one * inv_one * inv_one * mean_last(grad_n * inputs))
    )
    block = pl.ds(pl.multiple_of(place.e * 64, 64), 64)
    across(9).wait_recv()
    small_ref[block, :] = small_o[...] + small_i[...]
    ge.start()
    gj.arrive(2)
    gj.arrive_over(3, 4)
    gw.arrive(1)
    gw.arrive_over(1, 2)
    ge.arrive(1, 2, 3)
    output_ref[...] = (residual[...] + so.total()).astype(BF16)
    for k, total, part in ((7, gdown_ref, down_i), (5, ggate_ref, gate_i), (6, gup_ref, up_i)):
        across(k).wait_recv()
        total[...] = (total[...].astype(F32) + part[...].astype(F32)).astype(BF16)
    gj.arrive_over(5, 6)
    gw.arrive(2)
    gw.arrive_over(3, 4)
    ge.arrive_over(0, 1, 2, 3)
    gw.arrive_over(5, 6)
    for tree in (gj, gw):
        tree.from_sib(0, *range(7))
        tree.from_sib(1, *range(7))
    ge.from_sib()
    for k in (0, 1, 2, 3, 5, 6, 7, 8, 9, 10):
        across(k).wait_send()
    for tree in (so, sj, sw, se):
        tree.sib_sent()
    for tree in (gx, gg, gj, gw, ge, so, sj, sw, se):
        tree.sent()


def layer_call(capacity, *operands):
    vm, dma = pltpu.VMEM, pltpu.SemaphoreType.DMA
    spec = pl.BlockSpec(memory_space=pltpu.VMEM)
    sds = jax.ShapeDtypeStruct

    def body(*refs):
        return layer_kernel(capacity, *refs)

    outs = (
        sds((BLK, WIDTH), BF16),
        sds((BLK, WIDTH), F32),
        sds((WIDTH, WIDTH), BF16),
        sds((HALF, WIDTH), BF16),
        sds((WIDTH, BLK), F32),
        sds((WIDTH, 256), BF16),
        sds((WIDTH, 256), BF16),
        sds((256, WIDTH), BF16),
    )
    return pl.pallas_call(
        body,
        out_shape=outs,
        in_specs=[spec] * len(operands),
        out_specs=[spec] * len(outs),
        scratch_shapes=[
            vm((2048, EXT), BF16), vm((2048, WIDTH), BF16),
            vm((WIDTH, 256), BF16), vm((WIDTH, 256), BF16), vm((256, WIDTH), BF16),
            vm((2048, 512), BF16), vm((2048, 512), BF16), vm((2048, 512), BF16),
            vm((8, BLK, EXT), BF16), vm((8, BLK, EXT), BF16), vm((8, BLK, EXT), BF16),
            vm((8, BLK, WIDTH), BF16), vm((8, BLK, WIDTH), BF16), vm((8, BLK, WIDTH), BF16),
            vm((4, BLK, EXT), BF16), vm((4, BLK, EXT), BF16),
            vm((4, BLK, WIDTH), BF16), vm((4, BLK, WIDTH), BF16),
            vm((WIDTH, 256), BF16), vm((WIDTH, 256), BF16), vm((256, WIDTH), BF16),
            vm((WIDTH, 256), BF16), vm((WIDTH, 256), BF16), vm((256, WIDTH), BF16),
            vm((256, WIDTH), BF16), vm((256, 256), BF16), vm((256, 256), BF16), vm((256, 512), BF16),
            vm((4, 512, 256), F32), vm((256, 512), BF16),
            vm((BLK, WIDTH), BF16), vm((BLK, WIDTH), BF16), vm((BLK, WIDTH), F32),
            vm((BLK, BLK), F32), vm((BLK, BLK), F32),
            vm((256, WIDTH), BF16), vm((256, WIDTH), BF16),
            vm((24, WIDTH), F32), vm((WIDTH, BLK), F32), vm((64, BLK), F32), vm((64, BLK), F32), vm((512, WIDTH), BF16),
            vm((8, 64, WIDTH), BF16), vm((4, 64, WIDTH), BF16), vm((4, 64, WIDTH), BF16),
            vm((8, 32, WIDTH), BF16), vm((4, 32, WIDTH), BF16), vm((4, 32, WIDTH), BF16),
            vm((8, 64, BLK), F32), vm((8, 64, BLK), F32), vm((8, 64, BLK), F32),
            vm((4, 64, BLK), F32), vm((4, 64, BLK), F32), vm((BLK, WIDTH), BF16),
            dma((5, 27)), dma((5, 27)), dma((5, 7)), dma((5, 8)), dma((5, 8)), dma((5, 8)),
            dma((11,)), dma((11,)),
        ],
        compiler_params=pltpu.CompilerParams(
            collective_id=1, has_side_effects=True, vmem_limit_bytes=63 * 2**20
        ),
        cost_estimate=pl.CostEstimate(flops=24 * 10**9, bytes_accessed=10**7, transcendentals=10**6),
        name="layer",
    )(*operands)


def finish_kernel(
    joint_ref, wo_ref, small_ref, *refs,
):
    copied = refs[:5]
    query_out, key_out, value_out, wo_out, router_out, gain_one_out, gain_two_out = refs[5:12]
    query_out[...] = joint_ref[:, :512].astype(F32)
    key_out[...] = joint_ref[:, 512:768].astype(F32)
    value_out[...] = joint_ref[:, 768:].astype(F32)
    wo_out[...] = wo_ref[...].astype(F32)
    small = small_ref[...].T
    experts = router_out.shape[0]
    router_out[...] = small[:experts, :]
    gain_two_out[...] = small[experts : experts + 1, :]
    gain_one_out[...] = small[experts + 1 : experts + 2, :]
    for source, out in zip(copied, refs[12:]):
        out[...] = source[...].astype(out.dtype)


def finish_call(*operands):
    steps = 2
    sds = jax.ShapeDtypeStruct

    def rows(shape):
        if shape[0] < BLK:
            return pl.BlockSpec((shape[0], shape[1] // steps), lambda i: (0, i))
        return pl.BlockSpec((shape[0] // steps, shape[1]), lambda i: (i, 0))

    outs = [
        sds(shape, F32)
        for shape in (
            (WIDTH, 512), (WIDTH, 256), (WIDTH, 256), (HALF, WIDTH), (16, WIDTH), (1, WIDTH), (1, WIDTH),
            (WIDTH, 256), (WIDTH, 256), (256, WIDTH), (BLK, WIDTH),
        )
    ] + [sds((BLK, WIDTH), BF16)]
    return pl.pallas_call(
        finish_kernel,
        out_shape=outs,
        grid=(steps,),
        in_specs=[rows(a.shape) for a in operands],
        out_specs=[rows(a.shape) for a in outs],
        compiler_params=pltpu.CompilerParams(vmem_limit_bytes=62 * 2**20),
        cost_estimate=pl.CostEstimate(flops=10**6, bytes_accessed=16 * 10**6, transcendentals=0),
        name="finish",
    )(*operands)


def tables(rows):
    half = HEAD_DIM // 2
    freqs = np.exp(np.arange(half, dtype=np.float32) * np.float32(-2.0 * math.log(THETA_BASE) / HEAD_DIM))
    angles = np.arange(rows, dtype=np.float32)[:, None] * freqs[None, :]
    cos, sin = np.cos(angles), np.sin(angles)
    return (
        np.concatenate([cos] * 4, 1).astype(np.float32),
        np.concatenate([-sin, sin] * 2, 1).astype(np.float32),
    )


def on_device(
    tokens,
    gain_attn,
    w_query,
    w_key,
    w_value,
    w_out,
    gain_moe,
    router,
    expert_gate,
    expert_up,
    expert_down,
    routes,
    fill_order,
    cotangent,
):
    tok_rows, width = tokens.shape
    tensor_size = lax.axis_size("tensor")
    seq_rows = tok_rows * tensor_size
    head_size = HEAD_DIM
    q_cols = w_query.shape[1]
    kv_cols = w_key.shape[1]
    q_heads = q_cols // head_size
    kv_heads = kv_cols // head_size
    q_group = q_heads // kv_heads
    score_scale = head_size ** (-0.5)
    local_experts = expert_gate.shape[0]
    expert_groups = lax.axis_size("expert")
    experts = local_experts * expert_groups
    top_k = routes.shape[1]
    capacity = (5 * tok_rows * top_k + 4 * experts - 1) // (4 * experts)
    gate_w, up_w, down_w = (expert_gate, expert_up, expert_down)
    inputs = tokens.astype(jnp.float32)
    inv_one = lax.rsqrt(jnp.mean(inputs * inputs, -1, keepdims=True) + EPSILON)
    normed = (inputs * inv_one * gain_attn).astype(jnp.bfloat16)
    normed_all = lax.all_gather(normed, "tensor", axis=0, tiled=True)
    w_joint = jnp.concatenate([w_query, w_key, w_value], 1)
    joint = jnp.dot(normed_all, w_joint, preferred_element_type=jnp.float32)
    angles = angles_of(seq_rows, head_size)
    queries = rotate(joint[:, :q_cols].reshape(seq_rows, q_heads, head_size), angles, 1.0).astype(
        jnp.bfloat16
    )
    key_rows = rotate(
        joint[:, q_cols : q_cols + kv_cols].reshape(seq_rows, kv_heads, head_size), angles, 1.0
    ).astype(jnp.bfloat16)
    value_rows = (
        joint[:, q_cols + kv_cols :].astype(jnp.bfloat16).reshape(seq_rows, kv_heads, head_size)
    )
    q_size = min(512, seq_rows)
    blocks = seq_rows // q_size
    key_pos = jnp.arange(seq_rows)

    def scores_of(q_block, row_start):
        grouped = q_block.reshape(q_size, kv_heads, q_group, head_size)
        raw_scores = (
            jnp.einsum("qkgd,tkd->kgqt", grouped, key_rows, preferred_element_type=jnp.float32)
            * score_scale
        )
        allowed = (row_start + jnp.arange(q_size))[:, None] >= key_pos[None, :]
        return (grouped, jnp.where(allowed, raw_scores, MASKED))

    def forward_block(block_args):
        q_block, row_start = block_args
        grouped, scores = scores_of(q_block, row_start)
        top_score = jnp.max(scores, -1, keepdims=True)
        exp_scores = jnp.exp(scores - top_score)
        row_total = jnp.sum(exp_scores, -1, keepdims=True)
        attn_probs = (exp_scores / row_total).astype(jnp.bfloat16)
        mixed_rows = jnp.einsum(
            "kgqt,tkd->qkgd", attn_probs, value_rows, preferred_element_type=jnp.float32
        )
        return (mixed_rows.astype(jnp.bfloat16).reshape(q_size, q_cols), top_score, row_total)

    q_blocks = queries.reshape(blocks, q_size, q_heads, head_size)
    starts = jnp.arange(blocks) * q_size
    attended, maxima, totals = lax.map(forward_block, (q_blocks, starts))
    attended = attended.reshape(seq_rows, q_cols)
    row_block = attended
    branch = lax.psum_scatter(
        jnp.dot(row_block, w_out, preferred_element_type=jnp.float32),
        "tensor",
        scatter_dimension=0,
        tiled=True,
    )
    residual = inputs + branch
    inv_two = lax.rsqrt(jnp.mean(residual * residual, -1, keepdims=True) + EPSILON)
    scaled = residual * inv_two
    moe_in = (scaled * gain_moe).astype(jnp.bfloat16)
    logits = jnp.dot(moe_in, router, preferred_element_type=jnp.float32)
    expert_ids = jnp.arange(experts, dtype=jnp.int32)
    named = jnp.sum((routes[:, :, None] == expert_ids[None, None, :]).astype(jnp.float32), 1)
    place_of = (fill_order[0][:, None] == jnp.arange(tok_rows)[None, :]).astype(jnp.bfloat16)
    ordered = jnp.dot(place_of, named.astype(jnp.bfloat16), preferred_element_type=jnp.float32)
    earlier = (jnp.arange(tok_rows)[:, None] > jnp.arange(tok_rows)[None, :]).astype(jnp.bfloat16)
    before = jnp.dot(earlier, ordered.astype(jnp.bfloat16), preferred_element_type=jnp.float32)
    rank = contract_first(place_of, before.astype(jnp.bfloat16))
    kept = named * (rank < capacity).astype(jnp.float32)
    top_logit = jnp.max(jnp.where(named > 0, logits, MASKED), -1, keepdims=True)
    exp_logits = jnp.where(named > 0, jnp.exp(jnp.minimum(logits - top_logit, 0.0)), 0.0)
    gates = exp_logits / jnp.sum(exp_logits, -1, keepdims=True)
    weights = gates * kept

    gate_all = lax.all_gather(gate_w[0], "tensor", axis=1, tiled=True)
    up_all = lax.all_gather(up_w[0], "tensor", axis=1, tiled=True)
    down_all = lax.all_gather(down_w[0], "tensor", axis=0, tiled=True)
    grad_out = cotangent.astype(jnp.float32)
    plane_cot = lax.all_gather(cotangent, "expert", axis=0, tiled=True)
    plane_in = lax.all_gather(moe_in, "expert", axis=0, tiled=True)
    plane_weights = lax.all_gather(weights, "expert", axis=0, tiled=True)
    mine = (expert_ids == lax.axis_index("expert")).astype(jnp.float32)
    my_weight = jnp.sum(plane_weights * mine[None, :], -1, keepdims=True)

    gate_pre = jnp.dot(plane_in, gate_all, preferred_element_type=jnp.float32)
    up_pre = jnp.dot(plane_in, up_all, preferred_element_type=jnp.float32)
    back_down = contract_last(plane_cot, down_all)
    gate_sigmoid = jax.nn.sigmoid(gate_pre)
    active = gate_pre * gate_sigmoid
    hidden = active * up_pre
    pair_grad = jnp.sum(hidden * back_down, -1, keepdims=True)
    hidden_w = (hidden * my_weight).astype(jnp.bfloat16)
    grad_hidden = back_down * my_weight
    grad_gate_pre = (
        grad_hidden * up_pre * gate_sigmoid * (1.0 + gate_pre * (1.0 - gate_sigmoid))
    ).astype(jnp.bfloat16)
    grad_up_pre = (grad_hidden * active).astype(jnp.bfloat16)
    out_part = jnp.dot(hidden_w, down_all, preferred_element_type=jnp.float32)
    in_part = contract_last(grad_gate_pre, gate_all) + contract_last(grad_up_pre, up_all)
    out_sum = lax.psum_scatter(
        out_part.astype(jnp.bfloat16), "expert", scatter_dimension=0, tiled=True
    )
    in_sum = lax.psum_scatter(
        in_part.astype(jnp.bfloat16), "expert", scatter_dimension=0, tiled=True
    )
    grad_gates = lax.psum_scatter(
        pair_grad * mine[None, :], "expert", scatter_dimension=0, tiled=True
    ) * kept
    grad_down = lax.psum_scatter(
        contract_first(hidden_w, plane_cot).astype(jnp.bfloat16),
        "tensor", scatter_dimension=0, tiled=True,
    ).astype(jnp.float32)[None]
    grad_gate = lax.psum_scatter(
        contract_first(plane_in, grad_gate_pre).astype(jnp.bfloat16),
        "tensor", scatter_dimension=1, tiled=True,
    ).astype(jnp.float32)[None]
    grad_up = lax.psum_scatter(
        contract_first(plane_in, grad_up_pre).astype(jnp.bfloat16),
        "tensor", scatter_dimension=1, tiled=True,
    ).astype(jnp.float32)[None]
    output_rows = residual + out_sum.astype(jnp.float32)
    grad_logits = (
        gates * (grad_gates - jnp.sum(gates * grad_gates, -1, keepdims=True))
    ).astype(jnp.bfloat16)
    grad_moe_in = in_sum.astype(jnp.float32) + contract_last(grad_logits, router)
    grad_router = contract_first(moe_in, grad_logits)
    grad_gain_moe = jnp.sum(grad_moe_in * scaled, 0)
    grad_norm_two = grad_moe_in * gain_moe
    grad_residual = (
        grad_out
        + inv_two * grad_norm_two
        - residual * inv_two**3 * jnp.mean(grad_norm_two * residual, -1, keepdims=True)
    )
    grad_branch = grad_residual.astype(jnp.bfloat16)
    shard_piece = lax.all_gather(grad_branch, "tensor", axis=0, tiled=True)
    grad_part = contract_last(shard_piece, w_out).astype(jnp.bfloat16)
    grad_mixed = grad_part
    grad_wout = contract_first(attended, shard_piece)
    grad_mixed, grad_w_out = (grad_mixed, grad_wout)
    grad_blocks = grad_mixed.reshape(blocks, q_size, q_heads, head_size)

    def backward_block(carry, block_args):
        grad_keys, grad_values = carry
        q_block, grad_block, row_start, top_score, row_total = block_args
        grouped, scores = scores_of(q_block, row_start)
        attn_probs = jnp.exp(scores - top_score) / row_total
        grad_grouped = grad_block.reshape(q_size, kv_heads, q_group, head_size)
        grad_probs = jnp.einsum(
            "qkgd,tkd->kgqt", grad_grouped, value_rows, preferred_element_type=jnp.float32
        )
        grad_values = grad_values + jnp.einsum(
            "kgqt,qkgd->tkd",
            attn_probs.astype(jnp.bfloat16),
            grad_grouped,
            preferred_element_type=jnp.float32,
        )
        grad_scores = (
            attn_probs
            * (grad_probs - jnp.sum(attn_probs * grad_probs, -1, keepdims=True))
            * score_scale
        ).astype(jnp.bfloat16)
        grad_query = jnp.einsum(
            "kgqt,tkd->qkgd", grad_scores, key_rows, preferred_element_type=jnp.float32
        ).reshape(q_size, q_heads, head_size)
        grad_keys = grad_keys + jnp.einsum(
            "kgqt,qkgd->tkd", grad_scores, grouped, preferred_element_type=jnp.float32
        )
        return ((grad_keys, grad_values), grad_query)

    zero_rows = jnp.zeros((seq_rows, kv_heads, head_size), jnp.float32)
    (grad_keys, grad_values), grad_queries = lax.scan(
        backward_block, (zero_rows, zero_rows), (q_blocks, grad_blocks, starts, maxima, totals)
    )
    grad_queries = grad_queries.reshape(seq_rows, q_heads, head_size)
    grad_q = rotate(grad_queries, angles, -1.0).astype(jnp.bfloat16).reshape(seq_rows, q_cols)
    grad_k = rotate(grad_keys, angles, -1.0).astype(jnp.bfloat16).reshape(seq_rows, kv_cols)
    grad_v = grad_values.astype(jnp.bfloat16).reshape(seq_rows, kv_cols)
    grad_joint = jnp.concatenate([grad_q, grad_k, grad_v], 1)
    grad_w_joint = contract_first(normed_all, grad_joint)
    row_block = grad_joint
    grad_normed = lax.psum_scatter(
        contract_last(row_block, w_joint), "tensor", scatter_dimension=0, tiled=True
    )
    grad_gain_attn = jnp.sum(grad_normed * inputs * inv_one, 0)
    grad_norm_one = grad_normed * gain_attn
    grad_tokens = (
        grad_residual
        + inv_one * grad_norm_one
        - inputs * inv_one**3 * jnp.mean(grad_norm_one * inputs, -1, keepdims=True)
    )
    summed_joint, summed_out = lax.psum((grad_w_joint, grad_w_out), "expert")
    summed_gain_attn, summed_gain_moe, summed_router = lax.psum(
        (grad_gain_attn, grad_gain_moe, grad_router), ("expert", "tensor")
    )
    return (
        output_rows.astype(jnp.bfloat16),
        grad_tokens,
        summed_gain_attn,
        summed_joint[:, :q_cols],
        summed_joint[:, q_cols : q_cols + kv_cols],
        summed_joint[:, q_cols + kv_cols :],
        summed_out,
        summed_gain_moe,
        summed_router,
        grad_gate,
        grad_up,
        grad_down,
    )


def by_kernel(
    tokens,
    gain_attn,
    w_query,
    w_key,
    w_value,
    w_out,
    gain_moe,
    router,
    expert_gate,
    expert_up,
    expert_down,
    routes,
    fill_order,
    cotangent,
):
    tok_rows = tokens.shape[0]
    experts = router.shape[1]
    capacity = (5 * tok_rows * routes.shape[1] + 4 * experts - 1) // (4 * experts)
    cos, sin = tables(tok_rows * 2)
    out, grad_tokens, joint, wo_grad, small, *expert_grads = layer_call(
        capacity,
        tokens, cotangent, gain_attn[None], gain_moe[None], w_query, w_key, w_value, w_out,
        router.T, routes.T, fill_order, jnp.asarray(cos), jnp.asarray(sin),
        expert_gate[0], expert_up[0], expert_down[0],
    )
    gq, gk, gv, gwo, grad_router, grad_one, grad_two, ggate, gup, gdown, grad_tokens, out = finish_call(
        joint, wo_grad, small, *expert_grads, grad_tokens, out
    )
    return (
        out,
        grad_tokens,
        grad_one[0],
        gq,
        gk,
        gv,
        gwo,
        grad_two[0],
        grad_router.T,
        ggate[None],
        gup[None],
        gdown[None],
    )


def kernel_fits(mesh_shape, shapes):
    return mesh_shape == (16, 2) and shapes == (
        (128, 1024), (1024,), (1024, 512), (1024, 256), (1024, 256), (512, 1024), (1024,), (1024, 16),
        (1, 1024, 256), (1, 1024, 256), (1, 256, 1024), (128, 8), (1, 128), (128, 1024),
    )


def on_any(*operands):
    sizes = (lax.axis_size("expert"), lax.axis_size("tensor"))
    if kernel_fits(sizes, tuple(a.shape for a in operands)):
        return by_kernel(*operands)
    return on_device(*operands)


def solution(mesh):
    placed = (
        P(("expert", "tensor"), None),
        P(),
        P(None, "tensor"),
        P(None, "tensor"),
        P(None, "tensor"),
        P("tensor", None),
        P(),
        P(),
        P("expert", None, "tensor"),
        P("expert", None, "tensor"),
        P("expert", "tensor", None),
        P(("expert", "tensor"), None),
        P(("expert", "tensor"), None),
        P(("expert", "tensor"), None),
    )
    return jax.shard_map(
        on_any,
        mesh=mesh,
        in_specs=placed,
        out_specs=(
            P(("expert", "tensor"), None),
            P(("expert", "tensor"), None),
            P(),
            P(None, "tensor"),
            P(None, "tensor"),
            P(None, "tensor"),
            P("tensor", None),
            P(),
            P(),
            P("expert", None, "tensor"),
            P("expert", None, "tensor"),
            P("expert", "tensor", None),
        ),
        check_vma=False,
    )
```
